128 devices in a mesh: fsdp: 64 (over x, y, z_lo, core), rep: 2 (over z_hi).
Axes of the slice: x: 4, y: 4, z: 4 (z_hi: 2, z_lo: 2; z = z_hi * 2 + z_lo), core: 2. Of those that a mesh axis runs over, the one named last changes fastest.
Arguments:
- block_input: bfloat16 [32768, 768], P(('fsdp', 'rep')), may hold values from -6 to 6
- segment_ids: int32 [128, 256], P(('fsdp', 'rep')), may hold values from 0 to 3, never falling along the last dimension, each value on 1 to 128 neighbouring positions
- norm1_gain: bfloat16 [768], P('fsdp'), may hold values from 0.099609375 to 1.8984375
- norm1_bias: bfloat16 [768], P('fsdp'), may hold values from -3 to 3
- query_weight: bfloat16 [768, 768], P('fsdp'), may hold values from -0.21875 to 0.21875
- key_weight: bfloat16 [768, 768], P('fsdp'), may hold values from -0.21875 to 0.21875
- value_weight: bfloat16 [768, 768], P('fsdp'), may hold values from -0.21875 to 0.21875
- out_weight: bfloat16 [768, 768], P('fsdp'), may hold values from -0.875 to 0.875
- norm2_gain: bfloat16 [768], P('fsdp'), may hold values from 0.099609375 to 1.8984375
- norm2_bias: bfloat16 [768], P('fsdp'), may hold values from -3 to 3
- up_weight: bfloat16 [768, 3072], P('fsdp'), may hold values from -0.21875 to 0.21875
- down_weight: bfloat16 [3072, 768], P('fsdp'), may hold values from -0.15625 to 0.15625
- out_cotangent: bfloat16 [32768, 768], P(('fsdp', 'rep')), may hold values from -6 to 6
Outputs:
- block_output: bfloat16 [32768, 768], P(('fsdp', 'rep'))
- input_grad: float32 [32768, 768], P(('fsdp', 'rep'))
- norm1_gain_grad: float32 [768], P('fsdp')
- norm1_bias_grad: float32 [768], P('fsdp')
- query_grad: float32 [768, 768], P('fsdp')
- key_grad: float32 [768, 768], P('fsdp')
- value_grad: float32 [768, 768], P('fsdp')
- outproj_grad: float32 [768, 768], P('fsdp')
- norm2_gain_grad: float32 [768], P('fsdp')
- norm2_bias_grad: float32 [768], P('fsdp')
- up_grad: float32 [768, 3072], P('fsdp')
- down_grad: float32 [3072, 768], P('fsdp')
The draws below stay inside these ranges and needn't reach their ends.
Inputs may be any that keep to these rules, and one draw needn't show every extreme that they name: `segment_ids`: along each row segment numbers never fall; one number covers a run of 1 to 128 consecutive tokens, and some run has exactly 128.
All inputs are finite; a program needn't handle non-finite values.
Results may differ from the reference program's by a relative error of at most 0.012.
Values may be sent and summed in bfloat16 or wider, within the bound.
A program may use at most 128 MiB of HBM per device.

```python
import math
import jax
import jax.numpy as jnp
import numpy as np
from jax import lax

D = 768
HEADS = 24
HEAD_DIM = 32
FF = 3072
TOK_DEV = 256
SEG_COUNT = 4
SEG_MOST = 128
ROWS = 128
TOKENS = 32768


def steps_of(stream_key, shape, shards, smallest, high):
    def one(position, blocks):
        heights = jax.random.uniform(jax.random.fold_in(jax.random.fold_in(stream_key, 6), position), (blocks,), jnp.float32, smallest / len(shards), high / len(shards))
        return jnp.repeat(jnp.exp(heights), shape[position] // blocks).reshape((-1,) + (1,) * (len(shape) - position - 1))

    level = one(*shards[0])
    for cut in shards[1:]:
        level = level * one(*cut)
    return level


def length_profile(number_of, total, reach, skew):
    loads = [(1 << 20) // math.isqrt(rank ** skew) + 1 for rank in range(2, number_of + 1)]
    rest, given = total - reach - (number_of - 1), [1] * (number_of - 1)
    while rest > 0:
        free = [i for i in range(number_of - 1) if given[i] < reach]
        mass, budget = sum([loads[i] for i in free]), rest
        for i in free:
            more = min(reach - given[i], max(1, budget * loads[i] // mass), rest)
            given[i] = given[i] + more
            rest = rest - more
    return np.array([reach] + given)


def ragged(own_key, count, total, bound, skew):
    if count == 2:
        one = jax.random.randint(own_key, (), max(1, total - bound), min(bound, total - 1) + 1)
        return jnp.stack([one, total - one])
    sizes = jnp.asarray(length_profile(count, total, bound, skew), jnp.int32)
    couples = (count - 1) // 2
    source_of, taker = sizes[1:1 + 2 * couples:2], sizes[2:2 + 2 * couples:2]
    slack = jnp.minimum(source_of - 1, bound - taker)
    passed = jax.random.randint(jax.random.fold_in(own_key, 1), (couples,), 0, 1 << 20) % (slack + 1)
    sizes = sizes.at[1:1 + 2 * couples:2].set(source_of - passed).at[2:2 + 2 * couples:2].set(taker + passed)
    return sizes[jax.random.permutation(jax.random.fold_in(own_key, 2), count)]


def bell_draw(own_key, dims, scale, bound, shards=(), kind=jnp.bfloat16):
    level = steps_of(own_key, dims, shards, -0.22, 0.18) if shards else 1.0
    result = jax.random.normal(own_key, dims, jnp.float32) * scale * level
    return jnp.minimum(jnp.maximum(result, -bound), bound).astype(kind)


def setup_inputs(seed: int = 0) -> dict:
    arg_keys = jax.random.split(jax.random.key(seed), 14)
    block_input = bell_draw(arg_keys[0], (TOKENS, D), 1.0, 6.0, ((0, 128),))
    segment_ids = jax.vmap(lambda own: jnp.searchsorted(jnp.cumsum(ragged(own, SEG_COUNT, TOK_DEV, SEG_MOST, 0)), jnp.arange(TOK_DEV), side="right"))(jax.random.split(arg_keys[1], ROWS)).reshape((ROWS, TOK_DEV)).astype(jnp.int32)
    norm1_gain = jnp.clip(1.0 + 0.18 * jax.random.normal(arg_keys[2], (D,), jnp.float32), 0.099609375, 1.8984375).astype(jnp.bfloat16)
    norm1_bias = bell_draw(arg_keys[3], (D,), 0.5, 3.0, ((0, 64),))
    query_weight = bell_draw(arg_keys[4], (D, D), D ** -0.5, 0.21875, ((0, 64),))
    key_weight = bell_draw(arg_keys[5], (D, D), D ** -0.5, 0.21875, ((0, 64),))
    value_weight = bell_draw(arg_keys[6], (D, D), D ** -0.5, 0.21875, ((0, 64),))
    out_weight = bell_draw(arg_keys[7], (D, D), (D // 16) ** -0.5, 0.875, ((0, 64),))
    norm2_gain = jnp.clip(1.0 + 0.18 * jax.random.normal(arg_keys[8], (D,), jnp.float32), 0.099609375, 1.8984375).astype(jnp.bfloat16)
    norm2_bias = bell_draw(arg_keys[9], (D,), 0.5, 3.0, ((0, 64),))
    up_weight = bell_draw(arg_keys[10], (D, FF), D ** -0.5, 0.21875, ((0, 64),))
    down_weight = bell_draw(arg_keys[11], (FF, D), (FF // 2) ** -0.5, 0.15625, ((0, 64),))
    out_cotangent = bell_draw(arg_keys[12], (TOKENS, D), 1.0, 6.0, ((0, 128),))
    return dict(block_input=block_input, segment_ids=segment_ids, norm1_gain=norm1_gain, norm1_bias=norm1_bias, query_weight=query_weight, key_weight=key_weight, value_weight=value_weight, out_weight=out_weight, norm2_gain=norm2_gain, norm2_bias=norm2_bias, up_weight=up_weight, down_weight=down_weight, out_cotangent=out_cotangent)


@jax.custom_vjp
def low(v):
    return lax.optimization_barrier(v.astype(jnp.bfloat16)).astype(jnp.float32)

@jax.custom_vjp
def low_back(v):
    return v

def low_keep(v):
    return (low(v), None)

def low_pass(kept, grad):
    return (grad,)

def back_keep(v):
    return (v, None)

def back_low(kept, grad):
    return (low(grad),)
low.defvjp(low_keep, low_pass)
low_back.defvjp(back_keep, back_low)

def matmul_high(left, right):
    return jnp.dot(left, right, precision=lax.Precision.HIGHEST, preferred_element_type=jnp.float32)

def layer_norm(values, gain, shift):
    centre = lax.optimization_barrier(jnp.mean(values, axis=-1, keepdims=True))
    centred = values - centre
    spread = lax.optimization_barrier(jnp.mean(centred * centred, axis=-1, keepdims=True))
    return centred * lax.rsqrt(spread + 1e-05) * gain + shift

def reference(block_input, segment_ids, norm1_gain, norm1_bias, query_weight, key_weight, value_weight, out_weight, norm2_gain, norm2_bias, up_weight, down_weight, out_cotangent):
    group = min(ROWS, max(1, 4096 // TOK_DEV))
    blocks = ROWS // group
    scale = HEAD_DIM ** (-0.5)

    def attend(pieces):
        query, key, value, segments = pieces
        query_heads = query.reshape(group, TOK_DEV, HEADS, HEAD_DIM)
        key_heads = key.reshape(group, TOK_DEV, HEADS, HEAD_DIM)
        value_heads = value.reshape(group, TOK_DEV, HEADS, HEAD_DIM)
        scaled = jnp.einsum('gqhd,gkhd->ghqk', query_heads, key_heads, precision=lax.Precision.HIGHEST) * scale
        scaled = low_back(scaled)
        places = jnp.arange(TOK_DEV, dtype=jnp.int32)
        causal = places[:, None] >= places[None, :]
        allowed = causal[None] & (segments[:, :, None] == segments[:, None, :])
        probs = jax.nn.softmax(jnp.where(allowed[:, None], scaled, -1e+30), axis=-1)
        probs = low(probs)
        mixed = jnp.einsum('ghqk,gkhd->gqhd', probs, value_heads, precision=lax.Precision.HIGHEST)
        return mixed.reshape(group * TOK_DEV, D)
    segments_all = segment_ids.reshape(blocks, group, TOK_DEV)

    def forward(inputs, gain1, bias1, w_query, w_key, w_value, w_out, gain2, bias2, w_up, w_down):
        normed1 = low(layer_norm(inputs, gain1, bias1))
        query = low_back(low(matmul_high(normed1, w_query)))
        key = low_back(low(matmul_high(normed1, w_key)))
        value = low_back(low(matmul_high(normed1, w_value)))
        shaped = lambda tensor: tensor.reshape(blocks, group * TOK_DEV, D)
        mixed = lax.map(jax.checkpoint(attend), (shaped(query), shaped(key), shaped(value), segments_all))
        mixed = low_back(low(mixed.reshape(TOKENS, D)))
        hidden_state = inputs + low_back(matmul_high(mixed, w_out))
        normed2 = low(layer_norm(hidden_state, gain2, bias2))
        pre_act = low_back(matmul_high(normed2, w_up))
        activated = low(jax.nn.gelu(pre_act))
        return hidden_state + low_back(matmul_high(activated, w_down))
    floats = [item.astype(jnp.float32) for item in (block_input, norm1_gain, norm1_bias, query_weight, key_weight, value_weight, out_weight, norm2_gain, norm2_bias, up_weight, down_weight)]
    output, pull = jax.vjp(forward, *floats)
    grads = pull(out_cotangent.astype(jnp.float32))
    return (output.astype(jnp.bfloat16), grads[0], grads[1], grads[2], grads[3], grads[4], grads[5], grads[6], grads[7], grads[8], grads[9], grads[10])
```

```python
import functools

import jax
import jax.numpy as jnp
from jax import lax
from jax.experimental import pallas as pl
from jax.experimental.pallas import tpu as pltpu
from jax.sharding import PartitionSpec as P

HEADS = 24
HEAD_DIM = 32
D = 768
FF = 3072
BF = jnp.bfloat16
F32 = jnp.float32
MESH = pl.DeviceIdType.MESH

WIDE = 6400
START = (0, 2560)
HALF = (1280, 1920)
PART = ((640, 640), (896, 1024), (768, 768))
LOW = ((256, 256), (384, 512), (384, 384))
N_RECV = 240
N_SEND = 48


class Place:
    def __init__(self):
        f = lax.axis_index("fsdp")
        self.r = lax.axis_index("rep")
        self.c = lax.rem(f, 2)
        self.zl = lax.rem(lax.div(f, 2), 2)
        self.y = lax.rem(lax.div(f, 4), 4)
        self.x = lax.div(f, 16)

    def dev(self, dx=0, dy=0, zl=None, c=None, r=None):
        x, y = wrap(self.x, dx), wrap(self.y, dy)
        zl = self.zl if zl is None else zl
        c = self.c if c is None else c
        return {"fsdp": x * 16 + y * 4 + zl * 2 + c, "rep": self.r if r is None else r}

    def sibling(self):
        return self.dev(c=1 - self.c)

    def pair(self):
        return self.dev(zl=1 - self.zl)

    def other(self):
        return self.dev(r=1 - self.r)


def wrap(v, d):
    return v if d == 0 else lax.rem(v + (d + 4), 4)


class Wire:
    def __init__(self, place, send, recv):
        self.place, self.send_sem, self.recv_sem = place, send, recv
        self.n = self.m = 0
        self.open = {}

    def slot(self):
        k = self.m % N_SEND
        self.m += 1
        if k in self.open:
            self.open.pop(k).wait_send()
        return k

    def put(self, src, dst, to):
        k = self.slot()
        assert self.n < N_RECV
        copy = pltpu.make_async_remote_copy(
            src_ref=src,
            dst_ref=dst,
            send_sem=self.send_sem.at[k],
            recv_sem=self.recv_sem.at[self.n],
            device_id=to,
            device_id_type=MESH,
        )
        copy.start()
        self.open[k] = copy
        self.n += 1
        return copy

    def drain(self):
        for copy in self.open.values():
            copy.wait_send()
        self.open = {}


def greet(place):
    barrier = pltpu.get_barrier_semaphore()
    peers = [place.sibling(), place.pair(), place.other()]
    peers += [place.dev(dx=1), place.dev(dx=-1), place.dev(dy=1), place.dev(dy=-1)]
    for peer in peers:
        pl.semaphore_signal(barrier, inc=1, device_id=peer, device_id_type=MESH)
    pl.semaphore_wait(barrier, len(peers))


def span(g, p, h):
    if h is None:
        return 0, PART[g][p]
    return (0, LOW[g][p]) if h == 0 else (LOW[g][p], PART[g][p] - LOW[g][p])


def cols(g, p, c, h=None):
    off, width = span(g, p, h)
    base = START[g] + (PART[g][0] if p else 0) + off
    return pl.ds(pl.multiple_of(base + c * HALF[g], 128), width)


def block(wide, down, g, p, c, bx, by, h=None):
    if g < 2:
        return wide.at[bx, by, :, cols(g, p, c, h)]
    off, width = span(g, p, h)
    return down.at[bx, by, p, c, :, pl.ds(off, width)]


def gather_stream(wire, wide, down, g, p):
    me = wire.place

    def piece(du, dw, h=None, c=me.c):
        dx, dy = (du, dw) if p == 0 else (dw, du)
        return block(wide, down, g, p, c, wrap(me.x, dx), wrap(me.y, dy), h)

    def first(d):
        return me.dev(dx=d) if p == 0 else me.dev(dy=d)

    def second(d):
        return me.dev(dy=d) if p == 0 else me.dev(dx=d)

    def go(du, dw, to, h=None):
        ref = piece(du, dw, h)
        return wire.put(ref, ref, to)

    sib = []
    up, dn = {}, {}

    def spread(du):
        up[du] = go(du, 0, second(1))
        dn[du] = go(du, 0, second(-1))

    a, b = go(0, 0, first(1)), go(0, 0, first(-1))
    spread(0)
    yield
    a.wait_recv()
    far_a = go(-1, 0, first(1), 0)
    spread(-1)
    sib.append(go(-1, 0, me.sibling()))
    b.wait_recv()
    far_b = go(1, 0, first(-1), 1)
    spread(1)
    sib.append(go(1, 0, me.sibling()))
    yield
    far_a.wait_recv()
    far_b.wait_recv()
    spread(2)
    sib.append(go(2, 0, me.sibling()))
    yield
    far = {}
    for du in (0, -1, 1, 2):
        up[du].wait_recv()
        far_a = go(du, -1, second(1), 0)
        sib.append(go(du, -1, me.sibling()))
        dn[du].wait_recv()
        far_b = go(du, 1, second(-1), 1)
        sib.append(go(du, 1, me.sibling()))
        far[du] = far_a, far_b
        if du == -1:
            yield
    yield
    for du in (0, -1, 1, 2):
        far[du][0].wait_recv()
        far[du][1].wait_recv()
        sib.append(go(du, 2, me.sibling()))
    yield
    for copy in sib:
        copy.wait_recv()
    yield


def join(stage, wide, me, g):
    width = 2 * HALF[g]
    step = 640
    def body(i, _):
        at = pl.ds(pl.multiple_of(START[g] + i * step, 128), step)
        rows = [stage[o, :, at].astype(F32)[:12] for o in range(4)]
        wide[me.x, me.y, :, at] = jnp.concatenate(rows, axis=0).astype(BF)
        return 0
    lax.fori_loop(0, width // step, body, 0)


def gather_stage0(wire, own, own_down, stage, wide, down, g):
    me = wire.place
    mine = 2 * me.zl + me.c
    if g < 2:
        at = pl.ds(START[g], 2 * HALF[g])
        src, dst = own.at[:, at], lambda o: stage.at[o, :, at]
        hers = stage.at[2 * (1 - me.zl) + me.c, :, at]
        stage[mine, :, at] = own[:, at]
    else:
        src, dst = own_down, lambda o: down.at[me.x, me.y, me.zl, me.c]
        hers = down.at[me.x, me.y, 1 - me.zl, me.c]
        down[me.x, me.y, me.zl, me.c] = own_down[...]
    a = wire.put(src, dst(mine), me.pair())
    b = wire.put(src, dst(mine), me.sibling())
    yield
    a.wait_recv()
    c = wire.put(hers, hers, me.sibling())
    yield
    b.wait_recv()
    c.wait_recv()
    if g < 2:
        join(stage, wide, me, g)
    yield


def run(*streams):
    live = list(streams)
    while live:
        live = [s for s in live if next(s, StopIteration) is not StopIteration]


def chain(*streams):
    for s in streams:
        yield from s


def reduce_shapes():
    shapes = []
    for g in range(3):
        for p in range(2):
            n, low = PART[g][p], LOW[g][p]
            high = n - low
            shapes += [
                ((4, 4, 48, n), BF),
                ((4, 48, low), BF),
                ((4, 48, high), BF),
                ((4, 48, n), BF),
                ((4, 48, n), BF),
                ((48, low), BF),
                ((48, high), BF),
                ((48, n), BF),
                ((48, n), BF),
            ]
    return shapes


def reduce_stream(wire, wide, down, bufs, tail, g, p):
    me = wire.place
    sb, b1p, b1m, b2p, b2m, c1p, c1m, c2p, c2m = bufs
    low, n = LOW[g][p], PART[g][p]
    lo, hi = pl.ds(0, low), pl.ds(low, n - low)

    def first(d):
        return me.dev(dx=d) if p == 0 else me.dev(dy=d)

    def second(d):
        return me.dev(dy=d) if p == 0 else me.dev(dx=d)

    u, w = (me.x, me.y) if p == 0 else (me.y, me.x)

    def one(ui, wi, h=None, c=me.c):
        bx, by = (ui, wi) if p == 0 else (wi, ui)
        return block(wide, down, g, p, c, bx, by, h)

    def line(ui, h=None, c=me.c):
        bx, by = (ui, slice(None)) if p == 0 else (slice(None), ui)
        return block(wide, down, g, p, c, bx, by, h)

    def everything(c):
        return block(wide, down, g, p, c, slice(None), slice(None))

    def add_line(ui, h, fn):
        def body(i, _):
            ref = one(ui, i, h)
            ref[...] = fn(ref[...], i)
            return 0
        lax.fori_loop(0, 4, body, 0)

    got = wire.put(everything(1 - me.c), sb, me.sibling())
    yield
    got.wait_recv()

    def with_sibling(ui):
        def fn(v, i):
            bx, by = (ui, i) if p == 0 else (i, ui)
            return v + sb[bx, by]
        add_line(ui, None, fn)

    with_sibling(wrap(u, 2))
    r1p = wire.put(line(wrap(u, 2), 0), b1p, first(1))
    r1m = wire.put(line(wrap(u, 2), 1), b1m, first(-1))
    with_sibling(wrap(u, 1))
    r2p_hi = wire.put(line(wrap(u, 1), 1), b2p.at[:, :, hi], first(1))
    with_sibling(wrap(u, -1))
    r2m_lo = wire.put(line(wrap(u, -1), 0), b2m.at[:, :, lo], first(-1))
    with_sibling(u)
    yield
    r1p.wait_recv()
    add_line(wrap(u, 1), 0, lambda v, i: v + b1p[i])
    r2p_lo = wire.put(line(wrap(u, 1), 0), b2p.at[:, :, lo], first(1))
    r1m.wait_recv()
    add_line(wrap(u, -1), 1, lambda v, i: v + b1m[i])
    r2m_hi = wire.put(line(wrap(u, -1), 1), b2m.at[:, :, hi], first(-1))
    yield
    for copy in (r2p_hi, r2m_lo, r2p_lo, r2m_hi):
        copy.wait_recv()

    def close(wi):
        ref = one(u, wi)
        total = ref[...].astype(F32) + b2p[wi].astype(F32) + b2m[wi].astype(F32)
        ref[...] = total.astype(BF)

    close(wrap(w, 2))
    r1p = wire.put(one(u, wrap(w, 2), 0), c1p, second(1))
    r1m = wire.put(one(u, wrap(w, 2), 1), c1m, second(-1))
    close(wrap(w, 1))
    r2p_hi = wire.put(one(u, wrap(w, 1), 1), c2p.at[:, hi], second(1))
    close(wrap(w, -1))
    r2m_lo = wire.put(one(u, wrap(w, -1), 0), c2m.at[:, lo], second(-1))
    close(w)
    yield
    r1p.wait_recv()
    ref = one(u, wrap(w, 1), 0)
    ref[...] = ref[...] + c1p[...]
    r2p_lo = wire.put(ref, c2p.at[:, lo], second(1))
    r1m.wait_recv()
    ref = one(u, wrap(w, -1), 1)
    ref[...] = ref[...] + c1m[...]
    r2m_hi = wire.put(ref, c2m.at[:, hi], second(-1))
    yield
    for copy in (r2p_hi, r2m_lo, r2p_lo, r2m_hi):
        copy.wait_recv()
    total = one(u, w)[...].astype(F32) + c2p[...].astype(F32) + c2m[...].astype(F32)
    yield from tail(wire, total, g, p)


def tail_shapes():
    shapes = []
    for g in range(2):
        for p in range(2):
            n = PART[g][p]
            shapes += [((4, 16, n), BF), ((2, 16, n), BF), ((2, 16, n), BF), ((2, 16, n), BF), ((16, n), F32)]
    shapes += [((2, 48, 768), BF), ((48, 768), BF), ((48, 768), BF), ((48, 768), BF)]
    return shapes


def make_tail(bufs, final, final_down):
    done = []

    def tail(wire, total, g, p):
        me = wire.place
        if g < 2:
            st, rz, tt, rr, so = bufs[10 * g + 5 * p : 10 * g + 5 * p + 5]
            at = cols(g, p, me.c)
            zero = jnp.zeros((4, total.shape[1]), F32)
            for o in range(4):
                st[o] = jnp.concatenate([total[12 * o : 12 * o + 12], zero], axis=0).astype(BF)
            a = wire.put(st.at[pl.ds(2 * (1 - me.zl), 2)], rz, me.pair())
            yield
            a.wait_recv()
            tt[...] = (st[pl.ds(2 * me.zl, 2)].astype(F32) + rz[...].astype(F32)).astype(BF)
            b = wire.put(tt, rr, me.other())
            yield
            b.wait_recv()
            so[...] = tt[1 - me.c].astype(F32) + rr[1 - me.c].astype(F32)
            c = wire.put(so, final.at[:, at], me.sibling())
            final[:, at] = tt[me.c].astype(F32) + rr[me.c].astype(F32)
            yield
            c.wait_recv()
            yield
        else:
            sd, rz, tt, rr = bufs[20:24]
            sd[p] = total.astype(BF)
            done.append(p)
            if len(done) < 2:
                return
            a = wire.put(sd.at[1 - me.zl], rz, me.pair())
            yield
            a.wait_recv()
            tt[...] = (sd[me.zl].astype(F32) + rz[...].astype(F32)).astype(BF)
            b = wire.put(tt, rr, me.other())
            yield
            b.wait_recv()
            final_down[...] = tt[...].astype(F32) + rr[...].astype(F32)
            yield

    return tail


def gather_kernel(own, own_down, wide, down, stage, send, recv):
    place = Place()
    greet(place)
    wire = Wire(place, send, recv)
    front = [gather_stage0(wire, own, own_down, stage, wide, down, g) for g in range(3)]
    run(*front)
    run(*[gather_stream(wire, wide, down, g, p) for g in range(3) for p in range(2)])
    wire.drain()


def reduce_kernel(g_wide, g_down, final, final_down, wide, down, sems, *rest):
    nb = len(reduce_shapes())
    bufs, tbufs, (send, recv) = rest[:nb], rest[nb:-2], rest[-2:]
    place = Place()
    greet(place)
    a = pltpu.make_async_copy(g_wide, wide, sems.at[0])
    b = pltpu.make_async_copy(g_down, down, sems.at[1])
    a.start()
    b.start()
    a.wait()
    b.wait()
    wire = Wire(place, send, recv)
    tail = make_tail(tbufs, final, final_down)
    streams = []
    for g in (2, 1, 0):
        for p in range(2):
            k = 9 * (2 * g + p)
            streams.append(reduce_stream(wire, wide, down, bufs[k : k + 9], tail, g, p))
    run(*streams)
    wire.drain()


ANY = pl.BlockSpec(memory_space=pl.ANY)
VM = pl.BlockSpec(memory_space=pltpu.VMEM)


def gather_call(own, own_down):
    return pl.pallas_call(
        gather_kernel,
        out_shape=(
            jax.ShapeDtypeStruct((4, 4, 48, WIDE), BF),
            jax.ShapeDtypeStruct((4, 4, 2, 2, 48, 768), BF),
        ),
        in_specs=[VM, VM],
        out_specs=(VM, VM),
        scratch_shapes=[
            pltpu.VMEM((4, 16, WIDE), BF),
            pltpu.SemaphoreType.DMA((N_SEND,)),
            pltpu.SemaphoreType.DMA((N_RECV,)),
        ],
        compiler_params=pltpu.CompilerParams(
            collective_id=0, has_side_effects=True, vmem_limit_bytes=56 << 20
        ),
        name="gather",
    )(own, own_down)


def reduce_call(g_wide, g_down):
    return pl.pallas_call(
        reduce_kernel,
        out_shape=(
            jax.ShapeDtypeStruct((16, WIDE), F32),
            jax.ShapeDtypeStruct((48, 768), F32),
        ),
        in_specs=[ANY, ANY],
        out_specs=(VM, VM),
        scratch_shapes=[
            pltpu.VMEM((4, 4, 48, WIDE), BF),
            pltpu.VMEM((4, 4, 2, 2, 48, 768), BF),
            pltpu.SemaphoreType.DMA((2,)),
            *[pltpu.VMEM(s, t) for s, t in reduce_shapes()],
            *[pltpu.VMEM(s, t) for s, t in tail_shapes()],
            pltpu.SemaphoreType.DMA((N_SEND,)),
            pltpu.SemaphoreType.DMA((N_RECV,)),
        ],
        compiler_params=pltpu.CompilerParams(
            collective_id=1, has_side_effects=True, vmem_limit_bytes=56 << 20
        ),
        name="reduce",
    )(g_wide, g_down)


def pack_own(n1g, n1b, wq, wk, wv, wo, n2g, n2b, wu):
    def pad(*vs):
        return jnp.pad(jnp.stack(vs, axis=1), ((0, 0), (0, 128 - len(vs))))

    own = jnp.concatenate([wq, wk, wv, pad(n1g, n1b), pad(n2g, n2b), wo, wu], axis=1)
    return jnp.pad(own, ((0, 4), (0, 0)))


def layer_norm(values, gain, shift):
    centre = jnp.mean(values, axis=-1, keepdims=True)
    centred = values - centre
    spread = jnp.mean(centred * centred, axis=-1, keepdims=True)
    return centred * lax.rsqrt(spread + 1e-05) * gain + shift


def masked_scores(query, key, segment_ids):
    tokens = query.shape[0]
    query_heads = query.reshape(tokens, HEADS, HEAD_DIM)
    key_heads = key.reshape(tokens, HEADS, HEAD_DIM)
    scaled = jnp.einsum(
        "qhd,khd->hqk", query_heads, key_heads, preferred_element_type=jnp.float32
    ) * HEAD_DIM ** (-0.5)
    segments = segment_ids.reshape(tokens)
    rows_iota = lax.broadcasted_iota(jnp.int32, (tokens, tokens), 0)
    cols_iota = lax.broadcasted_iota(jnp.int32, (tokens, tokens), 1)
    allowed = (rows_iota >= cols_iota) & (segments[:, None] == segments[None, :])
    return jnp.where(allowed[None], scaled, -1e30)


def matmul_back(left, right):
    return jnp.einsum("te,de->td", left, right, preferred_element_type=jnp.float32)


def matmul_outer(left, right):
    return jnp.einsum("td,te->de", left, right, preferred_element_type=jnp.float32)


def per_device(
    block_input, segment_ids, norm1_gain, norm1_bias, query_weight, key_weight, value_weight, out_weight,
    norm2_gain, norm2_bias, up_weight, down_weight, out_cotangent,
):
    tokens = block_input.shape[0]
    inputs = block_input.astype(F32)
    own = pack_own(
        norm1_gain, norm1_bias, query_weight, key_weight, value_weight, out_weight, norm2_gain, norm2_bias, up_weight
    )
    wide, down = gather_call(own, down_weight)
    wide = wide.reshape(D, WIDE)
    down = down.reshape(FF, D)
    wq, wk, wv = wide[:, :768], wide[:, 768:1536], wide[:, 1536:2304]
    gain1, bias1 = wide[:, 2304].astype(F32), wide[:, 2305].astype(F32)
    gain2, bias2 = wide[:, 2432].astype(F32), wide[:, 2433].astype(F32)
    wo, wu = wide[:, 2560:3328], wide[:, 3328:]
    normed1_f, norm1_pull = jax.vjp(layer_norm, inputs, gain1, bias1)
    normed1 = normed1_f.astype(jnp.bfloat16)
    query = jnp.dot(normed1, wq, preferred_element_type=jnp.float32).astype(jnp.bfloat16)
    key = jnp.dot(normed1, wk, preferred_element_type=jnp.float32).astype(jnp.bfloat16)
    value = jnp.dot(normed1, wv, preferred_element_type=jnp.float32).astype(jnp.bfloat16)
    scores = masked_scores(query, key, segment_ids)
    maximum = jnp.max(scores, axis=-1, keepdims=True)
    exponent = jnp.exp(scores - maximum)
    summed = jnp.sum(exponent, axis=-1, keepdims=True)
    probs = exponent / summed
    log_total = maximum + jnp.log(summed)
    value_heads = value.reshape(tokens, HEADS, HEAD_DIM)
    mixed = jnp.einsum(
        "hqk,khd->qhd", probs.astype(jnp.bfloat16), value_heads, preferred_element_type=jnp.float32
    )
    mixed = mixed.reshape(tokens, HEADS * HEAD_DIM).astype(jnp.bfloat16)
    hidden_state = inputs + jnp.dot(mixed, wo, preferred_element_type=jnp.float32)
    normed2_f, norm2_pull = jax.vjp(layer_norm, hidden_state, gain2, bias2)
    normed2 = normed2_f.astype(jnp.bfloat16)
    pre_act = jnp.dot(normed2, wu, preferred_element_type=jnp.float32)
    activated_f, gelu_pull = jax.vjp(jax.nn.gelu, pre_act)
    activated = activated_f.astype(jnp.bfloat16)
    output = (
        hidden_state + jnp.dot(activated, down, preferred_element_type=jnp.float32)
    ).astype(jnp.bfloat16)
    down_term = matmul_outer(activated, out_cotangent)
    act_grad = matmul_back(out_cotangent, down)
    pre_grad = gelu_pull(act_grad)[0].astype(jnp.bfloat16)
    up_term = matmul_outer(normed2, pre_grad)
    normed2_grad = matmul_back(pre_grad, wu)
    hidden_extra, gain2_term, bias2_term = norm2_pull(normed2_grad)
    hidden_grad = out_cotangent.astype(jnp.float32) + hidden_extra
    branch_grad = hidden_grad.astype(jnp.bfloat16)
    outproj_term = matmul_outer(mixed, branch_grad)
    mixed_grad = matmul_back(branch_grad, wo).astype(jnp.bfloat16)
    mixed_heads = mixed_grad.reshape(tokens, HEADS, HEAD_DIM)
    again_probs = jnp.exp(masked_scores(query, key, segment_ids) - log_total)
    prob_grad = jnp.einsum(
        "qhd,khd->hqk", mixed_heads, value_heads, preferred_element_type=jnp.float32
    )
    value_act = jnp.einsum(
        "hqk,qhd->khd",
        again_probs.astype(jnp.bfloat16),
        mixed_heads,
        preferred_element_type=jnp.float32,
    )
    value_act = value_act.reshape(tokens, HEADS * HEAD_DIM).astype(jnp.bfloat16)
    row_dot = jnp.sum(prob_grad * again_probs, axis=-1, keepdims=True)
    score_grad = (again_probs * (prob_grad - row_dot)).astype(jnp.bfloat16)
    query_heads = query.reshape(tokens, HEADS, HEAD_DIM)
    key_heads = key.reshape(tokens, HEADS, HEAD_DIM)
    query_act = jnp.einsum(
        "hqk,khd->qhd", score_grad, key_heads, preferred_element_type=jnp.float32
    ) * HEAD_DIM ** (-0.5)
    key_act = jnp.einsum(
        "hqk,qhd->khd", score_grad, query_heads, preferred_element_type=jnp.float32
    ) * HEAD_DIM ** (-0.5)
    query_act = query_act.reshape(tokens, HEADS * HEAD_DIM).astype(jnp.bfloat16)
    key_act = key_act.reshape(tokens, HEADS * HEAD_DIM).astype(jnp.bfloat16)
    query_term = matmul_outer(normed1, query_act)
    key_term = matmul_outer(normed1, key_act)
    value_term = matmul_outer(normed1, value_act)
    normed1_grad = (
        matmul_back(query_act, wq)
        + matmul_back(key_act, wk)
        + matmul_back(value_act, wv)
    )
    input_extra, gain1_term, bias1_term = norm1_pull(normed1_grad)
    input_grad = hidden_grad + input_extra

    def columns(*vs):
        return jnp.pad(jnp.stack(vs, axis=1), ((0, 0), (0, 128 - len(vs)))).astype(BF)

    g_wide = jnp.concatenate(
        [
            query_term.astype(BF),
            key_term.astype(BF),
            value_term.astype(BF),
            columns(gain1_term, bias1_term),
            columns(gain2_term, bias2_term),
            outproj_term.astype(BF),
            up_term.astype(BF),
        ],
        axis=1,
    ).reshape(4, 4, 48, WIDE)
    g_down = down_term.astype(BF).reshape(4, 4, 2, 2, 48, 768)
    total, down_total = reduce_call(g_wide, g_down)
    total = total[:12]
    return (
        output,
        input_grad,
        total[:, 2304],
        total[:, 2305],
        total[:, :768],
        total[:, 768:1536],
        total[:, 1536:2304],
        total[:, 2560:3328],
        total[:, 2432],
        total[:, 2433],
        total[:, 3328:],
        down_total,
    )


def solution(mesh):
    placed = (
        P(("fsdp", "rep"), None),
        P(("fsdp", "rep"), None),
        P("fsdp"),
        P("fsdp"),
        P("fsdp", None),
        P("fsdp", None),
        P("fsdp", None),
        P("fsdp", None),
        P("fsdp"),
        P("fsdp"),
        P("fsdp", None),
        P("fsdp", None),
        P(("fsdp", "rep"), None),
    )
    return jax.shard_map(
        per_device,
        mesh=mesh,
        in_specs=placed,
        out_specs=(
            P(("fsdp", "rep"), None),
            P(("fsdp", "rep"), None),
            P("fsdp"),
            P("fsdp"),
            P("fsdp", None),
            P("fsdp", None),
            P("fsdp", None),
            P("fsdp", None),
            P("fsdp"),
            P("fsdp"),
            P("fsdp", None),
            P("fsdp", None),
        ),
        check_vma=False,
    )
```

```python
import functools

import jax
import jax.numpy as jnp
from jax import lax
from jax.experimental import pallas as pl
from jax.experimental.pallas import tpu as pltpu
from jax.sharding import PartitionSpec as P

HEADS = 24
HEAD_DIM = 32
D = 768
FF = 3072
BF = jnp.bfloat16
F32 = jnp.float32
MESH = pl.DeviceIdType.MESH

WIDE = 6400
START = (0, 2560)
HALF = (1280, 1920)
PART = ((640, 640), (896, 1024), (768, 768))
LOW = ((256, 256), (384, 512), (384, 384))
N_RECV = 340
VMEM_BYTES = 63 << 20
N_SEND = 48


class Place:
    def __init__(self):
        f = lax.axis_index("fsdp")
        self.r = lax.axis_index("rep")
        self.c = lax.rem(f, 2)
        self.zl = lax.rem(lax.div(f, 2), 2)
        self.y = lax.rem(lax.div(f, 4), 4)
        self.x = lax.div(f, 16)

    def dev(self, dx=0, dy=0, zl=None, c=None, r=None):
        x, y = wrap(self.x, dx), wrap(self.y, dy)
        zl = self.zl if zl is None else zl
        c = self.c if c is None else c
        return {"fsdp": x * 16 + y * 4 + zl * 2 + c, "rep": self.r if r is None else r}

    def sibling(self):
        return self.dev(c=1 - self.c)

    def pair(self):
        return self.dev(zl=1 - self.zl)

    def other(self):
        return self.dev(r=1 - self.r)


def wrap(v, d):
    return v if d == 0 else lax.rem(v + (d + 4), 4)


class Wire:
    def __init__(self, place, send, recv):
        self.place, self.send_sem, self.recv_sem = place, send, recv
        self.n = self.m = 0
        self.open = {}

    def slot(self):
        k = self.m % N_SEND
        self.m += 1
        if k in self.open:
            self.open.pop(k).wait_send()
        return k

    def put(self, src, dst, to):
        k = self.slot()
        assert self.n < N_RECV
        copy = pltpu.make_async_remote_copy(
            src_ref=src,
            dst_ref=dst,
            send_sem=self.send_sem.at[k],
            recv_sem=self.recv_sem.at[self.n],
            device_id=to,
            device_id_type=MESH,
        )
        copy.start()
        self.open[k] = copy
        self.n += 1
        return copy

    def drain(self):
        for copy in self.open.values():
            copy.wait_send()
        self.open = {}


def greet(place):
    barrier = pltpu.get_barrier_semaphore()
    peers = [place.sibling(), place.pair(), place.other()]
    peers += [place.dev(dx=1), place.dev(dx=-1), place.dev(dy=1), place.dev(dy=-1)]
    for peer in peers:
        pl.semaphore_signal(barrier, inc=1, device_id=peer, device_id_type=MESH)
    pl.semaphore_wait(barrier, len(peers))


def span(g, p, h):
    if h is None:
        return 0, PART[g][p]
    return (0, LOW[g][p]) if h == 0 else (LOW[g][p], PART[g][p] - LOW[g][p])


def cols(g, p, c, h=None):
    off, width = span(g, p, h)
    base = START[g] + (PART[g][0] if p else 0) + off
    return pl.ds(pl.multiple_of(base + c * HALF[g], 128), width)


def block(wide, down, g, p, c, bx, by, h=None):
    if g < 2:
        return wide.at[bx, by, :, cols(g, p, c, h)]
    off, width = span(g, p, h)
    return down.at[bx, by, p, c, :, pl.ds(off, width)]


def gather_stream(wire, wide, down, g, p):
    me = wire.place

    def piece(du, dw, h=None, c=me.c):
        dx, dy = (du, dw) if p == 0 else (dw, du)
        return block(wide, down, g, p, c, wrap(me.x, dx), wrap(me.y, dy), h)

    def first(d):
        return me.dev(dx=d) if p == 0 else me.dev(dy=d)

    def second(d):
        return me.dev(dy=d) if p == 0 else me.dev(dx=d)

    def go(du, dw, to, h=None):
        ref = piece(du, dw, h)
        return wire.put(ref, ref, to)

    sib = []
    up, dn = {}, {}

    def spread(du):
        up[du] = go(du, 0, second(1))
        dn[du] = go(du, 0, second(-1))

    a, b = go(0, 0, first(1)), go(0, 0, first(-1))
    spread(0)
    yield
    a.wait_recv()
    far_a = go(-1, 0, first(1), 0)
    spread(-1)
    sib.append(go(-1, 0, me.sibling()))
    b.wait_recv()
    far_b = go(1, 0, first(-1), 1)
    spread(1)
    sib.append(go(1, 0, me.sibling()))
    yield
    far_a.wait_recv()
    far_b.wait_recv()
    spread(2)
    sib.append(go(2, 0, me.sibling()))
    yield
    far = {}
    for du in (0, -1, 1, 2):
        up[du].wait_recv()
        far_a = go(du, -1, second(1), 0)
        sib.append(go(du, -1, me.sibling()))
        dn[du].wait_recv()
        far_b = go(du, 1, second(-1), 1)
        sib.append(go(du, 1, me.sibling()))
        far[du] = far_a, far_b
        if du == -1:
            yield
    yield
    for du in (0, -1, 1, 2):
        far[du][0].wait_recv()
        far[du][1].wait_recv()
        sib.append(go(du, 2, me.sibling()))
    yield
    for copy in sib:
        copy.wait_recv()
    yield


def join(stage, wide, me, g):
    width = 2 * HALF[g]
    step = 640

    def body(i, _):
        at = pl.ds(pl.multiple_of(START[g] + i * step, 128), step)
        rows = [stage[o, :, at].astype(F32)[:12] for o in range(4)]
        wide[me.x, me.y, :, at] = jnp.concatenate(rows, axis=0).astype(BF)
        return 0
    lax.fori_loop(0, width // step, body, 0)


def gather_stage0(wire, own_down, stage, wide, down, g):
    me = wire.place
    mine = 2 * me.zl + me.c
    if g < 2:
        at = pl.ds(START[g], 2 * HALF[g])
        src, dst = stage.at[mine, :, at], lambda o: stage.at[o, :, at]
        hers = stage.at[2 * (1 - me.zl) + me.c, :, at]
    else:
        src, dst = own_down, lambda o: down.at[me.x, me.y, me.zl, me.c]
        hers = down.at[me.x, me.y, 1 - me.zl, me.c]
        down[me.x, me.y, me.zl, me.c] = own_down[...]
    a = wire.put(src, dst(mine), me.pair())
    b = wire.put(src, dst(mine), me.sibling())
    yield
    a.wait_recv()
    c = wire.put(hers, hers, me.sibling())
    yield
    b.wait_recv()
    c.wait_recv()
    if g < 2:
        join(stage, wide, me, g)
    yield


def run(*streams):
    live = list(streams)
    while live:
        live = [s for s in live if next(s, StopIteration) is not StopIteration]


def chain(*streams):
    for s in streams:
        yield from s


def reduce_shapes():
    shapes = []
    for g in range(3):
        for p in range(2):
            n, low = PART[g][p], LOW[g][p]
            high = n - low
            shapes += [
                ((4, 4, 48, n), BF),
                ((4, 48, low), BF),
                ((4, 48, high), BF),
                ((4, 48, n), BF),
                ((4, 48, n), BF),
                ((48, low), BF),
                ((48, high), BF),
                ((48, n), BF),
                ((48, n), BF),
            ]
    return shapes


def reduce_stream(wire, wide, down, bufs, tail, g, p):
    me = wire.place
    sb, b1p, b1m, b2p, b2m, c1p, c1m, c2p, c2m = bufs
    low, n = LOW[g][p], PART[g][p]
    lo, hi = pl.ds(0, low), pl.ds(low, n - low)

    def first(d):
        return me.dev(dx=d) if p == 0 else me.dev(dy=d)

    def second(d):
        return me.dev(dy=d) if p == 0 else me.dev(dx=d)

    u, w = (me.x, me.y) if p == 0 else (me.y, me.x)

    def one(ui, wi, h=None, c=me.c):
        bx, by = (ui, wi) if p == 0 else (wi, ui)
        return block(wide, down, g, p, c, bx, by, h)

    def line(ui, h=None, c=me.c):
        bx, by = (ui, slice(None)) if p == 0 else (slice(None), ui)
        return block(wide, down, g, p, c, bx, by, h)

    def everything(c):
        return block(wide, down, g, p, c, slice(None), slice(None))

    def add_line(ui, h, fn):
        def body(i, _):
            ref = one(ui, i, h)
            ref[...] = fn(ref[...], i)
            return 0
        lax.fori_loop(0, 4, body, 0)

    got = wire.put(everything(1 - me.c), sb, me.sibling())
    yield
    got.wait_recv()

    def with_sibling(ui):
        def fn(v, i):
            bx, by = (ui, i) if p == 0 else (i, ui)
            return v + sb[bx, by]
        add_line(ui, None, fn)

    with_sibling(wrap(u, 2))
    r1p = wire.put(line(wrap(u, 2), 0), b1p, first(1))
    r1m = wire.put(line(wrap(u, 2), 1), b1m, first(-1))
    with_sibling(wrap(u, 1))
    r2p_hi = wire.put(line(wrap(u, 1), 1), b2p.at[:, :, hi], first(1))
    with_sibling(wrap(u, -1))
    r2m_lo = wire.put(line(wrap(u, -1), 0), b2m.at[:, :, lo], first(-1))
    with_sibling(u)
    yield
    r1p.wait_recv()
    add_line(wrap(u, 1), 0, lambda v, i: v + b1p[i])
    r2p_lo = wire.put(line(wrap(u, 1), 0), b2p.at[:, :, lo], first(1))
    r1m.wait_recv()
    add_line(wrap(u, -1), 1, lambda v, i: v + b1m[i])
    r2m_hi = wire.put(line(wrap(u, -1), 1), b2m.at[:, :, hi], first(-1))
    yield
    for copy in (r2p_hi, r2m_lo, r2p_lo, r2m_hi):
        copy.wait_recv()

    def close(wi):
        ref = one(u, wi)
        total = ref[...].astype(F32) + b2p[wi].astype(F32) + b2m[wi].astype(F32)
        ref[...] = total.astype(BF)

    close(wrap(w, 2))
    r1p = wire.put(one(u, wrap(w, 2), 0), c1p, second(1))
    r1m = wire.put(one(u, wrap(w, 2), 1), c1m, second(-1))
    close(wrap(w, 1))
    r2p_hi = wire.put(one(u, wrap(w, 1), 1), c2p.at[:, hi], second(1))
    close(wrap(w, -1))
    r2m_lo = wire.put(one(u, wrap(w, -1), 0), c2m.at[:, lo], second(-1))
    close(w)
    yield
    r1p.wait_recv()
    ref = one(u, wrap(w, 1), 0)
    ref[...] = ref[...] + c1p[...]
    r2p_lo = wire.put(ref, c2p.at[:, lo], second(1))
    r1m.wait_recv()
    ref = one(u, wrap(w, -1), 1)
    ref[...] = ref[...] + c1m[...]
    r2m_hi = wire.put(ref, c2m.at[:, hi], second(-1))
    yield
    for copy in (r2p_hi, r2m_lo, r2p_lo, r2m_hi):
        copy.wait_recv()
    total = one(u, w)[...].astype(F32) + c2p[...].astype(F32) + c2m[...].astype(F32)
    yield from tail(wire, total, g, p)


def tail_shapes():
    shapes = []
    for g in range(2):
        for p in range(2):
            n = PART[g][p]
            shapes += [((4, 16, n), BF), ((2, 16, n), BF), ((2, 16, n), BF), ((2, 16, n), BF), ((16, n), F32)]
    shapes += [((2, 48, 768), BF), ((48, 768), BF), ((48, 768), BF), ((48, 768), BF)]
    return shapes


def make_tail(bufs, final, final_down):
    done = []

    def tail(wire, total, g, p):
        me = wire.place
        if g < 2:
            st, rz, tt, rr, so = bufs[10 * g + 5 * p : 10 * g + 5 * p + 5]
            at = cols(g, p, me.c)
            zero = jnp.zeros((4, total.shape[1]), F32)
            for o in range(4):
                st[o] = jnp.concatenate([total[12 * o : 12 * o + 12], zero], axis=0).astype(BF)
            a = wire.put(st.at[pl.ds(2 * (1 - me.zl), 2)], rz, me.pair())
            yield
            a.wait_recv()
            tt[...] = (st[pl.ds(2 * me.zl, 2)].astype(F32) + rz[...].astype(F32)).astype(BF)
            b = wire.put(tt, rr, me.other())
            yield
            b.wait_recv()
            so[...] = tt[1 - me.c].astype(F32) + rr[1 - me.c].astype(F32)
            c = wire.put(so, final.at[:, at], me.sibling())
            final[:, at] = tt[me.c].astype(F32) + rr[me.c].astype(F32)
            yield
            c.wait_recv()
            yield
        else:
            sd, rz, tt, rr = bufs[20:24]
            sd[p] = total.astype(BF)
            done.append(p)
            if len(done) < 2:
                return
            a = wire.put(sd.at[1 - me.zl], rz, me.pair())
            yield
            a.wait_recv()
            tt[...] = (sd[me.zl].astype(F32) + rz[...].astype(F32)).astype(BF)
            b = wire.put(tt, rr, me.other())
            yield
            b.wait_recv()
            final_down[...] = tt[...].astype(F32) + rr[...].astype(F32)
            yield

    return tail


def dot(a, b):
    return lax.dot_general(a, b, (((1,), (0,)), ((), ())), preferred_element_type=F32)


def dot_nt(a, b):
    return lax.dot_general(a, b, (((1,), (1,)), ((), ())), preferred_element_type=F32)


def loop(n, body):
    def step(i, carry):
        body(i)
        return carry

    lax.fori_loop(0, n, step, 0)


def ds(i, n):
    return pl.ds(pl.multiple_of(i * n, n), n)


T = 256
SCALE = HEAD_DIM ** (-0.5)
O_AT, UP_AT, N1_AT, N2_AT = 2560, 3328, 2304, 2432
ROW = 64


def standardise(v):
    centre = jnp.mean(v, axis=-1, keepdims=True)
    centred = v - centre
    spread = jnp.mean(centred * centred, axis=-1, keepdims=True)
    rstd = lax.rsqrt(spread + 1e-05)
    return centred * rstd, rstd


def weight(wide, at, width):
    return wide[:, :, :, pl.ds(at, width)].reshape(D, width)


def layer_kernel(
    x_ref, seg_ref, n1g_ref, n1b_ref, wq_ref, wk_ref, wv_ref, wo_ref, n2g_ref, n2b_ref, wu_ref, wd_ref, cot_ref,
    out_ref, ig_ref, dn1g_ref, dn1b_ref, dq_ref, dk_ref, dv_ref, do_ref, dn2g_ref, dn2b_ref, du_ref, dd_ref,
    *scratch,
):
    nb, nt = len(reduce_shapes()), len(tail_shapes())
    bufs, scratch = scratch[:nb], scratch[nb:]
    tbufs, scratch = scratch[:nt], scratch[nt:]
    (
        wide, down, gwide, gdown, stage, final, final_down,
        mask, xhat, rstd1, xhat2, rstd2, n1, n1t, n2, qkv, mixed, probs, hidden,
        act, slope, acc_out, acc_in, dqkv, rows1, rows2, send, recv,
    ) = scratch
    place = me = Place()
    greet(place)
    wire = Wire(place, send, recv)
    mine = 2 * me.zl + me.c

    zero4 = lambda n: jnp.zeros((4, n), F32)

    def put_own(ref, at):
        n = ref.shape[1]
        rows = jnp.concatenate([ref[...].astype(F32), zero4(n)], axis=0)
        stage[mine, :, pl.ds(at, n)] = rows.astype(BF)

    def put_norm(gain, shift, at):
        eye = lax.broadcasted_iota(jnp.int32, (16, 12), 0) == lax.broadcasted_iota(jnp.int32, (16, 12), 1)
        lane = lax.broadcasted_iota(jnp.int32, (16, 128), 1)
        a = jnp.sum(jnp.where(eye, gain[...].astype(F32), 0.0), axis=1, keepdims=True)
        b = jnp.sum(jnp.where(eye, shift[...].astype(F32), 0.0), axis=1, keepdims=True)
        both = jnp.where(lane == 0, a, jnp.where(lane == 1, b, 0.0))
        stage[mine, :, pl.ds(at, 128)] = both.astype(BF)

    for i, ref in enumerate((wq_ref, wk_ref, wv_ref)):
        put_own(ref, 768 * i)
    put_norm(n1g_ref, n1b_ref, N1_AT)
    put_norm(n2g_ref, n2b_ref, N2_AT)
    front = [gather_stage0(wire, wd_ref, stage, wide, down, g) for g in range(3)]
    next(front[0])
    put_own(wo_ref, O_AT)
    put_own(wu_ref, UP_AT)
    next(front[1])
    next(front[2])

    segs = jnp.broadcast_to(seg_ref[...], (T, T))
    rows_iota = lax.broadcasted_iota(jnp.int32, (T, T), 0)
    cols_iota = lax.broadcasted_iota(jnp.int32, (T, T), 1)
    allowed = (rows_iota >= cols_iota) & (segs.astype(F32).T == segs.astype(F32))
    mask[...] = jnp.where(allowed, 0.0, -1e30)

    next(front[0])

    def norm1_rows(i):
        at = ds(i, ROW)
        hat, rstd = standardise(x_ref[at, :].astype(F32))
        xhat[at, :] = hat
        rstd1[at, :] = rstd

    loop(T // ROW, norm1_rows)
    next(front[0])

    def gather(g):
        return [gather_stream(wire, wide, down, g, p) for p in range(2)]

    def step(streams):
        return [s for s in streams if next(s, StopIteration) is not StopIteration]

    g0 = step(gather(0))
    next(front[1])
    next(front[2])
    g0 = step(g0)
    next(front[1])
    g1 = step(gather(1))
    g0 = step(g0)
    next(front[2])
    g2 = step(gather(2))
    while g0:
        g0 = step(g0)
        g1 = step(g1)
        g2 = step(g2)

    eye = (
        lax.broadcasted_iota(jnp.int32, (128, 128), 0) == lax.broadcasted_iota(jnp.int32, (128, 128), 1)
    ).astype(BF)
    rows1[...] = dot_nt(eye, weight(wide, N1_AT, 128))[:8]
    rows2[...] = dot_nt(eye, weight(wide, N2_AT, 128))[:8]

    def norm1_apply(i):
        at = ds(i, ROW)
        n1[at, :] = (xhat[at, :] * rows1[0:1, :] + rows1[1:2, :]).astype(BF)

    loop(T // ROW, norm1_apply)

    def project(i):
        at = ds(i, 256)
        w = wide[:, :, :, at].reshape(D, 256)
        qkv[:, at] = dot(n1[...], w).astype(BF)

    loop(9, project)
    g1 = step(g1)
    g2 = step(g2)
    lane = lax.broadcasted_iota(jnp.int32, (1, 128), 1)
    heads = [((lane >= 32 * h) & (lane < 32 * h + 32)).astype(F32).astype(BF) for h in range(4)]

    def group(ref, which, t):
        return ref[:, pl.ds(pl.multiple_of(768 * which + 128 * t, 128), 128)]

    def attend(t):
        q4, k4, v4 = [group(qkv, i, t) for i in range(3)]
        vh = [v4 * heads[h] for h in range(4)]
        for rb in range(2):
            rows, nk = slice(128 * rb, 128 * rb + 128), 128 * rb + 128
            total = jnp.zeros((128, 128), F32)
            for h in range(4):
                s = dot_nt(q4[rows] * heads[h], k4[:nk]) * SCALE + mask[rows, :nk]
                e = jnp.exp(s - jnp.max(s, axis=1, keepdims=True))
                p = (e * (1.0 / jnp.sum(e, axis=1, keepdims=True))).astype(BF)
                probs[4 * t + h, rows, :nk] = p
                total = total + dot(p, vh[h][:nk])
            mixed[rows, pl.ds(pl.multiple_of(128 * t, 128), 128)] = total.astype(BF)

    for part in range(3):
        loop(2, lambda i: attend(2 * part + i))
        g1 = step(g1)
        g2 = step(g2)

    n2t, mixt = [gwide.at[:, :, :, pl.ds(256 * k, 256)] for k in range(2)]

    def transpose(src, dst):
        def body(i):
            dst[ds(i, 2)] = src[:, ds(i, 384)].T.reshape(2, 4, 48, T)

        loop(2, body)

    def turn_n1(i):
        n1t[ds(i, 384), :] = n1[:, ds(i, 384)].T

    transpose(mixed, mixt)
    loop(2, turn_n1)
    while g1:
        g1 = step(g1)
        g2 = step(g2)

    def out_project(i):
        at = ds(i, 256)
        w = wide[:, :, :, pl.ds(pl.multiple_of(O_AT + 256 * i, 128), 256)].reshape(D, 256)
        hidden[:, at] = x_ref[:, at].astype(F32) + dot(mixed[...], w)

    loop(3, out_project)

    def norm2_rows(i):
        at = ds(i, ROW)
        hat, rstd = standardise(hidden[at, :])
        xhat2[at, :] = hat
        rstd2[at, :] = rstd
        n2[at, :] = (hat * rows2[0:1, :] + rows2[1:2, :]).astype(BF)

    loop(T // ROW, norm2_rows)
    transpose(n2, n2t)

    c0 = (2.0 / 3.141592653589793) ** 0.5

    def feed(i):
        def part(j):
            at = pl.ds(pl.multiple_of(UP_AT + 768 * i + 256 * j, 128), 256)
            v = dot(n2[...], wide[:, :, :, at].reshape(D, 256))
            sq = v * v
            th = jnp.tanh(c0 * v * (1.0 + 0.044715 * sq))
            half = 0.5 + 0.5 * th
            a = (v * half).astype(BF)
            keep = pl.ds(pl.multiple_of(768 * i + 256 * j, 128), 256)
            act[:, keep] = a
            slope[:, keep] = half + 0.5 * v * (1.0 - th * th) * (c0 * (1.0 + 0.134145 * sq))

        loop(3, part)
        a = act[:, ds(i, 768)].T

        def grad(j):
            at = ds(j, 256)
            gdown[i, :, :, :, :, at] = dot(a, cot_ref[:, at]).astype(BF).reshape(4, 2, 2, 48, 256)

        loop(3, grad)

    loop(4, feed)
    reduced = make_tail(tbufs, final, final_down)

    def reduce(g):
        return [
            reduce_stream(wire, gwide, gdown, bufs[9 * (2 * g + p) : 9 * (2 * g + p) + 9], reduced, g, p)
            for p in range(2)
        ]

    r2 = step(reduce(2))
    while g2:
        g2 = step(g2)
    r2 = step(r2)

    acc_out[...] = hidden[...]
    acc_in[...] = jnp.zeros((T, D), F32)

    def feed_back(i):
        at = ds(i, 768)
        wd = down[i].reshape(768, 768)
        acc_out[...] += dot(act[:, at], wd)
        pg = (dot_nt(cot_ref[...], wd) * slope[:, at]).astype(BF)
        act[:, at] = pg
        up_at = pl.ds(pl.multiple_of(UP_AT + 768 * i, 128), 768)
        acc_in[...] += dot_nt(pg, wide[:, :, :, up_at].reshape(D, 768))

        def grad(j):
            cols_j = pl.ds(pl.multiple_of(UP_AT + 768 * i + 256 * j, 128), 256)
            pg_j = act[:, pl.ds(pl.multiple_of(768 * i + 256 * j, 128), 256)]
            gwide[:, :, :, cols_j] = dot(n2t[...].reshape(D, T), pg_j).astype(BF).reshape(4, 4, 48, 256)

        loop(3, grad)

    for part in range(2):
        loop(2, lambda i: feed_back(2 * part + i))
        r2 = step(r2)
    out_ref[...] = acc_out[...].astype(BF)

    def norm_back(grad, hat, rstd, gain, at):
        gn = gain * grad
        m1 = jnp.mean(gn, axis=-1, keepdims=True)
        m2 = jnp.mean(gn * hat, axis=-1, keepdims=True)
        return (gn - m1 - hat * m2) * rstd

    def norm2_back(i, sums):
        at = ds(i, ROW)
        grad, hat = acc_in[at, :], xhat2[at, :]
        extra = norm_back(grad, hat, rstd2[at, :], rows2[0:1, :], at)
        hidden[at, :] = cot_ref[at, :].astype(F32) + extra
        a, b = sums
        return a + jnp.sum(grad * hat, axis=0, keepdims=True), b + jnp.sum(grad, axis=0, keepdims=True)

    def as_columns(sums, at):
        rows = jnp.concatenate([*sums, jnp.zeros((126, D), F32)], axis=0)
        gwide[:, :, :, pl.ds(at, 128)] = rows.T.astype(BF).reshape(4, 4, 48, 128)

    nothing = jnp.zeros((1, D), F32)
    as_columns(lax.fori_loop(0, T // ROW, norm2_back, (nothing, nothing)), N2_AT)
    n2[...] = hidden[...].astype(BF)

    def o_back(i):
        at = ds(i, 256)
        b = n2[:, at]
        gwide[:, :, :, pl.ds(pl.multiple_of(O_AT + 256 * i, 128), 256)] = (
            dot(mixt[...].reshape(D, T), b).astype(BF).reshape(4, 4, 48, 256)
        )

    loop(3, o_back)
    r1 = step(reduce(1))
    mgrad = n1
    mgrad[...] = dot_nt(n2[...], weight(wide, O_AT, D)).astype(BF)
    r2 = step(r2)
    r1 = step(r1)

    def attend_back(t):
        q4, k4, v4 = [group(qkv, i, t) for i in range(3)]
        do4, o4 = group(mgrad, 0, t), group(mixed, 0, t)
        q4t, do4t = q4.T, do4.T
        kh = [k4 * heads[h] for h in range(4)]
        dk, dv = [], []
        total = [jnp.zeros((128, 128), F32)] * 2
        for h in range(4):
            hrows = slice(32 * h, 32 * h + 32)
            dkh, dvh = [], []
            for rb in range(2):
                rows, nk = slice(128 * rb, 128 * rb + 128), 128 * rb + 128
                dob = do4[rows] * heads[h]
                dot_row = jnp.sum(dob.astype(F32) * o4[rows].astype(F32), axis=1, keepdims=True)
                p = probs[4 * t + h, rows, :nk]
                sg = (p.astype(F32) * (dot_nt(dob, v4[:nk]) - dot_row)).astype(BF)
                total[rb] = total[rb] + dot(sg, kh[h][:nk])
                dkh.append(dot(q4t[hrows, rows], sg))
                dvh.append(dot(do4t[hrows, rows], p))
            for both, parts in ((dk, dkh), (dv, dvh)):
                both.append(jnp.concatenate([parts[1][:, :128] + parts[0], parts[1][:, 128:]], axis=1))
        at = pl.multiple_of(128 * t, 128)
        for rb in range(2):
            dqkv[pl.ds(128 * rb, 128), pl.ds(at, 128)] = (total[rb] * SCALE).astype(BF)
        dqkv[:, pl.ds(at + 768, 128)] = (jnp.concatenate(dk, axis=0).T * SCALE).astype(BF)
        dqkv[:, pl.ds(at + 1536, 128)] = jnp.concatenate(dv, axis=0).T.astype(BF)

    for part in range(3):
        loop(2, lambda i: attend_back(2 * part + i))
        r2 = step(r2)
        r1 = step(r1)

    acc_in[...] = dot_nt(dqkv[:, :768], weight(wide, 0, D))
    acc_in[...] += dot_nt(dqkv[:, 768:1536], weight(wide, 768, D))
    acc_in[...] += dot_nt(dqkv[:, 1536:], weight(wide, 1536, D))

    def norm1_back(i, sums):
        at = ds(i, ROW)
        grad, hat = acc_in[at, :], xhat[at, :]
        extra = norm_back(grad, hat, rstd1[at, :], rows1[0:1, :], at)
        ig_ref[at, :] = hidden[at, :] + extra
        a, b = sums
        return a + jnp.sum(grad * hat, axis=0, keepdims=True), b + jnp.sum(grad, axis=0, keepdims=True)

    as_columns(lax.fori_loop(0, T // ROW, norm1_back, (nothing, nothing)), N1_AT)
    r2 = step(r2)
    r1 = step(r1)

    def qkv_grad(i):
        at = ds(i, 256)
        gwide[:, :, :, at] = dot(n1t[...], dqkv[:, at]).astype(BF).reshape(4, 4, 48, 256)

    loop(9, qkv_grad)
    r0 = step(reduce(0))
    while r0 or r1 or r2:
        r2, r1, r0 = step(r2), step(r1), step(r0)
    wire.drain()

    dd_ref[...] = final_down[...]
    for i, ref in enumerate((dq_ref, dk_ref, dv_ref)):
        ref[...] = final[:12, 768 * i : 768 * i + 768]
    do_ref[...] = final[:12, O_AT:UP_AT]
    du_ref[...] = final[:12, UP_AT:]
    diag = lax.broadcasted_iota(jnp.int32, (16, 128), 0) == lax.broadcasted_iota(jnp.int32, (16, 128), 1)
    for at, refs in ((N1_AT, (dn1g_ref, dn1b_ref)), (N2_AT, (dn2g_ref, dn2b_ref))):
        for k, ref in enumerate(refs):
            col = final[:, at + k : at + k + 1]
            ref[...] = jnp.sum(jnp.where(diag, col, 0.0), axis=0, keepdims=True)[:, :12]


VM = pl.BlockSpec(memory_space=pltpu.VMEM)


def per_device(*args):
    args = [a.reshape(1, 12) if a.ndim == 1 else a for a in args]
    like = jax.ShapeDtypeStruct
    vec, square = like((1, 12), F32), like((12, D), F32)
    scratch = [pltpu.VMEM(s, t) for s, t in reduce_shapes() + tail_shapes()]
    wide, down = pltpu.VMEM((4, 4, 48, WIDE), BF), pltpu.VMEM((4, 4, 2, 2, 48, D), BF)
    scratch += [wide, down, wide, down, pltpu.VMEM((4, 16, WIDE), BF), pltpu.VMEM((16, WIDE), F32), pltpu.VMEM((48, D), F32)]
    f32s, bfs = pltpu.VMEM((T, D), F32), pltpu.VMEM((T, D), BF)
    one, turned = pltpu.VMEM((T, 1), F32), pltpu.VMEM((D, T), BF)
    scratch += [pltpu.VMEM((T, T), F32), f32s, one, f32s, one]
    scratch += [bfs, turned, bfs, pltpu.VMEM((T, 3 * D), BF), bfs]
    scratch += [pltpu.VMEM((HEADS, T, T), BF), f32s]
    scratch += [pltpu.VMEM((T, FF), BF), pltpu.VMEM((T, FF), F32), f32s, f32s]
    scratch += [pltpu.VMEM((T, 3 * D), BF), pltpu.VMEM((8, D), F32), pltpu.VMEM((8, D), F32)]
    scratch += [pltpu.SemaphoreType.DMA((N_SEND,)), pltpu.SemaphoreType.DMA((N_RECV,))]
    outs = pl.pallas_call(
        layer_kernel,
        out_shape=(
            like((T, D), BF), like((T, D), F32), vec, vec, square, square, square, square, vec, vec,
            like((12, FF), F32), like((48, D), F32),
        ),
        in_specs=[VM] * 13,
        out_specs=(VM,) * 12,
        scratch_shapes=scratch,
        compiler_params=pltpu.CompilerParams(
            collective_id=0, has_side_effects=True, vmem_limit_bytes=VMEM_BYTES
        ),
        cost_estimate=pl.CostEstimate(flops=13 * 10**9, bytes_accessed=6 * 10**6, transcendentals=3 * 10**6),
        name="layer",
    )(*args)
    return tuple(o.reshape(12) if o.shape == (1, 12) else o for o in outs)


def solution(mesh):
    placed = (
        P(("fsdp", "rep"), None),
        P(("fsdp", "rep"), None),
        P("fsdp"),
        P("fsdp"),
        P("fsdp", None),
        P("fsdp", None),
        P("fsdp", None),
        P("fsdp", None),
        P("fsdp"),
        P("fsdp"),
        P("fsdp", None),
        P("fsdp", None),
        P(("fsdp", "rep"), None),
    )
    return jax.shard_map(
        per_device,
        mesh=mesh,
        in_specs=placed,
        out_specs=(
            P(("fsdp", "rep"), None),
            P(("fsdp", "rep"), None),
            P("fsdp"),
            P("fsdp"),
            P("fsdp", None),
            P("fsdp", None),
            P("fsdp", None),
            P("fsdp", None),
            P("fsdp"),
            P("fsdp"),
            P("fsdp", None),
            P("fsdp", None),
        ),
        check_vma=False,
    )
```

```python
import functools

import jax
import jax.numpy as jnp
from jax import lax
from jax.experimental import pallas as pl
from jax.experimental.pallas import tpu as pltpu
from jax.sharding import PartitionSpec as P

HEADS = 24
HEAD_DIM = 32
D = 768
FF = 3072
BF = jnp.bfloat16
F32 = jnp.float32
MESH = pl.DeviceIdType.MESH

WIDE = 6400
DOWN = 2
START = (0, 2560, 0, 0, 1536)
HALF = (1280, 1920, 0, 768, 512)
SIZE = ((512, 384), (896, 512), (384, 384), (384, 384), (256, 256))
LOW = ((256, 128), (384, 256), (128, 256), (128, 256), (128, 128))
ZED = (True, True, False, False, False)
P_, QM, QO = 0, 1, 2
N_RECV = 305
N_SEND = 40
VMEM_BYTES = 66700000


class Place:
    def __init__(self):
        f = lax.axis_index("fsdp")
        r = lax.axis_index("rep")
        c = lax.rem(f, 2)
        zl = lax.rem(lax.div(f, 2), 2)
        y = lax.rem(lax.div(f, 4), 4)
        x = lax.div(f, 16)
        self.r, self.c, self.zl, self.y, self.x = r, c, zl, y, x
        self.xs = {d: lax.rem(x + (d + 4), 4) if d else x for d in (-1, 0, 1, 2)}
        self.ys = {d: lax.rem(y + (d + 4), 4) if d else y for d in (-1, 0, 1, 2)}
        low = zl * 2 + c
        self.dx = {d: {"fsdp": self.xs[d] * 16 + y * 4 + low, "rep": r} for d in (-1, 1)}
        self.dy = {d: {"fsdp": x * 16 + self.ys[d] * 4 + low, "rep": r} for d in (-1, 1)}
        turned = f + 2 - 4 * zl
        self.sibling = {"fsdp": f + 1 - 2 * c, "rep": r}
        self.other = {"fsdp": f, "rep": 1 - r}
        self.above = {"fsdp": turned, "rep": lax.rem(r + zl, 2)}
        self.below = {"fsdp": turned, "rep": lax.rem(r + 1 - zl, 2)}
        self.share_to = {"fsdp": turned, "rep": lax.rem(r + zl * (1 - c) + (1 - zl) * c, 2)}
        self.peers = [self.sibling, self.above, self.below, self.other, *self.dx.values(), *self.dy.values()]
        self.starts = {}
        for g in range(len(START)):
            for core, cc in ((0, c), (1, 1 - c)):
                base = START[g] + cc * HALF[g]
                q = base + SIZE[g][0]
                self.starts[g, P_, core] = base
                self.starts[g, QM, core] = q + zl * SIZE[g][1] if ZED[g] else q
                self.starts[g, QO, core] = q + (1 - zl) * SIZE[g][1]


class Wire:
    def __init__(self, place, send, recv):
        self.place, self.send_sem, self.recv_sem = place, send, recv
        self.n = self.m = 0
        self.open = {}

    def slot(self):
        k = self.m % N_SEND
        self.m += 1
        if k in self.open:
            self.open.pop(k).wait_send()
        return k

    def put(self, src, dst, to):
        k = self.slot()
        assert self.n < N_RECV
        copy = pltpu.make_async_remote_copy(
            src_ref=src,
            dst_ref=dst,
            send_sem=self.send_sem.at[k],
            recv_sem=self.recv_sem.at[self.n],
            device_id=to,
            device_id_type=MESH,
        )
        copy.start()
        self.open[k] = copy
        self.n += 1
        return copy

    def drain(self):
        for copy in self.open.values():
            copy.wait_send()
        self.open = {}


def greet(place):
    barrier = pltpu.get_barrier_semaphore()
    for peer in place.peers:
        pl.semaphore_signal(barrier, inc=1, device_id=peer, device_id_type=MESH)
    pl.semaphore_wait(barrier, len(place.peers))


def kind(k):
    return 0 if k == P_ else 1


def halves(g, k):
    n, low = SIZE[g][kind(k)], LOW[g][kind(k)]
    return pl.ds(0, low), pl.ds(low, n - low)


def columns_of(g, k, me, h=None, core=0):
    n, low = SIZE[g][kind(k)], LOW[g][kind(k)]
    off, width = (0, n) if h is None else ((0, low) if h == 0 else (low, n - low))
    base = me.starts[g, k, core]
    return pl.ds(pl.multiple_of(base + off if off else base, 128), width)


class Piece:
    def __init__(self, me, wide, down, g, k):
        self.me, self.wide, self.down, self.g, self.k = me, wide, down, g, k
        self.us, self.ws = (me.xs, me.ys) if k == P_ else (me.ys, me.xs)
        self.first, self.second = (me.dx, me.dy) if k == P_ else (me.dy, me.dx)

    def ref(self, bu, bw, h=None, core=0):
        bx, by = (bu, bw) if self.k == P_ else (bw, bu)
        at = columns_of(self.g, self.k, self.me, h, core)
        if self.g != DOWN:
            return self.wide.at[bx, by, :, at]
        return self.down.at[bx, by, :, 1 - self.me.c if core else self.me.c, :, at]

    def at(self, du, dw, h=None):
        return self.ref(self.us[du], self.ws[dw], h)

    def across(self, dw, h=None):
        return self.ref(slice(None), self.ws[dw], h)

    def along(self, du, h=None):
        return self.ref(self.us[du], slice(None), h)

    def of_sibling(self):
        return self.ref(slice(None), slice(None), core=1)


def wait(*copies):
    yield copies
    for copy in copies:
        copy.wait_recv()


def gather_plane(wire, wide, down, g, k, sib, zs):
    me = wire.place
    s = Piece(me, wide, down, g, k)

    def go(ref, to):
        return wire.put(ref, ref, to)

    def share(name, *where):
        if k == QM and ZED[g]:
            out = [getattr(s, name)(*where, h) for h in range(2)]
            zs.append(((go(out[0], me.above), go(out[1], me.below)), name, where))
        sib.append(go(getattr(s, name)(*where), me.sibling))

    up, dn = {}, {}

    def spread(du):
        up[du] = go(s.at(du, 0), s.second[1])
        dn[du] = go(s.at(du, 0), s.second[-1])

    a, b = go(s.at(0, 0), s.first[1]), go(s.at(0, 0), s.first[-1])
    spread(0)
    yield from wait(a)
    a = go(s.at(-1, 0, 0), s.first[1])
    spread(-1)
    share("at", -1, 0)
    yield from wait(b)
    b = go(s.at(1, 0, 1), s.first[-1])
    spread(1)
    share("at", 1, 0)
    yield from wait(a, b)
    spread(2)
    share("at", 2, 0)
    yield from wait(*[up[du] for du in (0, -1, 1, 2)])
    a = go(s.across(-1, 0), s.second[1])
    share("across", -1)
    yield from wait(*[dn[du] for du in (0, -1, 1, 2)])
    b = go(s.across(1, 1), s.second[-1])
    share("across", 1)
    yield from wait(a, b)
    share("across", 2)


def gather_cross(wire, wide, down, g, sib, zs):
    me = wire.place
    theirs = Piece(me, wide, down, g, QO)
    for n in range(6):
        yield lambda: zs[n][0] if len(zs) > n else None
        copies, name, where = zs[n]
        for copy in copies:
            copy.wait_recv()
        ref = getattr(theirs, name)(*where)
        sib.append(wire.put(ref, ref, me.sibling))


def gather_end(g, sib):
    n = 18 if ZED[g] else 12
    for i in range(n):
        yield lambda: (sib[i],) if len(sib) > i else None
        sib[i].wait_recv()


def gather_streams(wire, wide, down, g):
    sib, zs = [], []
    streams = [gather_plane(wire, wide, down, g, k, sib, zs) for k in (P_, QM)]
    if ZED[g]:
        streams.append(gather_cross(wire, wide, down, g, sib, zs))
    return streams + [gather_end(g, sib)]


def join(stage, wide, me, g):
    step = 640

    def body(i, carry):
        at = pl.ds(pl.multiple_of(START[g] + i * step, 128), step)
        rows = [stage[o, :, at].astype(F32)[:12] for o in range(4)]
        wide[me.x, me.y, :, at] = jnp.concatenate(rows, axis=0).astype(BF)
        return carry

    lax.fori_loop(0, 2 * HALF[g] // step, body, 0)


def gather_front(wire, own_down, stage, wide, down, g):
    me = wire.place
    mine = 2 * me.zl + me.c
    if g != DOWN:
        at = pl.ds(START[g], 2 * HALF[g])
        src = dst = stage.at[mine, :, at]
        hers = stage.at[2 * (1 - me.zl) + me.c, :, at]
    else:
        src, dst = own_down, down.at[me.x, me.y, me.zl, me.c]
        hers = down.at[me.x, me.y, 1 - me.zl, me.c]
        down[me.x, me.y, me.zl, me.c] = own_down[...]
    a = wire.put(src, dst, me.share_to)
    b = wire.put(src, dst, me.sibling)
    yield from wait(a)
    c = wire.put(hers, hers, me.sibling)
    yield from wait(b, c)
    if g != DOWN:
        join(stage, wide, me, g)


def rows_of(g):
    return (2, 48) if g == DOWN else (48,)


REDUCED = (1, 2, 3, 4)


def reduce_shapes(g):
    rows, shapes = rows_of(g), []
    for k in (P_, QM):
        n, low = SIZE[g][kind(k)], LOW[g][kind(k)]
        high = n - low
        own = (48,) if g == DOWN else (2, 16)
        shapes += [(4, 4, *rows, n), (4, *rows, low), (4, *rows, high), (4, *rows, n), (4, *rows, n)]
        shapes += [(*rows, low), (*rows, high), (*rows, n), (*rows, n), (2, *own, n), (*own, n), (*own, n), (*own, n)]
    if ZED[g]:
        shapes += [(4, 4, *rows, SIZE[g][1])] * 2
    shapes = [(s, BF) for s in shapes]
    return shapes if g == DOWN else shapes + [((16, HALF[g]), F32)]


def add_blocks(dst, src):
    def body(i, carry):
        ref = dst(i)
        ref[...] = ref[...] + src(i)[...]
        return carry

    lax.fori_loop(0, 4, body, 0)


def add_one(ref, a):
    ref[...] = ref[...] + a[...]


def add_two(ref, a, b):
    ref[...] = (ref[...].astype(F32) + a[...].astype(F32) + b[...].astype(F32)).astype(BF)


def owners_rows(st, ref, a, b, g):
    total = ref[...].astype(F32) + a[...].astype(F32) + b[...].astype(F32)
    if g != DOWN:
        zero = jnp.zeros((4, total.shape[1]), F32)
        for o in range(4):
            st[o // 2, o % 2] = jnp.concatenate([total[12 * o : 12 * o + 12], zero], axis=0).astype(BF)
    else:
        st[...] = total.astype(BF)


def add_planes(me, g, k, st, rzp, rzm, rr, final, final_down, so):
    def total_of(core):
        def pick(ref):
            return (ref[...] if g == DOWN else ref[core]).astype(F32)

        first = pick(st.at[me.zl]) + pick(rr)
        second = pick(rzp) + pick(rzm)
        if k == QM and ZED[g]:
            return (QM, first), (QO, second)
        return ((k, first + second),)

    out = final_down if g == DOWN else final
    for kk, v in total_of(me.c):
        out[:, columns_of(g, kk, me)] = v
    if g != DOWN:
        for kk, v in total_of(1 - me.c):
            base = me.starts[g, kk, 0] - me.starts[g, P_, 0]
            so[:, pl.ds(pl.multiple_of(base, 128), v.shape[1])] = v


def reduce_plane(wire, wide, down, bufs, got, z_in, done, finals, g, k):
    me = wire.place
    s = Piece(me, wide, down, g, k)
    sb, b1p, b1m, b2p, b2m, c1p, c1m, c2p, c2m, st, rzp, rzm, rr = bufs[13 * k : 13 * k + 13]
    lo, hi = halves(g, k)
    any_lo, any_hi = (..., lo), (..., hi)
    crosses = k == QM and ZED[g]

    def add_along(du, buf):
        bu = s.us[du]
        add_blocks(lambda i: s.ref(bu, i), lambda i: buf.at[bu, i] if k == P_ else buf.at[i, bu])

    def add_half(du, h, buf):
        bu = s.us[du]
        add_blocks(lambda i: s.ref(bu, i, h), lambda i: buf.at[i])

    def ready(du):
        if crosses:
            yield lambda: z_in.get(du)
            for copy in z_in[du]:
                copy.wait_recv()
            add_along(du, bufs[27])
        else:
            add_along(du, sb)

    yield from wait(got)
    if crosses:
        for du in (2, 1, -1, 0):
            add_along(du, sb)
    yield from ready(2)
    r1p = wire.put(s.along(2, 0), b1p, s.first[1])
    r1m = wire.put(s.along(2, 1), b1m, s.first[-1])
    yield from ready(1)
    r2p_hi = wire.put(s.along(1, 1), b2p.at[any_hi], s.first[1])
    yield from ready(-1)
    r2m_lo = wire.put(s.along(-1, 0), b2m.at[any_lo], s.first[-1])
    yield from ready(0)
    yield from wait(r1p)
    add_half(1, 0, b1p)
    r2p_lo = wire.put(s.along(1, 0), b2p.at[any_lo], s.first[1])
    yield from wait(r1m)
    add_half(-1, 1, b1m)
    r2m_hi = wire.put(s.along(-1, 1), b2m.at[any_hi], s.first[-1])
    yield from wait(r2p_hi, r2m_lo, r2p_lo, r2m_hi)

    def close(dw):
        add_two(s.at(0, dw), b2p.at[s.ws[dw]], b2m.at[s.ws[dw]])

    close(2)
    r1p = wire.put(s.at(0, 2, 0), c1p, s.second[1])
    r1m = wire.put(s.at(0, 2, 1), c1m, s.second[-1])
    close(1)
    r2p_hi = wire.put(s.at(0, 1, 1), c2p.at[any_hi], s.second[1])
    close(-1)
    r2m_lo = wire.put(s.at(0, -1, 0), c2m.at[any_lo], s.second[-1])
    close(0)
    yield from wait(r1p)
    add_one(s.at(0, 1, 0), c1p)
    r2p_lo = wire.put(s.at(0, 1, 0), c2p.at[any_lo], s.second[1])
    yield from wait(r1m)
    add_one(s.at(0, -1, 1), c1m)
    r2m_hi = wire.put(s.at(0, -1, 1), c2m.at[any_hi], s.second[-1])
    yield from wait(r2p_hi, r2m_lo, r2p_lo, r2m_hi)
    owners_rows(st, s.at(0, 0), c2p, c2m, g)
    a = wire.put(st.at[1 - me.zl], rzp, me.above)
    b = wire.put(st.at[1 - me.zl], rzm, me.below)
    c = wire.put(st.at[me.zl], rr, me.other)
    yield from wait(a, b, c)
    add_planes(me, g, k, st, rzp, rzm, rr, *finals, None if g == DOWN else bufs[-1])
    done.append(k)
    if g != DOWN and len(done) == 2:
        at = pl.ds(pl.multiple_of(me.starts[g, P_, 0], 128), HALF[g])
        yield from wait(wire.put(bufs[-1], finals[0].at[:, at], me.sibling))


def reduce_cross(wire, wide, down, bufs, got, z_in, g):
    me = wire.place
    theirs = Piece(me, wide, down, g, QO)
    lo, hi = halves(g, QO)
    yield from wait(got)
    for du in (2, 1, -1, 0):
        bu = theirs.us[du]
        add_blocks(lambda i: theirs.ref(bu, i), lambda i: bufs[26].at[i, bu])
        a = wire.put(theirs.along(du, 0), bufs[27].at[:, bu, ..., lo], me.below)
        b = wire.put(theirs.along(du, 1), bufs[27].at[:, bu, ..., hi], me.above)
        z_in[du] = a, b
        if du:
            yield None


def reduce_streams(wire, wide, down, bufs, finals, g):
    me = wire.place
    pieces = {k: Piece(me, wide, down, g, k) for k in (P_, QM, QO)}
    z_in, done, streams = {}, [], []
    if ZED[g]:
        got = wire.put(pieces[QO].of_sibling(), bufs[26], me.sibling)
        streams.append(reduce_cross(wire, wide, down, bufs, got, z_in, g))
    for k in (P_, QM):
        got = wire.put(pieces[k].of_sibling(), bufs[13 * k], me.sibling)
        streams.append(reduce_plane(wire, wide, down, bufs, got, z_in, done, finals, g, k))
    return streams


class Conductor:
    def __init__(self, openers):
        self.openers = openers
        self.streams = {}
        self.place = 0

    def serve(self):
        for key, i in SCHEDULE[self.place]:
            if i < 0:
                self.streams.update({(key, k): s for k, s in enumerate(self.openers[key]())})
                for k in self.streams:
                    if k[0] == key:
                        next(self.streams[k])
            else:
                next(self.streams[key, i], None)
        self.place += 1


SCHEDULE = (
    ((5, -1),),
    (),
    ((6, -1), (7, -1),),
    ((5, 0), (5, 0), (0, -1), (6, 0), (7, 0), (6, 0), (0, 0), (0, 0), (7, 0), (0, 1), (0, 1), (0, 3), (0, 3), (0, 3),
     (0, 0), (0, 3), (0, 2), (0, 2), (0, 3), (0, 3), (0, 3), (0, 1), (1, -1), (0, 0), (0, 0), (0, 3), (0, 2), (0, 1),
     (0, 1), (0, 3), (0, 3), (0, 3), (0, 3), (0, 3), (1, 0), (1, 0), (1, 1), (1, 1), (1, 3), (0, 2), (1, 3), (1, 3),
     (1, 3), (0, 0), (0, 3), (0, 1), (0, 2), (1, 2), (0, 3), (1, 0), (1, 2), (0, 3), (0, 3), (1, 3), (1, 3), (1, 3),
     (0, 2), (1, 1), (0, 3), (2, -1), (1, 3),),
    ((1, 0), (1, 0), (1, 1), (1, 1), (1, 2), (2, 0), (2, 0),),
    ((1, 3), (1, 3), (1, 3), (2, 1), (2, 1), (1, 3), (1, 3),),
    ((1, 1), (1, 0), (1, 2), (1, 2), (2, 0), (2, 2), (2, 2), (2, 2), (2, 2),),
    ((1, 3), (1, 3), (1, 3),),
    ((1, 2), (1, 3), (2, 1), (2, 2), (2, 0), (2, 0), (1, 3),),
    ((2, 1), (2, 1), (2, 2), (2, 2), (2, 2),),
    ((2, 2), (2, 2),),
    ((2, 0),),
    ((2, 1), (2, 2),),
    ((2, 2),),
    ((12, -1),),
    (),
    ((12, 0), (12, 1),),
    ((12, 0),),
    ((12, 0), (12, 1), (12, 1),),
    ((11, -1),),
    (),
    ((11, 0), (11, 0), (11, 0), (11, 0), (12, 0), (11, 1), (12, 0), (12, 1), (11, 2), (11, 2), (12, 0),),
    ((11, 1), (11, 1), (11, 2), (11, 2),),
    ((11, 2), (11, 2), (11, 2), (12, 0), (12, 1), (12, 1),),
    ((13, -1),),
    ((11, 2), (12, 0), (13, 0), (11, 1), (13, 1), (11, 2), (11, 2), (12, 1), (13, 0), (11, 1), (11, 1),),
    ((14, -1), (13, 0), (11, 2), (13, 1), (13, 1), (12, 1), (14, 0), (14, 1), (13, 0), (11, 1), (14, 0), (14, 0),
     (11, 2), (13, 1), (14, 1), (14, 0), (14, 1), (13, 1), (13, 1), (13, 0), (13, 0), (11, 1), (13, 1), (14, 1),
     (14, 0), (14, 0), (11, 1), (13, 0), (14, 1), (14, 1), (14, 0), (13, 1), (14, 1), (13, 0), (14, 0), (13, 0),
     (14, 1), (14, 1),),
)


def dot(a, b):
    return lax.dot_general(a, b, (((1,), (0,)), ((), ())), preferred_element_type=F32)


def dot_nt(a, b):
    return lax.dot_general(a, b, (((1,), (1,)), ((), ())), preferred_element_type=F32)


def loop(n, body):
    def step(i, carry):
        body(i)
        return carry

    lax.fori_loop(0, n, step, 0)


def ds(i, n):
    return pl.ds(pl.multiple_of(i * n, n), n)


T = 256
SCALE = HEAD_DIM ** (-0.5)
O_AT, UP_AT, N1_AT, N2_AT = 2560, 3328, 2304, 2432
ROW = 64


def standardise(v):
    centre = jnp.mean(v, axis=-1, keepdims=True)
    centred = v - centre
    spread = jnp.mean(centred * centred, axis=-1, keepdims=True)
    rstd = lax.rsqrt(spread + 1e-05)
    return centred * rstd, rstd


def weight(wide, at, width):
    return wide[:, :, :, pl.ds(at, width)].reshape(D, width)


def layer_kernel(
    x_ref, seg_ref, n1g_ref, n1b_ref, wq_ref, wk_ref, wv_ref, wo_ref, n2g_ref, n2b_ref, wu_ref, wd_ref, cot_ref,
    out_ref, ig_ref, dn1g_ref, dn1b_ref, dq_ref, dk_ref, dv_ref, do_ref, dn2g_ref, dn2b_ref, du_ref, dd_ref,
    *scratch,
):
    bufs = {}
    for g in REDUCED:
        n = len(reduce_shapes(g))
        bufs[g], scratch = scratch[:n], scratch[n:]
    (
        wide, down, gwide, gdown, stage, final, final_down,
        mask, xhat, rstd1, xhat2, rstd2, n1, n1t, n2, qkv, mixed, probs, hidden,
        act, slope, acc_out, acc_in, dqkv, rows1, rows2, send, recv,
    ) = scratch
    place = me = Place()
    greet(place)
    wire = Wire(place, send, recv)
    openers = {g: lambda g=g: gather_streams(wire, wide, down, g) for g in range(3)}
    openers.update({5 + g: lambda g=g: [gather_front(wire, wd_ref, stage, wide, down, g)] for g in range(3)})
    finals = final, final_down
    openers.update({10 + g: lambda g=g: reduce_streams(wire, gwide, gdown, bufs[g], finals, g) for g in REDUCED})
    conductor = Conductor(openers)
    serve = conductor.serve
    mine = 2 * me.zl + me.c

    zero4 = lambda n: jnp.zeros((4, n), F32)

    def put_own(ref, at):
        n = ref.shape[1]
        rows = jnp.concatenate([ref[...].astype(F32), zero4(n)], axis=0)
        stage[mine, :, pl.ds(at, n)] = rows.astype(BF)

    def put_norm(gain, shift, at):
        eye = lax.broadcasted_iota(jnp.int32, (16, 12), 0) == lax.broadcasted_iota(jnp.int32, (16, 12), 1)
        lane = lax.broadcasted_iota(jnp.int32, (16, 128), 1)
        a = jnp.sum(jnp.where(eye, gain[...].astype(F32), 0.0), axis=1, keepdims=True)
        b = jnp.sum(jnp.where(eye, shift[...].astype(F32), 0.0), axis=1, keepdims=True)
        both = jnp.where(lane == 0, a, jnp.where(lane == 1, b, 0.0))
        stage[mine, :, pl.ds(at, 128)] = both.astype(BF)

    for i, ref in enumerate((wq_ref, wk_ref, wv_ref)):
        put_own(ref, 768 * i)
    put_norm(n1g_ref, n1b_ref, N1_AT)
    put_norm(n2g_ref, n2b_ref, N2_AT)
    serve()
    put_own(wo_ref, O_AT)
    put_own(wu_ref, UP_AT)
    serve()

    segs = jnp.broadcast_to(seg_ref[...], (T, T))
    rows_iota = lax.broadcasted_iota(jnp.int32, (T, T), 0)
    cols_iota = lax.broadcasted_iota(jnp.int32, (T, T), 1)
    allowed = (rows_iota >= cols_iota) & (segs.astype(F32).T == segs.astype(F32))
    mask[...] = jnp.where(allowed, 0.0, -1e30)

    serve()

    def norm1_rows(i):
        at = ds(i, ROW)
        hat, rstd = standardise(x_ref[at, :].astype(F32))
        xhat[at, :] = hat
        rstd1[at, :] = rstd

    loop(T // ROW, norm1_rows)
    serve()

    eye = (
        lax.broadcasted_iota(jnp.int32, (128, 128), 0) == lax.broadcasted_iota(jnp.int32, (128, 128), 1)
    ).astype(BF)
    rows1[...] = dot_nt(eye, weight(wide, N1_AT, 128))[:8]
    rows2[...] = dot_nt(eye, weight(wide, N2_AT, 128))[:8]

    def norm1_apply(i):
        at = ds(i, ROW)
        n1[at, :] = (xhat[at, :] * rows1[0:1, :] + rows1[1:2, :]).astype(BF)

    loop(T // ROW, norm1_apply)

    def project(i):
        at = ds(i, 256)
        w = wide[:, :, :, at].reshape(D, 256)
        qkv[:, at] = dot(n1[...], w).astype(BF)

    loop(9, project)
    serve()
    lane = lax.broadcasted_iota(jnp.int32, (1, 128), 1)
    heads = [((lane >= 32 * h) & (lane < 32 * h + 32)).astype(F32).astype(BF) for h in range(4)]

    def group(ref, which, t):
        return ref[:, pl.ds(pl.multiple_of(768 * which + 128 * t, 128), 128)]

    def attend(t):
        q4, k4, v4 = [group(qkv, i, t) for i in range(3)]
        vh = [v4 * heads[h] for h in range(4)]
        for rb in range(2):
            rows, nk = slice(128 * rb, 128 * rb + 128), 128 * rb + 128
            total = jnp.zeros((128, 128), F32)
            for h in range(4):
                s = dot_nt(q4[rows] * heads[h], k4[:nk]) * SCALE + mask[rows, :nk]
                e = jnp.exp(s - jnp.max(s, axis=1, keepdims=True))
                p = (e * (1.0 / jnp.sum(e, axis=1, keepdims=True))).astype(BF)
                probs[4 * t + h, rows, :nk] = p
                total = total + dot(p, vh[h][:nk])
            mixed[rows, pl.ds(pl.multiple_of(128 * t, 128), 128)] = total.astype(BF)

    for part in range(3):
        loop(2, lambda i: attend(2 * part + i))
        serve()

    n2t, mixt = [gwide.at[:, :, :, pl.ds(256 * k, 256)] for k in range(2)]

    def transpose(src, dst):
        def body(i):
            dst[ds(i, 2)] = src[:, ds(i, 384)].T.reshape(2, 4, 48, T)

        loop(2, body)

    def turn_n1(i):
        n1t[ds(i, 384), :] = n1[:, ds(i, 384)].T

    transpose(mixed, mixt)
    loop(2, turn_n1)
    serve()

    def out_project(i):
        at = ds(i, 256)
        w = wide[:, :, :, pl.ds(pl.multiple_of(O_AT + 256 * i, 128), 256)].reshape(D, 256)
        hidden[:, at] = x_ref[:, at].astype(F32) + dot(mixed[...], w)

    loop(3, out_project)

    def norm2_rows(i):
        at = ds(i, ROW)
        hat, rstd = standardise(hidden[at, :])
        xhat2[at, :] = hat
        rstd2[at, :] = rstd
        n2[at, :] = (hat * rows2[0:1, :] + rows2[1:2, :]).astype(BF)

    loop(T // ROW, norm2_rows)
    transpose(n2, n2t)
    serve()

    c0 = (2.0 / 3.141592653589793) ** 0.5

    def feed(i):
        def part(j):
            at = pl.ds(pl.multiple_of(UP_AT + 768 * i + 256 * j, 128), 256)
            v = dot(n2[...], wide[:, :, :, at].reshape(D, 256))
            sq = v * v
            th = jnp.tanh(c0 * v * (1.0 + 0.044715 * sq))
            half = 0.5 + 0.5 * th
            a = (v * half).astype(BF)
            keep = pl.ds(pl.multiple_of(768 * i + 256 * j, 128), 256)
            act[:, keep] = a
            slope[:, keep] = half + 0.5 * v * (1.0 - th * th) * (c0 * (1.0 + 0.134145 * sq))

        loop(3, part)
        a = act[:, ds(i, 768)].T

        def grad(j):
            at = ds(j, 256)
            gdown[i, :, :, :, :, at] = dot(a, cot_ref[:, at]).astype(BF).reshape(4, 2, 2, 48, 256)

        loop(3, grad)

    for i in range(4):
        feed(i)
        serve()
    serve()

    acc_out[...] = hidden[...]
    acc_in[...] = jnp.zeros((T, D), F32)

    def feed_back(i):
        at = ds(i, 768)
        wd = down[i].reshape(768, 768)
        acc_out[...] += dot(act[:, at], wd)
        pg = (dot_nt(cot_ref[...], wd) * slope[:, at]).astype(BF)
        act[:, at] = pg
        up_at = pl.ds(pl.multiple_of(UP_AT + 768 * i, 128), 768)
        acc_in[...] += dot_nt(pg, wide[:, :, :, up_at].reshape(D, 768))

        def grad(j):
            cols_j = pl.ds(pl.multiple_of(UP_AT + 768 * i + 256 * j, 128), 256)
            pg_j = act[:, pl.ds(pl.multiple_of(768 * i + 256 * j, 128), 256)]
            gwide[:, :, :, cols_j] = dot(n2t[...].reshape(D, T), pg_j).astype(BF).reshape(4, 4, 48, 256)

        loop(3, grad)

    for i in range(4):
        feed_back(i)
        serve()
    out_ref[...] = acc_out[...].astype(BF)

    def norm_back(grad, hat, rstd, gain, at):
        gn = gain * grad
        m1 = jnp.mean(gn, axis=-1, keepdims=True)
        m2 = jnp.mean(gn * hat, axis=-1, keepdims=True)
        return (gn - m1 - hat * m2) * rstd

    def norm2_back(i, sums):
        at = ds(i, ROW)
        grad, hat = acc_in[at, :], xhat2[at, :]
        extra = norm_back(grad, hat, rstd2[at, :], rows2[0:1, :], at)
        hidden[at, :] = cot_ref[at, :].astype(F32) + extra
        a, b = sums
        return a + jnp.sum(grad * hat, axis=0, keepdims=True), b + jnp.sum(grad, axis=0, keepdims=True)

    def as_columns(sums, at):
        rows = jnp.concatenate([*sums, jnp.zeros((126, D), F32)], axis=0)
        gwide[:, :, :, pl.ds(at, 128)] = rows.T.astype(BF).reshape(4, 4, 48, 128)

    nothing = jnp.zeros((1, D), F32)
    as_columns(lax.fori_loop(0, T // ROW, norm2_back, (nothing, nothing)), N2_AT)
    n2[...] = hidden[...].astype(BF)

    def o_back(i):
        at = ds(i, 256)
        b = n2[:, at]
        gwide[:, :, :, pl.ds(pl.multiple_of(O_AT + 256 * i, 128), 256)] = (
            dot(mixt[...].reshape(D, T), b).astype(BF).reshape(4, 4, 48, 256)
        )

    loop(3, o_back)
    serve()
    mgrad = n1
    mgrad[...] = dot_nt(n2[...], weight(wide, O_AT, D)).astype(BF)
    serve()

    def attend_back(t):
        q4, k4, v4 = [group(qkv, i, t) for i in range(3)]
        do4, o4 = group(mgrad, 0, t), group(mixed, 0, t)
        q4t, do4t = q4.T, do4.T
        kh = [k4 * heads[h] for h in range(4)]
        dk, dv = [], []
        total = [jnp.zeros((128, 128), F32)] * 2
        for h in range(4):
            hrows = slice(32 * h, 32 * h + 32)
            dkh, dvh = [], []
            for rb in range(2):
                rows, nk = slice(128 * rb, 128 * rb + 128), 128 * rb + 128
                dob = do4[rows] * heads[h]
                dot_row = jnp.sum(dob.astype(F32) * o4[rows].astype(F32), axis=1, keepdims=True)
                p = probs[4 * t + h, rows, :nk]
                sg = (p.astype(F32) * (dot_nt(dob, v4[:nk]) - dot_row)).astype(BF)
                total[rb] = total[rb] + dot(sg, kh[h][:nk])
                dkh.append(dot(q4t[hrows, rows], sg))
                dvh.append(dot(do4t[hrows, rows], p))
            for both, parts in ((dk, dkh), (dv, dvh)):
                both.append(jnp.concatenate([parts[1][:, :128] + parts[0], parts[1][:, 128:]], axis=1))
        at = pl.multiple_of(128 * t, 128)
        for rb in range(2):
            dqkv[pl.ds(128 * rb, 128), pl.ds(at, 128)] = (total[rb] * SCALE).astype(BF)
        dqkv[:, pl.ds(at + 768, 128)] = (jnp.concatenate(dk, axis=0).T * SCALE).astype(BF)
        dqkv[:, pl.ds(at + 1536, 128)] = jnp.concatenate(dv, axis=0).T.astype(BF)

    for part in range(3):
        loop(2, lambda i: attend_back(2 * part + i))
        serve()

    def qkv_grad(i):
        at = ds(i, 256)
        gwide[:, :, :, at] = dot(n1t[...], dqkv[:, at]).astype(BF).reshape(4, 4, 48, 256)

    loop(6, qkv_grad)
    serve()
    acc_in[...] = dot_nt(dqkv[:, :768], weight(wide, 0, D))
    acc_in[...] += dot_nt(dqkv[:, 768:1536], weight(wide, 768, D))
    acc_in[...] += dot_nt(dqkv[:, 1536:], weight(wide, 1536, D))
    serve()

    def norm1_back(i, sums):
        at = ds(i, ROW)
        grad, hat = acc_in[at, :], xhat[at, :]
        extra = norm_back(grad, hat, rstd1[at, :], rows1[0:1, :], at)
        ig_ref[at, :] = hidden[at, :] + extra
        a, b = sums
        return a + jnp.sum(grad * hat, axis=0, keepdims=True), b + jnp.sum(grad, axis=0, keepdims=True)

    as_columns(lax.fori_loop(0, T // ROW, norm1_back, (nothing, nothing)), N1_AT)
    loop(3, lambda i: qkv_grad(6 + i))
    serve()

    wire.drain()

    dd_ref[...] = final_down[...]
    for i, ref in enumerate((dq_ref, dk_ref, dv_ref)):
        ref[...] = final[:12, 768 * i : 768 * i + 768]
    do_ref[...] = final[:12, O_AT:UP_AT]
    du_ref[...] = final[:12, UP_AT:]
    diag = lax.broadcasted_iota(jnp.int32, (16, 128), 0) == lax.broadcasted_iota(jnp.int32, (16, 128), 1)
    for at, refs in ((N1_AT, (dn1g_ref, dn1b_ref)), (N2_AT, (dn2g_ref, dn2b_ref))):
        for k, ref in enumerate(refs):
            col = final[:, at + k : at + k + 1]
            ref[...] = jnp.sum(jnp.where(diag, col, 0.0), axis=0, keepdims=True)[:, :12]


def publish_kernel(*refs):
    n = len(refs) // 2
    for i in range(n):
        refs[n + i][...] = refs[i][...]


VM = pl.BlockSpec(memory_space=pltpu.VMEM)


def per_device(*args):
    args = [a.reshape(1, 12) if a.ndim == 1 else a for a in args]
    like = jax.ShapeDtypeStruct
    vec, square = like((1, 12), F32), like((12, D), F32)
    scratch = [pltpu.VMEM(s, t) for g in REDUCED for s, t in reduce_shapes(g)]
    wide, down = pltpu.VMEM((4, 4, 48, WIDE), BF), pltpu.VMEM((4, 4, 2, 2, 48, D), BF)
    scratch += [wide, down, wide, down, pltpu.VMEM((4, 16, WIDE), BF), pltpu.VMEM((16, WIDE), F32), pltpu.VMEM((48, D), F32)]
    f32s, bfs = pltpu.VMEM((T, D), F32), pltpu.VMEM((T, D), BF)
    one, turned = pltpu.VMEM((T, 1), F32), pltpu.VMEM((D, T), BF)
    scratch += [pltpu.VMEM((T, T), F32), f32s, one, f32s, one]
    scratch += [bfs, turned, bfs, pltpu.VMEM((T, 3 * D), BF), bfs]
    scratch += [pltpu.VMEM((HEADS, T, T), BF), f32s]
    scratch += [pltpu.VMEM((T, FF), BF), pltpu.VMEM((T, FF), F32), f32s, f32s]
    scratch += [pltpu.VMEM((T, 3 * D), BF), pltpu.VMEM((8, D), F32), pltpu.VMEM((8, D), F32)]
    scratch += [pltpu.SemaphoreType.DMA((N_SEND,)), pltpu.SemaphoreType.DMA((N_RECV,))]
    outs = pl.pallas_call(
        layer_kernel,
        out_shape=(
            like((T, D), BF), like((T, D), F32), vec, vec, square, square, square, square, vec, vec,
            like((12, FF), F32), like((48, D), F32),
        ),
        in_specs=[VM] * 13,
        out_specs=(VM,) * 12,
        scratch_shapes=scratch,
        compiler_params=pltpu.CompilerParams(
            collective_id=0, has_side_effects=True, vmem_limit_bytes=VMEM_BYTES
        ),
        cost_estimate=pl.CostEstimate(flops=13 * 10**9, bytes_accessed=6 * 10**6, transcendentals=3 * 10**6),
        name="layer",
    )(*args)
    outs = pl.pallas_call(
        publish_kernel,
        out_shape=tuple(like(o.shape, o.dtype) for o in outs),
        in_specs=[VM] * 12,
        out_specs=(VM,) * 12,
        name="publish",
    )(*outs)
    return tuple(o.reshape(12) if o.shape == (1, 12) else o for o in outs)


def solution(mesh):
    placed = (
        P(("fsdp", "rep"), None),
        P(("fsdp", "rep"), None),
        P("fsdp"),
        P("fsdp"),
        P("fsdp", None),
        P("fsdp", None),
        P("fsdp", None),
        P("fsdp", None),
        P("fsdp"),
        P("fsdp"),
        P("fsdp", None),
        P("fsdp", None),
        P(("fsdp", "rep"), None),
    )
    return jax.shard_map(
        per_device,
        mesh=mesh,
        in_specs=placed,
        out_specs=(
            P(("fsdp", "rep"), None),
            P(("fsdp", "rep"), None),
            P("fsdp"),
            P("fsdp"),
            P("fsdp", None),
            P("fsdp", None),
            P("fsdp", None),
            P("fsdp", None),
            P("fsdp"),
            P("fsdp"),
            P("fsdp", None),
            P("fsdp", None),
        ),
        check_vma=False,
    )
```

```python
import functools

import jax
import jax.numpy as jnp
from jax import lax
from jax.experimental import pallas as pl
from jax.experimental.pallas import tpu as pltpu
from jax.sharding import PartitionSpec as P

HEADS = 24
HEAD_DIM = 32
D = 768
FF = 3072
BF = jnp.bfloat16
F32 = jnp.float32
MESH = pl.DeviceIdType.MESH

WIDE = 6400
DOWN = 2
START = (0, 2560, 0, 0, 384, 768, 2560, 4096)
HALF = (1280, 1920, 0, 1280, 1280, 1280, 768, 1152)
WIDTH = (1280, 1920, 768, 384, 384, 512, 768, 1152)
P_AT = (768, 0, 0, 0, 0, 0, 0, 0)
Q_AT = (0, 384, 384, 256, 128, 256, 256, 384)
SIZE = ((512, 384), (384, 768), (384, 384), (256, 128), (128, 256), (256, 256), (256, 256), (384, 384))
LOW = ((256, 256), (128, 384), (128, 256), (128, 128), (128, 128), (128, 128), (128, 128), (128, 256))
ZED = (True, True, False, False, False, False, True, True)
STRAIGHT = (False, False, False)
DIRECT = (False, False, False, True, True, True, False, True)
P_, QM, QO = 0, 1, 2
N_RECV = 332
N_SEND = 40
VMEM_BYTES = 66700000


class Place:
    def __init__(self):
        f = lax.axis_index("fsdp")
        r = lax.axis_index("rep")
        c = lax.rem(f, 2)
        zl = lax.rem(lax.div(f, 2), 2)
        y = lax.rem(lax.div(f, 4), 4)
        x = lax.div(f, 16)
        self.r, self.c, self.zl, self.y, self.x = r, c, zl, y, x
        self.xs = {d: lax.rem(x + (d + 4), 4) if d else x for d in (-1, 0, 1, 2)}
        self.ys = {d: lax.rem(y + (d + 4), 4) if d else y for d in (-1, 0, 1, 2)}
        low = zl * 2 + c
        self.dx = {d: {"fsdp": self.xs[d] * 16 + y * 4 + low, "rep": r} for d in (-1, 1, 2)}
        self.dy = {d: {"fsdp": x * 16 + self.ys[d] * 4 + low, "rep": r} for d in (-1, 1, 2)}
        turned = f + 2 - 4 * zl
        self.sibling = {"fsdp": f + 1 - 2 * c, "rep": r}
        self.other = {"fsdp": f, "rep": 1 - r}
        self.above = {"fsdp": turned, "rep": lax.rem(r + zl, 2)}
        self.below = {"fsdp": turned, "rep": lax.rem(r + 1 - zl, 2)}
        self.share_to = {"fsdp": turned, "rep": lax.rem(r + zl * (1 - c) + (1 - zl) * c, 2)}
        self.peers = [self.sibling, self.above, self.below, self.other, *self.dx.values(), *self.dy.values()]
        self.starts = {}
        for g in range(len(START)):
            for core, cc in ((0, c), (1, 1 - c)):
                base = START[g] + cc * HALF[g]
                self.starts[g, None, core] = base
                q = base + Q_AT[g]
                self.starts[g, P_, core] = base + P_AT[g]
                self.starts[g, QM, core] = q + zl * SIZE[g][1] if ZED[g] else q
                self.starts[g, QO, core] = q + (1 - zl) * SIZE[g][1]


class Wire:
    def __init__(self, place, send, recv):
        self.place, self.send_sem, self.recv_sem = place, send, recv
        self.n = self.m = 0
        self.open = {}

    def slot(self):
        k = self.m % N_SEND
        self.m += 1
        if k in self.open:
            self.open.pop(k).wait_send()
        return k

    def put(self, src, dst, to):
        k = self.slot()
        assert self.n < N_RECV
        copy = pltpu.make_async_remote_copy(
            src_ref=src,
            dst_ref=dst,
            send_sem=self.send_sem.at[k],
            recv_sem=self.recv_sem.at[self.n],
            device_id=to,
            device_id_type=MESH,
        )
        copy.start()
        self.open[k] = copy
        self.n += 1
        return copy

    def drain(self):
        for copy in self.open.values():
            copy.wait_send()
        self.open = {}


def greet(place):
    barrier = pltpu.get_barrier_semaphore()
    for peer in place.peers:
        pl.semaphore_signal(barrier, inc=1, device_id=peer, device_id_type=MESH)
    pl.semaphore_wait(barrier, len(place.peers))


def kind(k):
    return 0 if k == P_ else 1


def halves(g, k):
    n, low = SIZE[g][kind(k)], LOW[g][kind(k)]
    return pl.ds(0, low), pl.ds(low, n - low)


def columns_of(g, k, me, h=None, core=0):
    n, low = SIZE[g][kind(k)], LOW[g][kind(k)]
    off, width = (0, n) if h is None else ((0, low) if h == 0 else (low, n - low))
    base = me.starts[g, k, core]
    return pl.ds(pl.multiple_of(base + off if off else base, 128), width)


class Piece:
    def __init__(self, me, wide, down, g, k):
        self.me, self.wide, self.down, self.g, self.k = me, wide, down, g, k
        self.us, self.ws = (me.xs, me.ys) if k == P_ else (me.ys, me.xs)
        self.first, self.second = (me.dx, me.dy) if k == P_ else (me.dy, me.dx)

    def ref(self, bu, bw, h=None, core=0):
        bx, by = (bu, bw) if self.k == P_ else (bw, bu)
        at = columns_of(self.g, self.k, self.me, h, core)
        if self.g != DOWN:
            return self.wide.at[bx, by, :, at]
        return self.down.at[bx, by, :, 1 - self.me.c if core else self.me.c, :, at]

    def at(self, du, dw, h=None):
        return self.ref(self.us[du], self.ws[dw], h)

    def across(self, dw, h=None):
        return self.ref(slice(None), self.ws[dw], h)

    def along(self, du, h=None):
        return self.ref(self.us[du], slice(None), h)

    def of_sibling(self):
        return self.ref(slice(None), slice(None), core=1)


def wait(*copies):
    yield copies
    for copy in copies:
        copy.wait_recv()


def gather_plane(wire, wide, down, g, k, sib, zs):
    me = wire.place
    s = Piece(me, wide, down, g, k)

    def go(ref, to):
        return wire.put(ref, ref, to)

    def share(name, *where):
        if k == QM and ZED[g]:
            lo, hi = [getattr(s, name)(*where, h) for h in range(2)]
            zs.append(((go(lo, me.above), go(hi, me.below)), name, where))
        sib.append(go(getattr(s, name)(*where), me.sibling))

    out = {}

    def spread(du):
        for d in reach:
            out[d, du] = go(s.at(du, 0), s.second[d])

    if not STRAIGHT[g]:
        reach = (1, -1)
        a, b = go(s.at(0, 0), s.first[1]), go(s.at(0, 0), s.first[-1])
        spread(0)
        yield from wait(a)
        a = go(s.at(-1, 0, 0), s.first[1])
        spread(-1)
        share("at", -1, 0)
        yield from wait(b)
        b = go(s.at(1, 0, 1), s.first[-1])
        spread(1)
        share("at", 1, 0)
        yield from wait(a, b)
        spread(2)
        share("at", 2, 0)
        yield from wait(*[out[1, du] for du in (0, -1, 1, 2)])
        a = go(s.across(-1, 0), s.second[1])
        share("across", -1)
        yield from wait(*[out[-1, du] for du in (0, -1, 1, 2)])
        b = go(s.across(1, 1), s.second[-1])
        share("across", 1)
        yield from wait(a, b)
        share("across", 2)
        return
    reach = (1, -1, 2)
    near = {d: go(s.at(0, 0), s.first[d]) for d in reach}
    spread(0)
    for d in (1, -1, 2):
        du = -d if d < 2 else 2
        yield from wait(near[d])
        spread(du)
        share("at", du, 0)
    for d in (1, -1, 2):
        dw = -d if d < 2 else 2
        yield from wait(*[out[d, du] for du in (0, -1, 1, 2)])
        share("across", dw)


def gather_cross(wire, wide, down, g, sib, zs):
    me = wire.place
    theirs = Piece(me, wide, down, g, QO)
    for n in range(6):
        yield lambda: zs[n][0] if len(zs) > n else None
        copies, name, where = zs[n]
        for copy in copies:
            copy.wait_recv()
        ref = getattr(theirs, name)(*where)
        sib.append(wire.put(ref, ref, me.sibling))


def gather_end(n, sib):
    for i in range(n):
        yield lambda: (sib[i],) if len(sib) > i else None
        sib[i].wait_recv()


def gather_streams(wire, wide, down, g):
    sib, zs = {P_: [], QM: [], QO: []}, []
    streams = [gather_plane(wire, wide, down, g, k, sib[k], zs) for k in (P_, QM)]
    streams += [gather_end(6, sib[k]) for k in (P_, QM)]
    if ZED[g]:
        streams += [gather_cross(wire, wide, down, g, sib[QO], zs), gather_end(6, sib[QO])]
    return streams


def join(stage, wide, me, g):
    step = 640

    def body(i, carry):
        at = pl.ds(pl.multiple_of(START[g] + i * step, 128), step)
        rows = [stage[o, :, at].astype(F32)[:12] for o in range(4)]
        wide[me.x, me.y, :, at] = jnp.concatenate(rows, axis=0).astype(BF)
        return carry

    lax.fori_loop(0, 2 * HALF[g] // step, body, 0)


def gather_front(wire, own_down, stage, wide, down, g):
    me = wire.place
    mine = 2 * me.zl + me.c
    if g != DOWN:
        at = pl.ds(START[g], 2 * HALF[g])
        src = dst = stage.at[mine, :, at]
        hers = stage.at[2 * (1 - me.zl) + me.c, :, at]
    else:
        src, dst = own_down, down.at[me.x, me.y, me.zl, me.c]
        hers = down.at[me.x, me.y, 1 - me.zl, me.c]
        down[me.x, me.y, me.zl, me.c] = own_down[...]
    a = wire.put(src, dst, me.share_to)
    b = wire.put(src, dst, me.sibling)
    yield from wait(a)
    c = wire.put(hers, hers, me.sibling)
    yield from wait(b, c)
    if g != DOWN:
        join(stage, wide, me, g)


def rows_of(g):
    return (2, 48) if g == DOWN else (48,)


REDUCED = (2, 3, 4, 5, 6, 7)


def reduce_shapes(g):
    rows, shapes = rows_of(g), []
    for k in (P_, QM):
        n, low = SIZE[g][kind(k)], LOW[g][kind(k)]
        high = n - low
        if DIRECT[g]:
            low, high = n, 128
        own = (48,) if g == DOWN else (2, 16)
        shapes += [(4, 4, *rows, n), (4, *rows, low), (4, *rows, high), (4, *rows, n), (4, *rows, n)]
        shapes += [(*rows, low), (*rows, high), (*rows, n), (*rows, n), (2, *own, n), (*own, n), (*own, n), (*own, n)]
    if ZED[g]:
        shapes += [(4, 4, *rows, SIZE[g][1])] * 2
    shapes = [(s, BF) for s in shapes]
    return shapes if g == DOWN else shapes + [((16, WIDTH[g]), F32)]


def add_blocks(dst, src):
    def body(i, carry):
        ref = dst(i)
        ref[...] = ref[...] + src(i)[...]
        return carry

    lax.fori_loop(0, 4, body, 0)


def add_one(ref, a):
    ref[...] = ref[...] + a[...]


def add_two(ref, a, b):
    ref[...] = (ref[...].astype(F32) + a[...].astype(F32) + b[...].astype(F32)).astype(BF)


def add_three(ref, a, b, c):
    total = ref[...].astype(F32) + a[...].astype(F32) + (b[...].astype(F32) + c[...].astype(F32))
    ref[...] = total.astype(BF)


def owners_rows(st, ref, others, g):
    total = ref[...].astype(F32)
    for other in others:
        total = total + other[...].astype(F32)
    if g != DOWN:
        zero = jnp.zeros((4, total.shape[1]), F32)
        for o in range(4):
            st[o // 2, o % 2] = jnp.concatenate([total[12 * o : 12 * o + 12], zero], axis=0).astype(BF)
    else:
        st[...] = total.astype(BF)


def add_planes(me, g, k, st, rzp, rzm, rr, final, final_down, so):
    def total_of(core):
        def pick(ref):
            return (ref[...] if g == DOWN else ref[core]).astype(F32)

        first = pick(st.at[me.zl]) + pick(rr)
        second = pick(rzp) + pick(rzm)
        if k == QM and ZED[g]:
            return (QM, first), (QO, second)
        return ((k, first + second),)

    out = final_down if g == DOWN else final
    for kk, v in total_of(me.c):
        out[:, columns_of(g, kk, me)] = v
    if g != DOWN:
        for kk, v in total_of(1 - me.c):
            base = me.starts[g, kk, 0] - me.starts[g, None, 0]
            so[:, pl.ds(pl.multiple_of(base, 128), v.shape[1])] = v


def reduce_plane(wire, wide, down, bufs, got, z_in, done, finals, g, k):
    me = wire.place
    s = Piece(me, wide, down, g, k)
    sb, b1p, b1m, b2p, b2m, c1p, c1m, c2p, c2m, st, rzp, rzm, rr = bufs[13 * k : 13 * k + 13]
    lo, hi = halves(g, k)
    any_lo, any_hi = (..., lo), (..., hi)
    crosses = k == QM and ZED[g]

    def add_along(du, buf):
        bu = s.us[du]
        add_blocks(lambda i: s.ref(bu, i), lambda i: buf.at[bu, i] if k == P_ else buf.at[i, bu])

    def add_half(du, h, buf):
        bu = s.us[du]
        add_blocks(lambda i: s.ref(bu, i, h), lambda i: buf.at[i])

    def ready(du):
        if crosses:
            yield lambda: z_in.get(du)
            for copy in z_in[du]:
                copy.wait_recv()
            add_along(du, bufs[27])
        else:
            add_along(du, sb)

    yield from wait(got)
    if crosses:
        for du in (2, 1, -1, 0):
            add_along(du, sb)
    if DIRECT[g]:
        got = []
        for du, buf in ((2, b1p), (1, b2p), (-1, b2m)):
            yield from ready(du)
            got.append(wire.put(s.along(du), buf, s.first[du]))
        yield from ready(0)
        yield from wait(*got)
        got = []
        for dw, buf in ((2, c1p), (1, c2p), (-1, c2m), (0, None)):
            bw = s.ws[dw]
            add_three(s.at(0, dw), b1p.at[bw], b2p.at[bw], b2m.at[bw])
            if dw:
                got.append(wire.put(s.at(0, dw), buf, s.second[dw]))
        yield from wait(*got)
        owners_rows(st, s.at(0, 0), (c1p, c2p, c2m), g)
        yield from over_planes(wire, me, g, k, bufs, st, rzp, rzm, rr, finals, done)
        return
    yield from ready(2)
    r1p = wire.put(s.along(2, 0), b1p, s.first[1])
    r1m = wire.put(s.along(2, 1), b1m, s.first[-1])
    yield from ready(1)
    r2p_hi = wire.put(s.along(1, 1), b2p.at[any_hi], s.first[1])
    yield from ready(-1)
    r2m_lo = wire.put(s.along(-1, 0), b2m.at[any_lo], s.first[-1])
    yield from ready(0)
    yield from wait(r1p)
    add_half(1, 0, b1p)
    r2p_lo = wire.put(s.along(1, 0), b2p.at[any_lo], s.first[1])
    yield from wait(r1m)
    add_half(-1, 1, b1m)
    r2m_hi = wire.put(s.along(-1, 1), b2m.at[any_hi], s.first[-1])
    yield from wait(r2p_hi, r2m_lo, r2p_lo, r2m_hi)

    def close(dw):
        add_two(s.at(0, dw), b2p.at[s.ws[dw]], b2m.at[s.ws[dw]])

    close(2)
    r1p = wire.put(s.at(0, 2, 0), c1p, s.second[1])
    r1m = wire.put(s.at(0, 2, 1), c1m, s.second[-1])
    close(1)
    r2p_hi = wire.put(s.at(0, 1, 1), c2p.at[any_hi], s.second[1])
    close(-1)
    r2m_lo = wire.put(s.at(0, -1, 0), c2m.at[any_lo], s.second[-1])
    close(0)
    yield from wait(r1p)
    add_one(s.at(0, 1, 0), c1p)
    r2p_lo = wire.put(s.at(0, 1, 0), c2p.at[any_lo], s.second[1])
    yield from wait(r1m)
    add_one(s.at(0, -1, 1), c1m)
    r2m_hi = wire.put(s.at(0, -1, 1), c2m.at[any_hi], s.second[-1])
    yield from wait(r2p_hi, r2m_lo, r2p_lo, r2m_hi)
    owners_rows(st, s.at(0, 0), (c2p, c2m), g)
    yield from over_planes(wire, me, g, k, bufs, st, rzp, rzm, rr, finals, done)


def over_planes(wire, me, g, k, bufs, st, rzp, rzm, rr, finals, done):
    a = wire.put(st.at[1 - me.zl], rzp, me.above)
    b = wire.put(st.at[1 - me.zl], rzm, me.below)
    c = wire.put(st.at[me.zl], rr, me.other)
    yield from wait(a, b, c)
    add_planes(me, g, k, st, rzp, rzm, rr, *finals, None if g == DOWN else bufs[-1])
    done.append(k)
    if g != DOWN and len(done) == 2:
        at = pl.ds(pl.multiple_of(me.starts[g, None, 0], 128), WIDTH[g])
        yield from wait(wire.put(bufs[-1], finals[0].at[:, at], me.sibling))


def reduce_cross(wire, wide, down, bufs, got, z_in, g):
    me = wire.place
    theirs = Piece(me, wide, down, g, QO)
    lo, hi = halves(g, QO)
    yield from wait(got)
    for du in (2, 1, -1, 0):
        bu = theirs.us[du]
        add_blocks(lambda i: theirs.ref(bu, i), lambda i: bufs[26].at[i, bu])
        a = wire.put(theirs.along(du, 0), bufs[27].at[:, bu, ..., lo], me.below)
        b = wire.put(theirs.along(du, 1), bufs[27].at[:, bu, ..., hi], me.above)
        z_in[du] = a, b
        if du:
            yield None


def reduce_streams(wire, wide, down, bufs, finals, g):
    me = wire.place
    pieces = {k: Piece(me, wide, down, g, k) for k in (P_, QM, QO)}
    z_in, done, streams = {}, [], []
    if ZED[g]:
        got = wire.put(pieces[QO].of_sibling(), bufs[26], me.sibling)
        streams.append(reduce_cross(wire, wide, down, bufs, got, z_in, g))
    for k in (P_, QM):
        got = wire.put(pieces[k].of_sibling(), bufs[13 * k], me.sibling)
        streams.append(reduce_plane(wire, wide, down, bufs, got, z_in, done, finals, g, k))
    return streams


class Conductor:
    def __init__(self, openers):
        self.openers = openers
        self.streams = {}
        self.place = 0

    def serve(self):
        for key, i in SCHEDULE[self.place]:
            if i < 0:
                self.streams.update({(key, k): s for k, s in enumerate(self.openers[key]())})
                for k in self.streams:
                    if k[0] == key:
                        next(self.streams[k])
            else:
                next(self.streams[key, i], None)
        self.place += 1


SCHEDULE = (
    ((5, -1),),
    (),
    ((6, -1), (7, -1),),
    ((5, 0), (6, 0), (5, 0), (0, -1), (7, 0), (6, 0), (7, 0), (0, 0), (0, 0), (0, 1), (0, 1), (0, 2), (0, 2), (0, 0),
     (1, -1), (0, 3), (0, 3), (0, 4), (0, 4), (0, 2), (0, 1), (1, 0), (0, 5), (1, 0), (0, 0), (0, 0), (0, 5), (0, 3),
     (0, 4), (1, 2), (1, 2), (0, 1), (0, 1), (0, 2), (1, 1), (1, 1), (1, 0), (0, 2), (0, 5), (0, 3), (0, 3), (1, 3),
     (1, 3), (1, 2), (0, 1), (0, 4), (0, 0), (1, 1), (1, 0), (1, 0), (0, 4), (0, 3), (0, 5), (0, 2), (2, -1), (1, 4),),
    ((1, 2), (1, 2), (1, 3), (1, 4),),
    ((0, 5), (1, 1), (1, 1), (1, 5),),
    ((0, 4), (1, 0),),
    (),
    ((1, 4), (1, 5), (2, 0), (2, 0),),
    ((1, 3),),
    ((1, 3), (2, 1), (0, 5),),
    (),
    ((1, 2), (1, 5), (2, 1), (2, 2), (2, 2),),
    ((1, 4),),
    ((2, 3),),
    ((1, 1), (2, 0), (2, 3), (1, 5), (2, 1), (1, 4), (1, 3), (2, 2), (2, 3), (2, 0), (2, 0), (1, 5), (2, 1), (2, 1),
     (1, 4), (2, 2), (2, 2), (2, 3), (2, 3), (1, 5),),
    ((2, 0), (2, 1),),
    (),
    (),
    (),
    (),
    (),
    (),
    (),
    ((2, 2),),
    ((12, -1), (2, 3),),
    (),
    (),
    (),
    (),
    (),
    ((16, -1), (12, 0),),
    (),
    ((12, 1), (16, 0), (16, 0), (16, 0), (16, 0),),
    ((16, 1), (12, 0), (16, 2),),
    ((16, 2),),
    ((12, 0),),
    ((16, 2),),
    ((16, 2),),
    ((17, -1), (12, 1), (12, 1),),
    ((16, 2), (16, 1), (16, 1),),
    (),
    ((17, 0), (17, 0), (17, 0), (17, 0), (17, 1), (16, 2), (16, 2),),
    ((13, -1), (17, 2),),
    ((12, 0),),
    ((13, 0), (13, 1), (17, 2), (12, 1), (16, 1), (17, 2), (12, 0), (12, 0), (16, 2),),
    ((17, 2),),
    ((14, -1),),
    ((13, 1), (17, 1),),
    ((14, 0), (17, 2), (14, 1),),
    ((13, 0), (12, 1), (12, 1), (16, 1), (16, 1),),
    (),
    ((15, -1), (16, 2), (16, 2), (12, 0), (13, 1), (17, 2), (17, 1), (15, 0), (14, 0), (15, 1), (12, 1), (16, 2),
     (12, 0), (17, 2), (13, 1), (17, 1), (14, 1), (13, 0), (16, 1), (12, 1), (14, 0), (16, 2), (15, 0), (17, 2),
     (14, 1), (13, 0), (16, 1), (17, 2), (14, 0), (15, 1), (13, 0), (14, 1), (15, 0), (16, 1), (15, 1), (14, 1),
     (15, 0), (15, 1), (15, 1),),
)


def dot(a, b):
    return lax.dot_general(a, b, (((1,), (0,)), ((), ())), preferred_element_type=F32)


def dot_nt(a, b):
    return lax.dot_general(a, b, (((1,), (1,)), ((), ())), preferred_element_type=F32)


def loop(n, body):
    if n <= UNROLLED:
        for i in range(n):
            body(i)
        return

    def step(i, carry):
        body(i)
        return carry

    lax.fori_loop(0, n, step, 0)


def mult(v, n):
    return v if isinstance(v, int) else pl.multiple_of(v, n)


def ds(i, n):
    return pl.ds(mult(i * n, n), n)


UNROLLED = 3
T = 256
SCALE = HEAD_DIM ** (-0.5)
O_AT, N1_AT, N2_AT = 4096, 1152, 2432


def set_at(half, s):
    return 1280 * half + 384 * s


def up_at(i):
    return 2560 + 768 * i + (768 if i > 1 else 0)


ROW = 64


def standardise(v):
    centre = jnp.mean(v, axis=-1, keepdims=True)
    centred = v - centre
    spread = jnp.mean(centred * centred, axis=-1, keepdims=True)
    rstd = lax.rsqrt(spread + 1e-05)
    return centred * rstd, rstd


def weight(wide, at, width):
    return wide[:, :, :, pl.ds(at, width)].reshape(D, width)


def layer_kernel(
    x_ref, seg_ref, n1g_ref, n1b_ref, wq_ref, wk_ref, wv_ref, wo_ref, n2g_ref, n2b_ref, wu_ref, wd_ref, cot_ref,
    out_ref, ig_ref, dn1g_ref, dn1b_ref, dq_ref, dk_ref, dv_ref, do_ref, dn2g_ref, dn2b_ref, du_ref, dd_ref,
    *scratch,
):
    bufs = {}
    for g in REDUCED:
        n = len(reduce_shapes(g))
        bufs[g], scratch = scratch[:n], scratch[n:]
    (
        wide, down, gwide, gdown, final,
        mask, xhat, rstd1, xhat2, rstd2, n1, n1t, n2, qkv, mixed, probs, hidden,
        act, slope, acc_in, dqkv, rows1, rows2, send, recv,
    ) = scratch
    stage = gwide.at[0, :, pl.ds(0, 16)]
    acc_out = ig_ref
    place = me = Place()
    greet(place)
    wire = Wire(place, send, recv)
    openers = {g: lambda g=g: gather_streams(wire, wide, down, g) for g in range(3)}
    openers.update({5 + g: lambda g=g: [gather_front(wire, wd_ref, stage, wide, down, g)] for g in range(3)})
    finals = final, dd_ref
    openers.update({10 + g: lambda g=g: reduce_streams(wire, gwide, gdown, bufs[g], finals, g) for g in REDUCED})
    conductor = Conductor(openers)
    serve = conductor.serve
    mine = 2 * me.zl + me.c

    zero4 = lambda n: jnp.zeros((4, n), F32)

    def put_own(ref, width, place_of):
        for i in range(ref.shape[1] // width):
            rows = jnp.concatenate([ref[:, pl.ds(width * i, width)].astype(F32), zero4(width)], axis=0)
            stage[mine, :, pl.ds(place_of(i), width)] = rows.astype(BF)

    def put_norm(gain, shift, at):
        eye = lax.broadcasted_iota(jnp.int32, (16, 12), 0) == lax.broadcasted_iota(jnp.int32, (16, 12), 1)
        lane = lax.broadcasted_iota(jnp.int32, (16, 128), 1)
        a = jnp.sum(jnp.where(eye, gain[...].astype(F32), 0.0), axis=1, keepdims=True)
        b = jnp.sum(jnp.where(eye, shift[...].astype(F32), 0.0), axis=1, keepdims=True)
        both = jnp.where(lane == 0, a, jnp.where(lane == 1, b, 0.0))
        stage[mine, :, pl.ds(at, 128)] = both.astype(BF)

    for k, ref in enumerate((wq_ref, wk_ref, wv_ref)):
        put_own(ref, 128, lambda i: set_at(i // 3, i % 3) + 128 * k)
    put_norm(n1g_ref, n1b_ref, N1_AT)
    put_norm(n2g_ref, n2b_ref, N2_AT)
    serve()
    put_own(wo_ref, D, lambda i: O_AT)
    put_own(wu_ref, D, up_at)
    serve()

    segs = jnp.broadcast_to(seg_ref[...], (T, T))
    rows_iota = lax.broadcasted_iota(jnp.int32, (T, T), 0)
    cols_iota = lax.broadcasted_iota(jnp.int32, (T, T), 1)
    allowed = (rows_iota >= cols_iota) & (segs.astype(F32).T == segs.astype(F32))
    mask[...] = jnp.where(allowed, 0.0, -1e30)

    serve()

    def norm1_rows(i):
        at = ds(i, ROW)
        hat, rstd = standardise(x_ref[at, :].astype(F32))
        xhat[at, :] = hat
        rstd1[at, :] = rstd

    loop(T // ROW, norm1_rows)
    serve()

    eye = (
        lax.broadcasted_iota(jnp.int32, (128, 128), 0) == lax.broadcasted_iota(jnp.int32, (128, 128), 1)
    ).astype(BF)
    rows1[...] = dot_nt(eye, weight(wide, N1_AT, 128))[:8]
    rows2[...] = dot_nt(eye, weight(wide, N2_AT, 128))[:8]

    def norm1_apply(i):
        at = ds(i, ROW)
        n1[at, :] = (xhat[at, :] * rows1[0:1, :] + rows1[1:2, :]).astype(BF)

    loop(T // ROW, norm1_apply)

    def project(half, s):
        w = wide[:, :, :, pl.ds(mult(set_at(half, s), 128), 384)].reshape(D, 384)
        qkv[:, pl.ds(mult(384 * (3 * half + s), 128), 384)] = dot(n1[...], w).astype(BF)

    lane = lax.broadcasted_iota(jnp.int32, (1, 128), 1)
    heads = [((lane >= 32 * h) & (lane < 32 * h + 32)).astype(F32).astype(BF) for h in range(4)]

    def group(ref, which, t, width=384):
        return ref[:, pl.ds(mult(width * t + 128 * which, 128), 128)]

    def attend(t):
        q4, k4, v4 = [group(qkv, i, t) for i in range(3)]
        vh = [v4 * heads[h] for h in range(4)]
        for rb in range(2):
            rows, nk = slice(128 * rb, 128 * rb + 128), 128 * rb + 128
            total = jnp.zeros((128, 128), F32)
            for h in range(4):
                s = dot_nt(q4[rows] * heads[h], k4[:nk]) * SCALE + mask[rows, :nk]
                e = jnp.exp(s - jnp.max(s, axis=1, keepdims=True))
                p = (e * (1.0 / jnp.sum(e, axis=1, keepdims=True))).astype(BF)
                probs[4 * t + h, rows, :nk] = p
                total = total + dot(p, vh[h][:nk])
            mixed[rows, pl.ds(mult(128 * t, 128), 128)] = total.astype(BF)

    for turn, s in enumerate((2, me.zl, 1 - me.zl)):
        if turn:
            serve()
        for half in range(2):
            project(half, s)
        serve()
        for half in range(2):
            attend(3 * half + s)
            serve()

    n2t, mixt = [gwide.at[:, :, :, pl.ds(256 * k, 256)] for k in range(2)]

    def transpose(src, dst):
        def body(i):
            dst[ds(i, 2)] = src[:, ds(i, 384)].T.reshape(2, 4, 48, T)

        loop(2, body)

    def turn_n1(i):
        n1t[ds(i, 384), :] = n1[:, ds(i, 384)].T

    transpose(mixed, mixt)
    loop(2, turn_n1)
    serve()

    def out_project(i):
        at = ds(i, 256)
        w = wide[:, :, :, pl.ds(mult(O_AT + 256 * i, 128), 256)].reshape(D, 256)
        hidden[:, at] = x_ref[:, at].astype(F32) + dot(mixed[...], w)

    loop(3, out_project)

    def norm2_rows(i):
        at = ds(i, ROW)
        hat, rstd = standardise(hidden[at, :])
        xhat2[at, :] = hat
        rstd2[at, :] = rstd
        n2[at, :] = (hat * rows2[0:1, :] + rows2[1:2, :]).astype(BF)

    loop(T // ROW, norm2_rows)
    transpose(n2, n2t)
    serve()

    c0 = (2.0 / 3.141592653589793) ** 0.5

    def feed(i):
        def part(j):
            at = pl.ds(up_at(i) + 256 * j, 256)
            v = dot(n2[...], wide[:, :, :, at].reshape(D, 256))
            sq = v * v
            th = jnp.tanh(c0 * v * (1.0 + 0.044715 * sq))
            half = 0.5 + 0.5 * th
            a = (v * half).astype(BF)
            keep = pl.ds(mult(768 * i + 256 * j, 128), 256)
            act[:, keep] = a
            slope[:, keep] = half + 0.5 * v * (1.0 - th * th) * (c0 * (1.0 + 0.134145 * sq))

        loop(3, part)
        serve()
        a = act[:, ds(i, 768)].T

        def grad(j):
            at = ds(j, 256)
            gdown[i, :, :, :, :, at] = dot(a, cot_ref[:, at]).astype(BF).reshape(4, 2, 2, 48, 256)

        loop(3, grad)

    for i in range(4):
        feed(i)
        serve()
    serve()

    acc_out[...] = hidden[...]
    acc_in[...] = jnp.zeros((T, D), F32)

    def feed_back(i):
        at = ds(i, 768)
        wd = down[i].reshape(768, 768)
        acc_out[...] += dot(act[:, at], wd)
        pg = (dot_nt(cot_ref[...], wd) * slope[:, at]).astype(BF)
        act[:, at] = pg
        serve()
        acc_in[...] += dot_nt(pg, weight(wide, up_at(i), D))
        serve()

        def grad(j):
            cols_j = pl.ds(up_at(i) + 256 * j, 256)
            pg_j = act[:, pl.ds(mult(768 * i + 256 * j, 128), 256)]
            gwide[:, :, :, cols_j] = dot(n2t[...].reshape(D, T), pg_j).astype(BF).reshape(4, 4, 48, 256)

        loop(3, grad)

    for i in range(4):
        feed_back(i)
        serve()
    out_ref[...] = acc_out[...].astype(BF)

    def norm_back(grad, hat, rstd, gain, at):
        gn = gain * grad
        m1 = jnp.mean(gn, axis=-1, keepdims=True)
        m2 = jnp.mean(gn * hat, axis=-1, keepdims=True)
        return (gn - m1 - hat * m2) * rstd

    def norm2_back(i, sums):
        at = ds(i, ROW)
        grad, hat = acc_in[at, :], xhat2[at, :]
        extra = norm_back(grad, hat, rstd2[at, :], rows2[0:1, :], at)
        hidden[at, :] = cot_ref[at, :].astype(F32) + extra
        a, b = sums
        return a + jnp.sum(grad * hat, axis=0, keepdims=True), b + jnp.sum(grad, axis=0, keepdims=True)

    def as_columns(sums, at):
        rows = jnp.concatenate([*sums, jnp.zeros((126, D), F32)], axis=0)
        gwide[:, :, :, pl.ds(at, 128)] = rows.T.astype(BF).reshape(4, 4, 48, 128)

    nothing = jnp.zeros((1, D), F32)
    as_columns(lax.fori_loop(0, T // ROW, norm2_back, (nothing, nothing)), N2_AT)
    n2[...] = hidden[...].astype(BF)

    serve()

    def o_back(i):
        at = ds(i, 256)
        b = n2[:, at]
        gwide[:, :, :, pl.ds(mult(O_AT + 256 * i, 128), 256)] = (
            dot(mixt[...].reshape(D, T), b).astype(BF).reshape(4, 4, 48, 256)
        )

    loop(3, o_back)
    serve()
    mgrad = n1
    mgrad[...] = dot_nt(n2[...], weight(wide, O_AT, D)).astype(BF)
    serve()

    def attend_back(t):
        q4, k4, v4 = [group(qkv, i, t) for i in range(3)]
        do4, o4 = group(mgrad, 0, t, 128), group(mixed, 0, t, 128)
        q4t, do4t = q4.T, do4.T
        kh = [k4 * heads[h] for h in range(4)]
        dk, dv = [], []
        total = [jnp.zeros((128, 128), F32)] * 2
        for h in range(4):
            hrows = slice(32 * h, 32 * h + 32)
            dkh, dvh = [], []
            for rb in range(2):
                rows, nk = slice(128 * rb, 128 * rb + 128), 128 * rb + 128
                dob = do4[rows] * heads[h]
                dot_row = jnp.sum(dob.astype(F32) * o4[rows].astype(F32), axis=1, keepdims=True)
                p = probs[4 * t + h, rows, :nk]
                sg = (p.astype(F32) * (dot_nt(dob, v4[:nk]) - dot_row)).astype(BF)
                total[rb] = total[rb] + dot(sg, kh[h][:nk])
                dkh.append(dot(q4t[hrows, rows], sg))
                dvh.append(dot(do4t[hrows, rows], p))
            for both, parts in ((dk, dkh), (dv, dvh)):
                both.append(jnp.concatenate([parts[1][:, :128] + parts[0], parts[1][:, 128:]], axis=1))
        at = 384 * t
        for rb in range(2):
            dqkv[pl.ds(128 * rb, 128), pl.ds(at, 128)] = (total[rb] * SCALE).astype(BF)
        dqkv[:, pl.ds(at + 128, 128)] = (jnp.concatenate(dk, axis=0).T * SCALE).astype(BF)
        dqkv[:, pl.ds(at + 256, 128)] = jnp.concatenate(dv, axis=0).T.astype(BF)

    for s in range(3):
        for half in range(2):
            attend_back(3 * half + s)
            serve()
        for half in range(2):
            part = dqkv[:, pl.ds(384 * (3 * half + s), 384)]
            gwide[:, :, :, pl.ds(set_at(half, s), 384)] = dot(n1t[...], part).astype(BF).reshape(4, 4, 48, 384)
        serve()
        for half in range(2):
            part = dqkv[:, pl.ds(384 * (3 * half + s), 384)]
            grad = dot_nt(part, weight(wide, set_at(half, s), 384))
            acc_in[...] = grad if s + half == 0 else acc_in[...] + grad
        if s < 2:
            serve()

    def norm1_back(i, sums):
        at = ds(i, ROW)
        grad, hat = acc_in[at, :], xhat[at, :]
        extra = norm_back(grad, hat, rstd1[at, :], rows1[0:1, :], at)
        ig_ref[at, :] = hidden[at, :] + extra
        a, b = sums
        return a + jnp.sum(grad * hat, axis=0, keepdims=True), b + jnp.sum(grad, axis=0, keepdims=True)

    as_columns(lax.fori_loop(0, T // ROW, norm1_back, (nothing, nothing)), N1_AT)
    serve()

    assert conductor.place == len(SCHEDULE)
    wire.drain()

    for k, ref in enumerate((dq_ref, dk_ref, dv_ref)):
        for i in range(6):
            ref[:, pl.ds(128 * i, 128)] = final[:12, pl.ds(set_at(i // 3, i % 3) + 128 * k, 128)]
    do_ref[...] = final[:12, pl.ds(O_AT, D)]
    for i in range(4):
        du_ref[:, pl.ds(768 * i, 768)] = final[:12, pl.ds(up_at(i), 768)]
    diag = lax.broadcasted_iota(jnp.int32, (16, 128), 0) == lax.broadcasted_iota(jnp.int32, (16, 128), 1)
    for at, refs in ((N1_AT, (dn1g_ref, dn1b_ref)), (N2_AT, (dn2g_ref, dn2b_ref))):
        for k, ref in enumerate(refs):
            col = final[:, at + k : at + k + 1]
            ref[...] = jnp.sum(jnp.where(diag, col, 0.0), axis=0, keepdims=True)[:, :12]


def publish_kernel(*refs):
    n = len(refs) // 2
    for i in range(n):
        refs[n + i][...] = refs[i][...]


VM = pl.BlockSpec(memory_space=pltpu.VMEM)


def per_device(*args):
    args = [a.reshape(1, 12) if a.ndim == 1 else a for a in args]
    like = jax.ShapeDtypeStruct
    vec, square = like((1, 12), F32), like((12, D), F32)
    scratch = [pltpu.VMEM(s, t) for g in REDUCED for s, t in reduce_shapes(g)]
    wide, down = pltpu.VMEM((4, 4, 48, WIDE), BF), pltpu.VMEM((4, 4, 2, 2, 48, D), BF)
    scratch += [wide, down, wide, down, pltpu.VMEM((16, WIDE), F32)]
    f32s, bfs = pltpu.VMEM((T, D), F32), pltpu.VMEM((T, D), BF)
    one, turned = pltpu.VMEM((T, 1), F32), pltpu.VMEM((D, T), BF)
    scratch += [pltpu.VMEM((T, T), F32), f32s, one, f32s, one]
    scratch += [bfs, turned, bfs, pltpu.VMEM((T, 3 * D), BF), bfs]
    scratch += [pltpu.VMEM((HEADS, T, T), BF), f32s]
    scratch += [pltpu.VMEM((T, FF), BF), pltpu.VMEM((T, FF), F32), f32s]
    scratch += [pltpu.VMEM((T, 3 * D), BF), pltpu.VMEM((8, D), F32), pltpu.VMEM((8, D), F32)]
    scratch += [pltpu.SemaphoreType.DMA((N_SEND,)), pltpu.SemaphoreType.DMA((N_RECV,))]
    outs = pl.pallas_call(
        layer_kernel,
        out_shape=(
            like((T, D), BF), like((T, D), F32), vec, vec, square, square, square, square, vec, vec,
            like((12, FF), F32), like((48, D), F32),
        ),
        in_specs=[VM] * 13,
        out_specs=(VM,) * 12,
        scratch_shapes=scratch,
        compiler_params=pltpu.CompilerParams(
            collective_id=0, has_side_effects=True, vmem_limit_bytes=VMEM_BYTES
        ),
        cost_estimate=pl.CostEstimate(flops=13 * 10**9, bytes_accessed=6 * 10**6, transcendentals=3 * 10**6),
        name="layer",
    )(*args)
    outs = pl.pallas_call(
        publish_kernel,
        out_shape=tuple(like(o.shape, o.dtype) for o in outs),
        in_specs=[VM] * 12,
        out_specs=(VM,) * 12,
        name="publish",
    )(*outs)
    return tuple(o.reshape(12) if o.shape == (1, 12) else o for o in outs)


def solution(mesh):
    placed = (
        P(("fsdp", "rep"), None),
        P(("fsdp", "rep"), None),
        P("fsdp"),
        P("fsdp"),
        P("fsdp", None),
        P("fsdp", None),
        P("fsdp", None),
        P("fsdp", None),
        P("fsdp"),
        P("fsdp"),
        P("fsdp", None),
        P("fsdp", None),
        P(("fsdp", "rep"), None),
    )
    return jax.shard_map(
        per_device,
        mesh=mesh,
        in_specs=placed,
        out_specs=(
            P(("fsdp", "rep"), None),
            P(("fsdp", "rep"), None),
            P("fsdp"),
            P("fsdp"),
            P("fsdp", None),
            P("fsdp", None),
            P("fsdp", None),
            P("fsdp", None),
            P("fsdp"),
            P("fsdp"),
            P("fsdp", None),
            P("fsdp", None),
        ),
        check_vma=False,
    )
```

```python
import functools

import jax
import jax.numpy as jnp
from jax import lax
from jax.experimental import pallas as pl
from jax.experimental.pallas import tpu as pltpu
from jax.sharding import PartitionSpec as P

HEADS = 24
HEAD_DIM = 32
D = 768
FF = 3072
BF = jnp.bfloat16
F32 = jnp.float32
MESH = pl.DeviceIdType.MESH

WIDE = 6400
DOWN = 2, 4
START = (0, 2560, 0, 0, 0, 768, 2560, 4096)
HALF = (1280, 1920, 0, 1280, 0, 1280, 768, 1152)
WIDTH = (1280, 1920, 768, 768, 768, 512, 768, 1152)
P_AT = (768, 0, 0, 0, 0, 0, 0, 0)
Q_AT = (0, 384, 384, 256, 384, 256, 384, 384)
SIZE = ((512, 384), (384, 768), (384, 384), (256, 256), (384, 384), (256, 256), (384, 384), (384, 384))
LOW = ((256, 256), (128, 384), (128, 256), (128, 128), (128, 256), (128, 128), (128, 256), (128, 256))
ZED = (True, True, False, True, False, False, False, True)
STRAIGHT = (False, False, False)
SPLIT = (False, False, False, False, False, False, False, False)
FINE = (0, 0, 0)
DIRECT = (False, False, False, False, False, True, False, False)
P_, QM, QO = 0, 1, 2
N_RECV = 335
N_SEND = 40
VMEM_BYTES = 66700000


class Place:
    def __init__(self):
        f = lax.axis_index("fsdp")
        r = lax.axis_index("rep")
        c = lax.rem(f, 2)
        zl = lax.rem(lax.div(f, 2), 2)
        y = lax.rem(lax.div(f, 4), 4)
        x = lax.div(f, 16)
        self.r, self.c, self.zl, self.y, self.x = r, c, zl, y, x
        self.xs = {d: lax.rem(x + (d + 4), 4) if d else x for d in (-1, 0, 1, 2)}
        self.ys = {d: lax.rem(y + (d + 4), 4) if d else y for d in (-1, 0, 1, 2)}
        low = zl * 2 + c
        self.dx = {d: {"fsdp": self.xs[d] * 16 + y * 4 + low, "rep": r} for d in (-1, 1, 2)}
        self.dy = {d: {"fsdp": x * 16 + self.ys[d] * 4 + low, "rep": r} for d in (-1, 1, 2)}
        turned = f + 2 - 4 * zl
        self.sibling = {"fsdp": f + 1 - 2 * c, "rep": r}
        self.other = {"fsdp": f, "rep": 1 - r}
        self.above = {"fsdp": turned, "rep": lax.rem(r + zl, 2)}
        self.below = {"fsdp": turned, "rep": lax.rem(r + 1 - zl, 2)}
        self.share_to = {"fsdp": turned, "rep": lax.rem(r + zl * (1 - c) + (1 - zl) * c, 2)}
        self.peers = [self.sibling, self.above, self.below, self.other, *self.dx.values(), *self.dy.values()]
        self.starts = {}
        for g in range(len(START)):
            for core, cc in ((0, c), (1, 1 - c)):
                base = START[g] + cc * HALF[g]
                self.starts[g, None, core] = base
                q = base + Q_AT[g]
                self.starts[g, P_, core] = base + P_AT[g]
                self.starts[g, QM, core] = q + zl * SIZE[g][1] if ZED[g] else q
                self.starts[g, QO, core] = q + (1 - zl) * SIZE[g][1]


class Wire:
    def __init__(self, place, send, recv):
        self.place, self.send_sem, self.recv_sem = place, send, recv
        self.n = self.m = 0
        self.open = {}

    def slot(self):
        k = self.m % N_SEND
        self.m += 1
        if k in self.open:
            self.open.pop(k).wait_send()
        return k

    def put(self, src, dst, to):
        k = self.slot()
        assert self.n < N_RECV
        copy = pltpu.make_async_remote_copy(
            src_ref=src,
            dst_ref=dst,
            send_sem=self.send_sem.at[k],
            recv_sem=self.recv_sem.at[self.n],
            device_id=to,
            device_id_type=MESH,
        )
        copy.start()
        self.open[k] = copy
        self.n += 1
        return copy

    def drain(self):
        for copy in self.open.values():
            copy.wait_send()
        self.open = {}


def call_out(place):
    barrier = pltpu.get_barrier_semaphore()
    for peer in place.peers:
        pl.semaphore_signal(barrier, inc=1, device_id=peer, device_id_type=MESH)
    return barrier


def kind(k):
    return 0 if k == P_ else 1


def halves(g, k):
    n, low = SIZE[g][kind(k)], LOW[g][kind(k)]
    return pl.ds(0, low), pl.ds(low, n - low)


def columns_of(g, k, me, h=None, core=0):
    n, low = SIZE[g][kind(k)], LOW[g][kind(k)]
    off, width = (0, n) if h is None else ((0, low) if h == 0 else (low, n - low))
    base = me.starts[g, k, core]
    return pl.ds(pl.multiple_of(base + off if off else base, 128), width)


class Piece:
    def __init__(self, me, wide, down, g, k):
        self.me, self.wide, self.down, self.g, self.k = me, wide, down, g, k
        self.us, self.ws = (me.xs, me.ys) if k == P_ else (me.ys, me.xs)
        self.first, self.second = (me.dx, me.dy) if k == P_ else (me.dy, me.dx)

    def ref(self, bu, bw, h=None, core=0):
        bx, by = (bu, bw) if self.k == P_ else (bw, bu)
        at = columns_of(self.g, self.k, self.me, h, core)
        if self.g not in DOWN:
            return self.wide.at[bx, by, :, at]
        return self.down.at[bx, by, :, 1 - self.me.c if core else self.me.c, :, at]

    def at(self, du, dw, h=None):
        return self.ref(self.us[du], self.ws[dw], h)

    def across(self, dw, h=None):
        return self.ref(slice(None), self.ws[dw], h)

    def along(self, du, h=None):
        return self.ref(self.us[du], slice(None), h)

    def of_sibling(self):
        return self.ref(slice(None), slice(None), core=1)


def wait(*copies):
    yield copies
    for copy in copies:
        copy.wait_recv()


def gather_plane(wire, wide, down, g, k, sib, zs):
    me = wire.place
    s = Piece(me, wide, down, g, k)

    def go(ref, to):
        return wire.put(ref, ref, to)

    def share(name, *where):
        if k == QM and ZED[g]:
            lo, hi = [getattr(s, name)(*where, h) for h in range(2)]
            zs.append(((go(lo, me.above), go(hi, me.below)), name, where))
        sib.append(go(getattr(s, name)(*where), me.sibling))

    out = {}

    def spread(du):
        for d in reach:
            out[d, du] = go(s.at(du, 0), s.second[d])

    if not STRAIGHT[g]:
        reach = (1, -1)
        a, b = go(s.at(0, 0), s.first[1]), go(s.at(0, 0), s.first[-1])
        spread(0)
        yield from wait(a)
        a = go(s.at(-1, 0, 0), s.first[1])
        spread(-1)
        share("at", -1, 0)
        yield from wait(b)
        b = go(s.at(1, 0, 1), s.first[-1])
        spread(1)
        share("at", 1, 0)
        yield from wait(a, b)
        spread(2)
        share("at", 2, 0)
        if FINE[g] == 2 or (FINE[g] == 1 and k == QM):
            far = []
            for du in (0, -1, 1, 2):
                yield from wait(out[1, du])
                a = go(s.at(du, -1, 0), s.second[1])
                share("at", du, -1)
                yield from wait(out[-1, du])
                b = go(s.at(du, 1, 1), s.second[-1])
                share("at", du, 1)
                far.append((a, b))
            for du, copies in zip((0, -1, 1, 2), far):
                yield from wait(*copies)
                share("at", du, 2)
            return
        yield from wait(*[out[1, du] for du in (0, -1, 1, 2)])
        a = go(s.across(-1, 0), s.second[1])
        share("across", -1)
        yield from wait(*[out[-1, du] for du in (0, -1, 1, 2)])
        b = go(s.across(1, 1), s.second[-1])
        share("across", 1)
        yield from wait(a, b)
        share("across", 2)
        return
    reach = (1, -1, 2)
    near = {d: go(s.at(0, 0), s.first[d]) for d in reach}
    spread(0)
    for d in (1, -1, 2):
        du = -d if d < 2 else 2
        yield from wait(near[d])
        spread(du)
        share("at", du, 0)
    for d in (1, -1, 2):
        dw = -d if d < 2 else 2
        yield from wait(*[out[d, du] for du in (0, -1, 1, 2)])
        share("across", dw)


def gather_cross(wire, wide, down, g, sib, zs):
    me = wire.place
    theirs = Piece(me, wide, down, g, QO)
    for n in range(15 if FINE[g] else 6):
        yield lambda: zs[n][0] if len(zs) > n else None
        copies, name, where = zs[n]
        for copy in copies:
            copy.wait_recv()
        ref = getattr(theirs, name)(*where)
        sib.append(wire.put(ref, ref, me.sibling))


def gather_end(n, sib):
    for i in range(n):
        yield lambda: (sib[i],) if len(sib) > i else None
        sib[i].wait_recv()


def gather_streams(wire, wide, down, g):
    sib, zs = {P_: [], QM: [], QO: []}, []
    streams = [gather_plane(wire, wide, down, g, k, sib[k], zs) for k in (P_, QM)]
    fine = {P_: FINE[g] == 2, QM: FINE[g] > 0}
    streams += [gather_end(15 if fine[k] else 6, sib[k]) for k in (P_, QM)]
    if ZED[g]:
        streams += [gather_cross(wire, wide, down, g, sib[QO], zs), gather_end(15 if FINE[g] else 6, sib[QO])]
    return streams


def join(stage, wide, me, g):
    step = 640

    def body(i, carry):
        at = pl.ds(pl.multiple_of(START[g] + i * step, 128), step)
        rows = [stage[o, :, at].astype(F32)[:12] for o in range(4)]
        wide[me.x, me.y, :, at] = jnp.concatenate(rows, axis=0).astype(BF)
        return carry

    lax.fori_loop(0, 2 * HALF[g] // step, body, 0)


def gather_front(wire, own_down, stage, wide, down, g):
    me = wire.place
    mine = 2 * me.zl + me.c
    if g not in DOWN:
        at = pl.ds(START[g], 2 * HALF[g])
        src = dst = stage.at[mine, :, at]
        hers = stage.at[2 * (1 - me.zl) + me.c, :, at]
    else:
        src, dst = own_down, down.at[me.x, me.y, me.zl, me.c]
        hers = down.at[me.x, me.y, 1 - me.zl, me.c]
        down[me.x, me.y, me.zl, me.c] = own_down[...]
    a = wire.put(src, dst, me.share_to)
    b = wire.put(src, dst, me.sibling)
    yield from wait(a)
    c = wire.put(hers, hers, me.sibling)
    yield from wait(b, c)
    if g not in DOWN:
        join(stage, wide, me, g)


def rows_of(g):
    return (2, 48) if g in DOWN else (48,)


REDUCED = (3, 4, 5, 6, 7)


def reduce_shapes(g):
    rows, shapes = rows_of(g), []
    for k in (P_, QM):
        n, low = SIZE[g][kind(k)], LOW[g][kind(k)]
        high = n - low
        if DIRECT[g]:
            low, high = n, 128
        own = (48,) if g in DOWN else (2, 16)
        shapes += [(4, 4, *rows, n), (4, *rows, low), (4, *rows, high), (4, *rows, n), (4, *rows, n)]
        shapes += [(*rows, low), (*rows, high), (*rows, n), (*rows, n), (2, *own, n), (*own, n), (*own, n), (*own, n)]
    if ZED[g]:
        shapes += [(4, 4, *rows, SIZE[g][1])] * 2
    shapes = [(s, BF) for s in shapes]
    return shapes if g in DOWN else shapes + [((16, WIDTH[g]), F32)]


def add_blocks(dst, src):
    def body(i, carry):
        ref = dst(i)
        ref[...] = ref[...] + src(i)[...]
        return carry

    lax.fori_loop(0, 4, body, 0)


def add_one(ref, a):
    ref[...] = ref[...] + a[...]


def add_two(ref, a, b):
    ref[...] = (ref[...].astype(F32) + a[...].astype(F32) + b[...].astype(F32)).astype(BF)


def add_three(ref, a, b, c):
    total = ref[...].astype(F32) + a[...].astype(F32) + (b[...].astype(F32) + c[...].astype(F32))
    ref[...] = total.astype(BF)


def owners_rows(st, ref, others, g):
    total = ref[...].astype(F32)
    for other in others:
        total = total + other[...].astype(F32)
    if g not in DOWN:
        zero = jnp.zeros((4, total.shape[1]), F32)
        for o in range(4):
            st[o // 2, o % 2] = jnp.concatenate([total[12 * o : 12 * o + 12], zero], axis=0).astype(BF)
    else:
        st[...] = total.astype(BF)


def add_planes(me, g, k, st, rzp, rzm, rr, final, final_down, so):
    def total_of(core):
        def pick(ref):
            return (ref[...] if g in DOWN else ref[core]).astype(F32)

        first = pick(st.at[me.zl]) + pick(rr)
        second = pick(rzp) + pick(rzm)
        if k == QM and ZED[g]:
            return (QM, first), (QO, second)
        return ((k, first + second),)

    out = final_down if g in DOWN else final
    for kk, v in total_of(me.c):
        out[:, columns_of(g, kk, me)] = v
    if g not in DOWN:
        for kk, v in total_of(1 - me.c):
            base = me.starts[g, kk, 0] - me.starts[g, None, 0]
            so[:, pl.ds(pl.multiple_of(base, 128), v.shape[1])] = v


def reduce_plane(wire, wide, down, bufs, got, z_in, done, finals, g, k):
    me = wire.place
    s = Piece(me, wide, down, g, k)
    sb, b1p, b1m, b2p, b2m, c1p, c1m, c2p, c2m, st, rzp, rzm, rr = bufs[13 * k : 13 * k + 13]
    lo, hi = halves(g, k)
    any_lo, any_hi = (..., lo), (..., hi)
    crosses = k == QM and ZED[g]

    def add_along(du, buf):
        bu = s.us[du]
        add_blocks(lambda i: s.ref(bu, i), lambda i: buf.at[bu, i] if k == P_ else buf.at[i, bu])

    def add_half(du, h, buf):
        bu = s.us[du]
        add_blocks(lambda i: s.ref(bu, i, h), lambda i: buf.at[i])

    def ready(du):
        if crosses:
            yield lambda: z_in.get(du)
            for copy in z_in[du]:
                copy.wait_recv()
            add_along(du, bufs[27])
        else:
            if len(got) > 1:
                yield from wait(got[du])
            add_along(du, sb)

    if crosses or len(got) == 1:
        yield from wait(*got.values())
    if crosses:
        for du in (2, 1, -1, 0):
            add_along(du, sb)
    if DIRECT[g]:
        near = []
        for du, buf in ((2, b1p), (1, b2p), (-1, b2m)):
            yield from ready(du)
            near.append(wire.put(s.along(du), buf, s.first[du]))
        yield from ready(0)
        yield from wait(*near)
        near = []
        for dw, buf in ((2, c1p), (1, c2p), (-1, c2m), (0, None)):
            bw = s.ws[dw]
            add_three(s.at(0, dw), b1p.at[bw], b2p.at[bw], b2m.at[bw])
            if dw:
                near.append(wire.put(s.at(0, dw), buf, s.second[dw]))
        yield from wait(*near)
        owners_rows(st, s.at(0, 0), (c1p, c2p, c2m), g)
        yield from over_planes(wire, me, g, k, bufs, st, rzp, rzm, rr, finals, done)
        return
    yield from ready(2)
    r1p = wire.put(s.along(2, 0), b1p, s.first[1])
    r1m = wire.put(s.along(2, 1), b1m, s.first[-1])
    yield from ready(1)
    r2p_hi = wire.put(s.along(1, 1), b2p.at[any_hi], s.first[1])
    yield from ready(-1)
    r2m_lo = wire.put(s.along(-1, 0), b2m.at[any_lo], s.first[-1])
    yield from ready(0)
    yield from wait(r1p)
    add_half(1, 0, b1p)
    r2p_lo = wire.put(s.along(1, 0), b2p.at[any_lo], s.first[1])
    yield from wait(r1m)
    add_half(-1, 1, b1m)
    r2m_hi = wire.put(s.along(-1, 1), b2m.at[any_hi], s.first[-1])
    yield from wait(r2p_hi, r2m_lo, r2p_lo, r2m_hi)

    def close(dw):
        add_two(s.at(0, dw), b2p.at[s.ws[dw]], b2m.at[s.ws[dw]])

    close(2)
    r1p = wire.put(s.at(0, 2, 0), c1p, s.second[1])
    r1m = wire.put(s.at(0, 2, 1), c1m, s.second[-1])
    close(1)
    r2p_hi = wire.put(s.at(0, 1, 1), c2p.at[any_hi], s.second[1])
    close(-1)
    r2m_lo = wire.put(s.at(0, -1, 0), c2m.at[any_lo], s.second[-1])
    close(0)
    yield from wait(r1p)
    add_one(s.at(0, 1, 0), c1p)
    r2p_lo = wire.put(s.at(0, 1, 0), c2p.at[any_lo], s.second[1])
    yield from wait(r1m)
    add_one(s.at(0, -1, 1), c1m)
    r2m_hi = wire.put(s.at(0, -1, 1), c2m.at[any_hi], s.second[-1])
    yield from wait(r2p_hi, r2m_lo, r2p_lo, r2m_hi)
    owners_rows(st, s.at(0, 0), (c2p, c2m), g)
    yield from over_planes(wire, me, g, k, bufs, st, rzp, rzm, rr, finals, done)


def over_planes(wire, me, g, k, bufs, st, rzp, rzm, rr, finals, done):
    a = wire.put(st.at[1 - me.zl], rzp, me.above)
    b = wire.put(st.at[1 - me.zl], rzm, me.below)
    c = wire.put(st.at[me.zl], rr, me.other)
    yield from wait(a, b, c)
    add_planes(me, g, k, st, rzp, rzm, rr, *finals, None if g in DOWN else bufs[-1])
    done.append(k)
    if g not in DOWN and len(done) == 2:
        at = pl.ds(pl.multiple_of(me.starts[g, None, 0], 128), WIDTH[g])
        yield from wait(wire.put(bufs[-1], finals[0].at[:, at], me.sibling))


def reduce_cross(wire, wide, down, bufs, got, z_in, g):
    me = wire.place
    theirs = Piece(me, wide, down, g, QO)
    lo, hi = halves(g, QO)
    yield from wait(got)
    for du in (2, 1, -1, 0):
        bu = theirs.us[du]
        add_blocks(lambda i: theirs.ref(bu, i), lambda i: bufs[26].at[i, bu])
        a = wire.put(theirs.along(du, 0), bufs[27].at[:, bu, ..., lo], me.below)
        b = wire.put(theirs.along(du, 1), bufs[27].at[:, bu, ..., hi], me.above)
        z_in[du] = a, b
        if du:
            yield None


def reduce_streams(wire, wide, down, bufs, finals, g):
    me = wire.place
    pieces = {k: Piece(me, wide, down, g, k) for k in (P_, QM, QO)}
    z_in, done, streams = {}, [], []
    if ZED[g]:
        got = wire.put(pieces[QO].of_sibling(), bufs[26], me.sibling)
        streams.append(reduce_cross(wire, wide, down, bufs, got, z_in, g))
    for k in (P_, QM):
        s, sb = pieces[k], bufs[13 * k]
        if SPLIT[g]:
            got = {}
            for du in (2, 1, -1, 0):
                bu = s.us[du]
                dst = sb.at[bu] if k == P_ else sb.at[:, bu]
                got[du] = wire.put(s.ref(s.us[du], slice(None), core=1), dst, me.sibling)
        else:
            got = {0: wire.put(s.of_sibling(), sb, me.sibling)}
        streams.append(reduce_plane(wire, wide, down, bufs, got, z_in, done, finals, g, k))
    return streams


class Conductor:
    def __init__(self, openers):
        self.openers = openers
        self.streams = {}
        self.place = 0

    def serve(self):
        for key, i in SCHEDULE[self.place]:
            if i < 0:
                self.streams.update({(key, k): s for k, s in enumerate(self.openers[key]())})
                for k in self.streams:
                    if k[0] == key:
                        next(self.streams[k])
            else:
                next(self.streams[key, i], None)
        self.place += 1


SCHEDULE = (
    ((5, -1),),
    (),
    ((6, -1), (7, -1),),
    ((5, 0), (6, 0), (5, 0), (0, -1), (7, 0), (6, 0), (7, 0), (0, 0), (0, 0), (0, 1), (0, 1), (0, 2), (0, 2), (0, 0),
     (1, -1), (0, 3), (0, 3), (0, 4), (0, 4), (0, 2), (0, 1), (1, 0), (0, 5), (1, 0), (0, 0), (0, 0), (0, 5), (0, 3),
     (0, 4), (1, 2), (1, 2), (0, 1), (0, 1), (0, 2), (1, 1), (1, 1), (1, 0), (0, 2), (0, 5), (0, 3), (0, 3), (1, 3),
     (1, 3), (1, 2), (0, 1), (0, 4), (0, 0), (1, 1), (1, 0), (1, 0), (0, 4), (0, 3), (0, 5), (0, 2), (2, -1), (1, 4),),
    ((1, 2), (1, 2), (1, 3), (1, 4),),
    ((0, 5), (1, 1), (1, 1), (1, 5),),
    ((0, 4), (1, 0),),
    (),
    ((1, 4), (1, 5), (2, 0), (2, 0),),
    ((1, 3),),
    ((1, 3), (2, 1), (0, 5),),
    (),
    ((1, 2), (1, 5), (2, 1), (2, 2), (2, 2),),
    ((1, 4),),
    ((2, 3),),
    ((1, 1), (2, 0), (2, 3), (1, 5), (2, 1), (1, 4), (1, 3), (2, 2), (2, 3), (2, 0), (2, 0), (1, 5), (2, 1), (2, 1),
     (1, 4), (2, 2), (2, 2), (2, 3), (2, 3), (1, 5),),
    ((2, 0), (2, 1),),
    (),
    (),
    (),
    (),
    (),
    (),
    (),
    ((2, 2),),
    ((14, -1), (2, 3),),
    (),
    (),
    (),
    (),
    (),
    ((16, -1), (14, 0),),
    (),
    ((14, 1),),
    ((16, 0),),
    ((14, 0), (16, 1),),
    (),
    ((14, 0),),
    (),
    ((17, -1),),
    ((14, 1), (14, 1),),
    ((16, 0),),
    ((17, 0), (17, 0), (17, 0), (17, 0), (17, 1), (16, 0), (16, 1), (16, 1),),
    ((17, 2),),
    (),
    ((17, 2), (17, 1), (14, 0),),
    ((17, 1), (17, 2), (14, 1),),
    ((13, -1),),
    (),
    ((17, 2), (16, 0), (14, 1), (13, 0), (13, 0), (13, 0), (13, 0), (17, 2), (17, 2), (17, 2), (13, 1), (14, 0),
     (14, 0), (16, 1), (13, 2), (17, 1), (14, 1),),
    ((13, 1), (13, 1), (13, 2), (13, 2), (16, 0), (16, 0),),
    (),
    ((15, -1), (13, 2), (13, 2), (17, 2), (17, 1), (17, 1), (14, 0), (14, 1), (13, 1), (16, 1), (16, 1), (13, 2),
     (13, 2), (15, 0), (17, 2), (17, 2), (15, 1), (16, 0), (13, 1), (17, 1), (13, 1), (16, 1), (14, 0), (13, 2),
     (14, 1), (16, 0), (15, 0), (17, 1), (17, 2), (13, 2), (13, 2), (16, 1), (15, 1), (13, 1), (15, 0), (13, 2),
     (16, 1), (17, 2), (15, 1), (13, 1), (15, 0), (17, 2), (13, 2), (15, 1), (13, 2), (15, 1),),
)


def dot(a, b):
    return lax.dot_general(a, b, (((1,), (0,)), ((), ())), preferred_element_type=F32)


def dot_nt(a, b):
    return lax.dot_general(a, b, (((1,), (1,)), ((), ())), preferred_element_type=F32)


def loop(n, body):
    if n <= UNROLLED:
        for i in range(n):
            body(i)
        return

    def step(i, carry):
        body(i)
        return carry

    lax.fori_loop(0, n, step, 0)


def mult(v, n):
    return v if isinstance(v, int) else pl.multiple_of(v, n)


def ds(i, n):
    return pl.ds(mult(i * n, n), n)


UNROLLED = 3
T = 256
SCALE = HEAD_DIM ** (-0.5)
O_AT, N1_AT, N2_AT = 4096, 1152, 2432


def set_at(half, s):
    return 1280 * half + 384 * s


def up_at(i):
    return 2560 + 768 * i + (768 if i > 1 else 0)


ROW = 64


def standardise(v):
    centre = jnp.mean(v, axis=-1, keepdims=True)
    centred = v - centre
    spread = jnp.mean(centred * centred, axis=-1, keepdims=True)
    rstd = lax.rsqrt(spread + 1e-05)
    return centred * rstd, rstd


def weight(wide, at, width):
    return wide[:, :, :, pl.ds(at, width)].reshape(D, width)


def layer_kernel(
    x_hbm, seg_ref, n1g_ref, n1b_ref, wq_ref, wk_ref, wv_ref, wo_ref, n2g_ref, n2b_ref, wu_ref, wd_ref, cot_hbm,
    out_hbm, ig_hbm, dn1g_ref, dn1b_ref, dq_ref, dk_ref, dv_ref, do_ref, dn2g_ref, dn2b_ref, du_ref, dd_ref,
    *scratch,
):
    bufs = {}
    for g in REDUCED:
        n = len(reduce_shapes(g))
        bufs[g], scratch = scratch[:n], scratch[n:]
    (
        wide, down, gwide, gdown, final,
        mask, xhat, rstd1, xhat2, rstd2, n1, n1t, n2, qkv, mixed, probs, hidden,
        act, slope, acc_in, dqkv, rows1, rows2, x_ref, cot_ref, out_ref, ig_ref, io, send, recv,
    ) = scratch
    stage = gwide.at[0, :, pl.ds(0, 16)]
    acc_out = ig_ref
    place = me = Place()
    x_in = pltpu.make_async_copy(x_hbm, x_ref, io.at[0])
    cot_in = pltpu.make_async_copy(cot_hbm, cot_ref, io.at[1])
    x_in.start()
    cot_in.start()
    barrier = call_out(place)
    wire = Wire(place, send, recv)
    openers = {g: lambda g=g: gather_streams(wire, wide, down, g) for g in range(3)}
    openers.update({5 + g: lambda g=g: [gather_front(wire, wd_ref, stage, wide, down, g)] for g in range(3)})
    finals = final, dd_ref
    openers.update({10 + g: lambda g=g: reduce_streams(wire, gwide, gdown, bufs[g], finals, g) for g in REDUCED})
    conductor = Conductor(openers)
    serve = conductor.serve
    mine = 2 * me.zl + me.c

    zero4 = lambda n: jnp.zeros((4, n), F32)

    def put_own(ref, width, place_of):
        for i in range(ref.shape[1] // width):
            rows = jnp.concatenate([ref[:, pl.ds(width * i, width)].astype(F32), zero4(width)], axis=0)
            stage[mine, :, pl.ds(place_of(i), width)] = rows.astype(BF)

    def put_norm(gain, shift, at):
        eye = lax.broadcasted_iota(jnp.int32, (16, 12), 0) == lax.broadcasted_iota(jnp.int32, (16, 12), 1)
        lane = lax.broadcasted_iota(jnp.int32, (16, 128), 1)
        a = jnp.sum(jnp.where(eye, gain[...].astype(F32), 0.0), axis=1, keepdims=True)
        b = jnp.sum(jnp.where(eye, shift[...].astype(F32), 0.0), axis=1, keepdims=True)
        both = jnp.where(lane == 0, a, jnp.where(lane == 1, b, 0.0))
        stage[mine, :, pl.ds(at, 128)] = both.astype(BF)

    for k, ref in enumerate((wq_ref, wk_ref, wv_ref)):
        put_own(ref, 128, lambda i: set_at(i // 3, i % 3) + 128 * k)
    put_norm(n1g_ref, n1b_ref, N1_AT)
    put_norm(n2g_ref, n2b_ref, N2_AT)
    pl.semaphore_wait(barrier, len(place.peers))
    serve()
    put_own(wo_ref, D, lambda i: O_AT)
    put_own(wu_ref, D, up_at)
    serve()

    segs = jnp.broadcast_to(seg_ref[...], (T, T))
    rows_iota = lax.broadcasted_iota(jnp.int32, (T, T), 0)
    cols_iota = lax.broadcasted_iota(jnp.int32, (T, T), 1)
    allowed = (rows_iota >= cols_iota) & (segs.astype(F32).T == segs.astype(F32))
    mask[...] = jnp.where(allowed, 0.0, -1e30)

    serve()

    def norm1_rows(i):
        at = ds(i, ROW)
        hat, rstd = standardise(x_ref[at, :].astype(F32))
        xhat[at, :] = hat
        rstd1[at, :] = rstd

    x_in.wait()
    loop(T // ROW, norm1_rows)
    serve()

    eye = (
        lax.broadcasted_iota(jnp.int32, (128, 128), 0) == lax.broadcasted_iota(jnp.int32, (128, 128), 1)
    ).astype(BF)
    rows1[...] = dot_nt(eye, weight(wide, N1_AT, 128))[:8]
    rows2[...] = dot_nt(eye, weight(wide, N2_AT, 128))[:8]

    def norm1_apply(i):
        at = ds(i, ROW)
        n1[at, :] = (xhat[at, :] * rows1[0:1, :] + rows1[1:2, :]).astype(BF)

    loop(T // ROW, norm1_apply)

    def project(half, s):
        w = wide[:, :, :, pl.ds(mult(set_at(half, s), 128), 384)].reshape(D, 384)
        qkv[:, pl.ds(mult(384 * (3 * half + s), 128), 384)] = dot(n1[...], w).astype(BF)

    lane = lax.broadcasted_iota(jnp.int32, (1, 128), 1)
    heads = [((lane >= 32 * h) & (lane < 32 * h + 32)).astype(F32).astype(BF) for h in range(4)]

    def group(ref, which, t, width=384):
        return ref[:, pl.ds(mult(width * t + 128 * which, 128), 128)]

    def attend(t):
        q4, k4, v4 = [group(qkv, i, t) for i in range(3)]
        vh = [v4 * heads[h] for h in range(4)]
        for rb in range(2):
            rows, nk = slice(128 * rb, 128 * rb + 128), 128 * rb + 128
            total = jnp.zeros((128, 128), F32)
            for h in range(4):
                s = dot_nt(q4[rows] * heads[h], k4[:nk]) * SCALE + mask[rows, :nk]
                e = jnp.exp(s - jnp.max(s, axis=1, keepdims=True))
                p = (e * (1.0 / jnp.sum(e, axis=1, keepdims=True))).astype(BF)
                probs[4 * t + h, rows, :nk] = p
                total = total + dot(p, vh[h][:nk])
            mixed[rows, pl.ds(mult(128 * t, 128), 128)] = total.astype(BF)

    for turn, s in enumerate((2, me.zl, 1 - me.zl)):
        if turn:
            serve()
        for half in range(2):
            project(half, s)
        serve()
        for half in range(2):
            attend(3 * half + s)
            serve()

    n2t, mixt = [gwide.at[:, :, :, pl.ds(256 * k, 256)] for k in range(2)]

    def transpose(src, dst):
        def body(i):
            dst[ds(i, 2)] = src[:, ds(i, 384)].T.reshape(2, 4, 48, T)

        loop(2, body)

    def turn_n1(i):
        n1t[ds(i, 384), :] = n1[:, ds(i, 384)].T

    transpose(mixed, mixt)
    loop(2, turn_n1)
    serve()

    def out_project(i):
        at = ds(i, 256)
        w = wide[:, :, :, pl.ds(mult(O_AT + 256 * i, 128), 256)].reshape(D, 256)
        hidden[:, at] = x_ref[:, at].astype(F32) + dot(mixed[...], w)

    loop(3, out_project)

    def norm2_rows(i):
        at = ds(i, ROW)
        hat, rstd = standardise(hidden[at, :])
        xhat2[at, :] = hat
        rstd2[at, :] = rstd
        n2[at, :] = (hat * rows2[0:1, :] + rows2[1:2, :]).astype(BF)

    loop(T // ROW, norm2_rows)
    transpose(n2, n2t)
    serve()

    cot_in.wait()
    c0 = (2.0 / 3.141592653589793) ** 0.5

    def feed(i):
        def part(j):
            at = pl.ds(up_at(i) + 256 * j, 256)
            v = dot(n2[...], wide[:, :, :, at].reshape(D, 256))
            sq = v * v
            th = jnp.tanh(c0 * v * (1.0 + 0.044715 * sq))
            half = 0.5 + 0.5 * th
            a = (v * half).astype(BF)
            keep = pl.ds(mult(768 * i + 256 * j, 128), 256)
            act[:, keep] = a
            slope[:, keep] = half + 0.5 * v * (1.0 - th * th) * (c0 * (1.0 + 0.134145 * sq))

        loop(3, part)
        serve()
        a = act[:, ds(i, 768)].T

        def grad(j):
            at = ds(j, 256)
            gdown[i, :, :, :, :, at] = dot(a, cot_ref[:, at]).astype(BF).reshape(4, 2, 2, 48, 256)

        loop(3, grad)

    for i in range(4):
        feed(i)
        serve()
    serve()

    acc_out[...] = hidden[...]
    acc_in[...] = jnp.zeros((T, D), F32)

    def feed_back(i):
        at = ds(i, 768)
        wd = down[i].reshape(768, 768)
        acc_out[...] += dot(act[:, at], wd)
        pg = (dot_nt(cot_ref[...], wd) * slope[:, at]).astype(BF)
        act[:, at] = pg
        serve()
        acc_in[...] += dot_nt(pg, weight(wide, up_at(i), D))
        serve()

        def grad(j):
            cols_j = pl.ds(up_at(i) + 256 * j, 256)
            pg_j = act[:, pl.ds(mult(768 * i + 256 * j, 128), 256)]
            gwide[:, :, :, cols_j] = dot(n2t[...].reshape(D, T), pg_j).astype(BF).reshape(4, 4, 48, 256)

        loop(3, grad)

    for i in range(4):
        feed_back(i)
        serve()
    out_ref[...] = acc_out[...].astype(BF)
    out_copy = pltpu.make_async_copy(out_ref, out_hbm, io.at[2])
    out_copy.start()

    def norm_back(grad, hat, rstd, gain, at):
        gn = gain * grad
        m1 = jnp.mean(gn, axis=-1, keepdims=True)
        m2 = jnp.mean(gn * hat, axis=-1, keepdims=True)
        return (gn - m1 - hat * m2) * rstd

    def norm2_back(i, sums):
        at = ds(i, ROW)
        grad, hat = acc_in[at, :], xhat2[at, :]
        extra = norm_back(grad, hat, rstd2[at, :], rows2[0:1, :], at)
        hidden[at, :] = cot_ref[at, :].astype(F32) + extra
        a, b = sums
        return a + jnp.sum(grad * hat, axis=0, keepdims=True), b + jnp.sum(grad, axis=0, keepdims=True)

    def as_columns(sums, at):
        rows = jnp.concatenate([*sums, jnp.zeros((126, D), F32)], axis=0)
        gwide[:, :, :, pl.ds(at, 128)] = rows.T.astype(BF).reshape(4, 4, 48, 128)

    nothing = jnp.zeros((1, D), F32)
    as_columns(lax.fori_loop(0, T // ROW, norm2_back, (nothing, nothing)), N2_AT)
    n2[...] = hidden[...].astype(BF)

    serve()

    def o_back(i):
        at = ds(i, 256)
        b = n2[:, at]
        gwide[:, :, :, pl.ds(mult(O_AT + 256 * i, 128), 256)] = (
            dot(mixt[...].reshape(D, T), b).astype(BF).reshape(4, 4, 48, 256)
        )

    loop(3, o_back)
    serve()
    mgrad = n1
    mgrad[...] = dot_nt(n2[...], weight(wide, O_AT, D)).astype(BF)
    serve()

    def attend_back(t):
        q4, k4, v4 = [group(qkv, i, t) for i in range(3)]
        do4, o4 = group(mgrad, 0, t, 128), group(mixed, 0, t, 128)
        q4t, do4t = q4.T, do4.T
        kh = [k4 * heads[h] for h in range(4)]
        dk, dv = [], []
        total = [jnp.zeros((128, 128), F32)] * 2
        for h in range(4):
            hrows = slice(32 * h, 32 * h + 32)
            dkh, dvh = [], []
            for rb in range(2):
                rows, nk = slice(128 * rb, 128 * rb + 128), 128 * rb + 128
                dob = do4[rows] * heads[h]
                dot_row = jnp.sum(dob.astype(F32) * o4[rows].astype(F32), axis=1, keepdims=True)
                p = probs[4 * t + h, rows, :nk]
                sg = (p.astype(F32) * (dot_nt(dob, v4[:nk]) - dot_row)).astype(BF)
                total[rb] = total[rb] + dot(sg, kh[h][:nk])
                dkh.append(dot(q4t[hrows, rows], sg))
                dvh.append(dot(do4t[hrows, rows], p))
            for both, parts in ((dk, dkh), (dv, dvh)):
                both.append(jnp.concatenate([parts[1][:, :128] + parts[0], parts[1][:, 128:]], axis=1))
        at = 384 * t
        for rb in range(2):
            dqkv[pl.ds(128 * rb, 128), pl.ds(at, 128)] = (total[rb] * SCALE).astype(BF)
        dqkv[:, pl.ds(at + 128, 128)] = (jnp.concatenate(dk, axis=0).T * SCALE).astype(BF)
        dqkv[:, pl.ds(at + 256, 128)] = jnp.concatenate(dv, axis=0).T.astype(BF)

    for s in range(3):
        for half in range(2):
            attend_back(3 * half + s)
            serve()
        for half in range(2):
            part = dqkv[:, pl.ds(384 * (3 * half + s), 384)]
            gwide[:, :, :, pl.ds(set_at(half, s), 384)] = dot(n1t[...], part).astype(BF).reshape(4, 4, 48, 384)
        serve()
        for half in range(2):
            part = dqkv[:, pl.ds(384 * (3 * half + s), 384)]
            grad = dot_nt(part, weight(wide, set_at(half, s), 384))
            acc_in[...] = grad if s + half == 0 else acc_in[...] + grad
        if s < 2:
            serve()

    def norm1_back(i, sums):
        at = ds(i, ROW)
        grad, hat = acc_in[at, :], xhat[at, :]
        extra = norm_back(grad, hat, rstd1[at, :], rows1[0:1, :], at)
        ig_ref[at, :] = hidden[at, :] + extra
        a, b = sums
        return a + jnp.sum(grad * hat, axis=0, keepdims=True), b + jnp.sum(grad, axis=0, keepdims=True)

    as_columns(lax.fori_loop(0, T // ROW, norm1_back, (nothing, nothing)), N1_AT)
    ig_copy = pltpu.make_async_copy(ig_ref, ig_hbm, io.at[3])
    ig_copy.start()
    serve()

    assert conductor.place == len(SCHEDULE)
    out_copy.wait()
    ig_copy.wait()
    wire.drain()

    for k, ref in enumerate((dq_ref, dk_ref, dv_ref)):
        for i in range(6):
            ref[:, pl.ds(128 * i, 128)] = final[:12, pl.ds(set_at(i // 3, i % 3) + 128 * k, 128)]
    do_ref[...] = final[:12, pl.ds(O_AT, D)]
    for i in range(4):
        du_ref[:, pl.ds(768 * i, 768)] = final[:12, pl.ds(up_at(i), 768)]
    diag = lax.broadcasted_iota(jnp.int32, (16, 128), 0) == lax.broadcasted_iota(jnp.int32, (16, 128), 1)
    for at, refs in ((N1_AT, (dn1g_ref, dn1b_ref)), (N2_AT, (dn2g_ref, dn2b_ref))):
        for k, ref in enumerate(refs):
            col = final[:, at + k : at + k + 1]
            ref[...] = jnp.sum(jnp.where(diag, col, 0.0), axis=0, keepdims=True)[:, :12]


def publish_kernel(*refs):
    n = len(refs) // 2
    for i in range(n):
        refs[n + i][...] = refs[i][...]


VM = pl.BlockSpec(memory_space=pltpu.VMEM)
ANY = pl.BlockSpec(memory_space=pl.ANY)


def per_device(*args):
    args = [a.reshape(1, 12) if a.ndim == 1 else a for a in args]
    like = jax.ShapeDtypeStruct
    vec, square = like((1, 12), F32), like((12, D), F32)
    scratch = [pltpu.VMEM(s, t) for g in REDUCED for s, t in reduce_shapes(g)]
    wide, down = pltpu.VMEM((4, 4, 48, WIDE), BF), pltpu.VMEM((4, 4, 2, 2, 48, D), BF)
    scratch += [wide, down, wide, down, pltpu.VMEM((16, WIDE), F32)]
    f32s, bfs = pltpu.VMEM((T, D), F32), pltpu.VMEM((T, D), BF)
    one, turned = pltpu.VMEM((T, 1), F32), pltpu.VMEM((D, T), BF)
    scratch += [pltpu.VMEM((T, T), F32), f32s, one, f32s, one]
    scratch += [bfs, turned, bfs, pltpu.VMEM((T, 3 * D), BF), bfs]
    scratch += [pltpu.VMEM((HEADS, T, T), BF), f32s]
    scratch += [pltpu.VMEM((T, FF), BF), pltpu.VMEM((T, FF), F32), f32s]
    scratch += [pltpu.VMEM((T, 3 * D), BF), pltpu.VMEM((8, D), F32), pltpu.VMEM((8, D), F32)]
    scratch += [bfs, bfs, bfs, f32s, pltpu.SemaphoreType.DMA((4,))]
    scratch += [pltpu.SemaphoreType.DMA((N_SEND,)), pltpu.SemaphoreType.DMA((N_RECV,))]
    outs = pl.pallas_call(
        layer_kernel,
        out_shape=(
            like((T, D), BF), like((T, D), F32), vec, vec, square, square, square, square, vec, vec,
            like((12, FF), F32), like((48, D), F32),
        ),
        in_specs=[ANY] + [VM] * 11 + [ANY],
        out_specs=(ANY, ANY) + (VM,) * 10,
        scratch_shapes=scratch,
        compiler_params=pltpu.CompilerParams(
            collective_id=0, has_side_effects=True, vmem_limit_bytes=VMEM_BYTES
        ),
        cost_estimate=pl.CostEstimate(flops=13 * 10**9, bytes_accessed=6 * 10**6, transcendentals=3 * 10**6),
        name="layer",
    )(*args)
    outs = pl.pallas_call(
        publish_kernel,
        out_shape=tuple(like(o.shape, o.dtype) for o in outs),
        in_specs=[VM] * 12,
        out_specs=(VM,) * 12,
        name="publish",
    )(*outs)
    return tuple(o.reshape(12) if o.shape == (1, 12) else o for o in outs)


def solution(mesh):
    placed = (
        P(("fsdp", "rep"), None),
        P(("fsdp", "rep"), None),
        P("fsdp"),
        P("fsdp"),
        P("fsdp", None),
        P("fsdp", None),
        P("fsdp", None),
        P("fsdp", None),
        P("fsdp"),
        P("fsdp"),
        P("fsdp", None),
        P("fsdp", None),
        P(("fsdp", "rep"), None),
    )
    return jax.shard_map(
        per_device,
        mesh=mesh,
        in_specs=placed,
        out_specs=(
            P(("fsdp", "rep"), None),
            P(("fsdp", "rep"), None),
            P("fsdp"),
            P("fsdp"),
            P("fsdp", None),
            P("fsdp", None),
            P("fsdp", None),
            P("fsdp", None),
            P("fsdp"),
            P("fsdp"),
            P("fsdp", None),
            P("fsdp", None),
        ),
        check_vma=False,
    )
```

```python
import functools

import jax
import jax.numpy as jnp
from jax import lax
from jax.experimental import pallas as pl
from jax.experimental.pallas import tpu as pltpu
from jax.sharding import PartitionSpec as P

HEADS = 24
HEAD_DIM = 32
D = 768
FF = 3072
BF = jnp.bfloat16
F32 = jnp.float32
MESH = pl.DeviceIdType.MESH

WIDE = 6400
DOWN = 2, 4
START = (0, 2560, 0, 0, 0, 768, 2560, 4096)
HALF = (1280, 1920, 0, 1280, 0, 1280, 768, 1152)
WIDTH = (1280, 1920, 768, 768, 768, 512, 768, 1152)
P_AT = (768, 0, 0, 0, 0, 0, 0, 0)
Q_AT = (0, 384, 384, 256, 256, 256, 384, 640)
SIZE = ((512, 384), (384, 768), (384, 384), (256, 256), (256, 256), (256, 256), (384, 384), (640, 512))
LOW = ((256, 256), (128, 384), (128, 256), (128, 128), (128, 128), (128, 128), (128, 256), (256, 256))
ZED = (True, True, False, True, True, False, False, False)
STRAIGHT = (False, False, False)
SPLIT = (False, False, False, False, False, False, False, False)
FINE = (0, 0, 0)
DIRECT = (False, False, False, False, False, True, True, False)
P_, QM, QO = 0, 1, 2
N_RECV = 323
N_SEND = 40
VMEM_BYTES = 66700000


class Place:
    def __init__(self):
        f = lax.axis_index("fsdp")
        r = lax.axis_index("rep")
        c = lax.rem(f, 2)
        zl = lax.rem(lax.div(f, 2), 2)
        y = lax.rem(lax.div(f, 4), 4)
        x = lax.div(f, 16)
        self.r, self.c, self.zl, self.y, self.x = r, c, zl, y, x
        self.xs = {d: lax.rem(x + (d + 4), 4) if d else x for d in (-1, 0, 1, 2)}
        self.ys = {d: lax.rem(y + (d + 4), 4) if d else y for d in (-1, 0, 1, 2)}
        low = zl * 2 + c
        self.dx = {d: {"fsdp": self.xs[d] * 16 + y * 4 + low, "rep": r} for d in (-1, 1, 2)}
        self.dy = {d: {"fsdp": x * 16 + self.ys[d] * 4 + low, "rep": r} for d in (-1, 1, 2)}
        turned = f + 2 - 4 * zl
        self.sibling = {"fsdp": f + 1 - 2 * c, "rep": r}
        self.other = {"fsdp": f, "rep": 1 - r}
        self.above = {"fsdp": turned, "rep": lax.rem(r + zl, 2)}
        self.below = {"fsdp": turned, "rep": lax.rem(r + 1 - zl, 2)}
        self.share_to = {"fsdp": turned, "rep": lax.rem(r + zl * (1 - c) + (1 - zl) * c, 2)}
        self.peers = [self.sibling, self.above, self.below, self.other, *self.dx.values(), *self.dy.values()]
        self.starts = {}
        for g in range(len(START)):
            for core, cc in ((0, c), (1, 1 - c)):
                base = START[g] + cc * HALF[g]
                self.starts[g, None, core] = base
                q = base + Q_AT[g]
                self.starts[g, P_, core] = base + P_AT[g]
                self.starts[g, QM, core] = q + zl * SIZE[g][1] if ZED[g] else q
                self.starts[g, QO, core] = q + (1 - zl) * SIZE[g][1]


class Wire:
    def __init__(self, place, send, recv):
        self.place, self.send_sem, self.recv_sem = place, send, recv
        self.n = self.m = 0
        self.open = {}

    def slot(self):
        k = self.m % N_SEND
        self.m += 1
        if k in self.open:
            self.open.pop(k).wait_send()
        return k

    def put(self, src, dst, to):
        k = self.slot()
        assert self.n < N_RECV
        copy = pltpu.make_async_remote_copy(
            src_ref=src,
            dst_ref=dst,
            send_sem=self.send_sem.at[k],
            recv_sem=self.recv_sem.at[self.n],
            device_id=to,
            device_id_type=MESH,
        )
        copy.start()
        self.open[k] = copy
        self.n += 1
        return copy

    def drain(self):
        for copy in self.open.values():
            copy.wait_send()
        self.open = {}


def call_out(place):
    barrier = pltpu.get_barrier_semaphore()
    for peer in place.peers:
        pl.semaphore_signal(barrier, inc=1, device_id=peer, device_id_type=MESH)
    return barrier


def kind(k):
    return 0 if k == P_ else 1


def halves(g, k):
    n, low = SIZE[g][kind(k)], LOW[g][kind(k)]
    return pl.ds(0, low), pl.ds(low, n - low)


def columns_of(g, k, me, h=None, core=0):
    n, low = SIZE[g][kind(k)], LOW[g][kind(k)]
    off, width = (0, n) if h is None else ((0, low) if h == 0 else (low, n - low))
    base = me.starts[g, k, core]
    return pl.ds(pl.multiple_of(base + off if off else base, 128), width)


class Piece:
    def __init__(self, me, wide, down, g, k):
        self.me, self.wide, self.down, self.g, self.k = me, wide, down, g, k
        self.us, self.ws = (me.xs, me.ys) if k == P_ else (me.ys, me.xs)
        self.first, self.second = (me.dx, me.dy) if k == P_ else (me.dy, me.dx)

    def ref(self, bu, bw, h=None, core=0):
        bx, by = (bu, bw) if self.k == P_ else (bw, bu)
        at = columns_of(self.g, self.k, self.me, h, core)
        if self.g not in DOWN:
            return self.wide.at[bx, by, :, at]
        return self.down.at[bx, by, :, 1 - self.me.c if core else self.me.c, :, at]

    def at(self, du, dw, h=None):
        return self.ref(self.us[du], self.ws[dw], h)

    def across(self, dw, h=None):
        return self.ref(slice(None), self.ws[dw], h)

    def along(self, du, h=None):
        return self.ref(self.us[du], slice(None), h)

    def of_sibling(self):
        return self.ref(slice(None), slice(None), core=1)


def wait(*copies):
    yield copies
    for copy in copies:
        copy.wait_recv()


def gather_plane(wire, wide, down, g, k, sib, zs):
    me = wire.place
    s = Piece(me, wide, down, g, k)

    def go(ref, to):
        return wire.put(ref, ref, to)

    def share(name, *where):
        if k == QM and ZED[g]:
            lo, hi = [getattr(s, name)(*where, h) for h in range(2)]
            zs.append(((go(lo, me.above), go(hi, me.below)), name, where))
        sib.append(go(getattr(s, name)(*where), me.sibling))

    out = {}

    def spread(du):
        for d in reach:
            out[d, du] = go(s.at(du, 0), s.second[d])

    if not STRAIGHT[g]:
        reach = (1, -1)
        a, b = go(s.at(0, 0), s.first[1]), go(s.at(0, 0), s.first[-1])
        spread(0)
        yield from wait(a)
        a = go(s.at(-1, 0, 0), s.first[1])
        spread(-1)
        share("at", -1, 0)
        yield from wait(b)
        b = go(s.at(1, 0, 1), s.first[-1])
        spread(1)
        share("at", 1, 0)
        yield from wait(a, b)
        spread(2)
        share("at", 2, 0)
        if FINE[g] == 2 or (FINE[g] == 1 and k == QM):
            far = []
            for du in (0, -1, 1, 2):
                yield from wait(out[1, du])
                a = go(s.at(du, -1, 0), s.second[1])
                share("at", du, -1)
                yield from wait(out[-1, du])
                b = go(s.at(du, 1, 1), s.second[-1])
                share("at", du, 1)
                far.append((a, b))
            for du, copies in zip((0, -1, 1, 2), far):
                yield from wait(*copies)
                share("at", du, 2)
            return
        yield from wait(*[out[1, du] for du in (0, -1, 1, 2)])
        a = go(s.across(-1, 0), s.second[1])
        share("across", -1)
        yield from wait(*[out[-1, du] for du in (0, -1, 1, 2)])
        b = go(s.across(1, 1), s.second[-1])
        share("across", 1)
        yield from wait(a, b)
        share("across", 2)
        return
    reach = (1, -1, 2)
    near = {d: go(s.at(0, 0), s.first[d]) for d in reach}
    spread(0)
    for d in (1, -1, 2):
        du = -d if d < 2 else 2
        yield from wait(near[d])
        spread(du)
        share("at", du, 0)
    for d in (1, -1, 2):
        dw = -d if d < 2 else 2
        yield from wait(*[out[d, du] for du in (0, -1, 1, 2)])
        share("across", dw)


def gather_cross(wire, wide, down, g, sib, zs):
    me = wire.place
    theirs = Piece(me, wide, down, g, QO)
    for n in range(15 if FINE[g] else 6):
        yield lambda: zs[n][0] if len(zs) > n else None
        copies, name, where = zs[n]
        for copy in copies:
            copy.wait_recv()
        ref = getattr(theirs, name)(*where)
        sib.append(wire.put(ref, ref, me.sibling))


def gather_end(n, sib):
    for i in range(n):
        yield lambda: (sib[i],) if len(sib) > i else None
        sib[i].wait_recv()


def gather_streams(wire, wide, down, g):
    sib, zs = {P_: [], QM: [], QO: []}, []
    streams = [gather_plane(wire, wide, down, g, k, sib[k], zs) for k in (P_, QM)]
    fine = {P_: FINE[g] == 2, QM: FINE[g] > 0}
    streams += [gather_end(15 if fine[k] else 6, sib[k]) for k in (P_, QM)]
    if ZED[g]:
        streams += [gather_cross(wire, wide, down, g, sib[QO], zs), gather_end(15 if FINE[g] else 6, sib[QO])]
    return streams


def join(stage, wide, me, g):
    step = 640

    def body(i, carry):
        at = pl.ds(pl.multiple_of(START[g] + i * step, 128), step)
        rows = [stage[o, :, at].astype(F32)[:12] for o in range(4)]
        wide[me.x, me.y, :, at] = jnp.concatenate(rows, axis=0).astype(BF)
        return carry

    lax.fori_loop(0, 2 * HALF[g] // step, body, 0)


def gather_front(wire, own_down, stage, wide, down, g):
    me = wire.place
    mine = 2 * me.zl + me.c
    if g not in DOWN:
        at = pl.ds(START[g], 2 * HALF[g])
        src = dst = stage.at[mine, :, at]
        hers = stage.at[2 * (1 - me.zl) + me.c, :, at]
    else:
        src, dst = own_down, down.at[me.x, me.y, me.zl, me.c]
        hers = down.at[me.x, me.y, 1 - me.zl, me.c]
        down[me.x, me.y, me.zl, me.c] = own_down[...]
    a = wire.put(src, dst, me.share_to)
    b = wire.put(src, dst, me.sibling)
    yield from wait(a)
    c = wire.put(hers, hers, me.sibling)
    yield from wait(b, c)
    if g not in DOWN:
        join(stage, wide, me, g)


def rows_of(g):
    return (2, 48) if g in DOWN else (48,)


REDUCED = (3, 4, 5, 6, 7)


def reduce_shapes(g):
    rows, shapes = rows_of(g), []
    for k in (P_, QM):
        n, low = SIZE[g][kind(k)], LOW[g][kind(k)]
        high = n - low
        if DIRECT[g]:
            low, high = n, 128
        own = (48,) if g in DOWN else (2, 16)
        shapes += [(4, 4, *rows, n), (4, *rows, low), (4, *rows, high), (4, *rows, n), (4, *rows, n)]
        shapes += [(*rows, low), (*rows, high), (*rows, n), (*rows, n), (2, *own, n), (*own, n), (*own, n), (*own, n)]
    if ZED[g]:
        shapes += [(4, 4, *rows, SIZE[g][1])] * 2
    shapes = [(s, BF) for s in shapes]
    return shapes if g in DOWN else shapes + [((16, WIDTH[g]), F32)]


def add_blocks(dst, src):
    def body(i, carry):
        ref = dst(i)
        ref[...] = ref[...] + src(i)[...]
        return carry

    lax.fori_loop(0, 4, body, 0)


def add_one(ref, a):
    ref[...] = ref[...] + a[...]


def add_two(ref, a, b):
    ref[...] = (ref[...].astype(F32) + a[...].astype(F32) + b[...].astype(F32)).astype(BF)


def add_three(ref, a, b, c):
    total = ref[...].astype(F32) + a[...].astype(F32) + (b[...].astype(F32) + c[...].astype(F32))
    ref[...] = total.astype(BF)


def owners_rows(st, ref, others, g):
    total = ref[...].astype(F32)
    for other in others:
        total = total + other[...].astype(F32)
    if g not in DOWN:
        zero = jnp.zeros((4, total.shape[1]), F32)
        for o in range(4):
            st[o // 2, o % 2] = jnp.concatenate([total[12 * o : 12 * o + 12], zero], axis=0).astype(BF)
    else:
        st[...] = total.astype(BF)


def add_planes(me, g, k, st, rzp, rzm, rr, final, final_down, so):
    def total_of(core):
        def pick(ref):
            return (ref[...] if g in DOWN else ref[core]).astype(F32)

        first = pick(st.at[me.zl]) + pick(rr)
        second = pick(rzp) + pick(rzm)
        if k == QM and ZED[g]:
            return (QM, first), (QO, second)
        return ((k, first + second),)

    out = final_down if g in DOWN else final
    for kk, v in total_of(me.c):
        out[:, columns_of(g, kk, me)] = v
    if g not in DOWN:
        for kk, v in total_of(1 - me.c):
            base = me.starts[g, kk, 0] - me.starts[g, None, 0]
            so[:, pl.ds(pl.multiple_of(base, 128), v.shape[1])] = v


def reduce_plane(wire, wide, down, bufs, got, z_in, done, finals, g, k):
    me = wire.place
    s = Piece(me, wide, down, g, k)
    sb, b1p, b1m, b2p, b2m, c1p, c1m, c2p, c2m, st, rzp, rzm, rr = bufs[13 * k : 13 * k + 13]
    lo, hi = halves(g, k)
    any_lo, any_hi = (..., lo), (..., hi)
    crosses = k == QM and ZED[g]

    def add_along(du, buf):
        bu = s.us[du]
        add_blocks(lambda i: s.ref(bu, i), lambda i: buf.at[bu, i] if k == P_ else buf.at[i, bu])

    def add_half(du, h, buf):
        bu = s.us[du]
        add_blocks(lambda i: s.ref(bu, i, h), lambda i: buf.at[i])

    def ready(du):
        if crosses:
            yield lambda: z_in.get(du)
            for copy in z_in[du]:
                copy.wait_recv()
            add_along(du, bufs[27])
        else:
            if len(got) > 1:
                yield from wait(got[du])
            add_along(du, sb)

    if crosses or len(got) == 1:
        yield from wait(*got.values())
    if crosses:
        for du in (2, 1, -1, 0):
            add_along(du, sb)
    if DIRECT[g]:
        near = []
        for du, buf in ((2, b1p), (1, b2p), (-1, b2m)):
            yield from ready(du)
            near.append(wire.put(s.along(du), buf, s.first[du]))
        yield from ready(0)
        yield from wait(*near)
        near = []
        for dw, buf in ((2, c1p), (1, c2p), (-1, c2m), (0, None)):
            bw = s.ws[dw]
            add_three(s.at(0, dw), b1p.at[bw], b2p.at[bw], b2m.at[bw])
            if dw:
                near.append(wire.put(s.at(0, dw), buf, s.second[dw]))
        yield from wait(*near)
        owners_rows(st, s.at(0, 0), (c1p, c2p, c2m), g)
        yield from over_planes(wire, me, g, k, bufs, st, rzp, rzm, rr, finals, done)
        return
    yield from ready(2)
    r1p = wire.put(s.along(2, 0), b1p, s.first[1])
    r1m = wire.put(s.along(2, 1), b1m, s.first[-1])
    yield from ready(1)
    r2p_hi = wire.put(s.along(1, 1), b2p.at[any_hi], s.first[1])
    yield from ready(-1)
    r2m_lo = wire.put(s.along(-1, 0), b2m.at[any_lo], s.first[-1])
    yield from ready(0)
    yield from wait(r1p)
    add_half(1, 0, b1p)
    r2p_lo = wire.put(s.along(1, 0), b2p.at[any_lo], s.first[1])
    yield from wait(r1m)
    add_half(-1, 1, b1m)
    r2m_hi = wire.put(s.along(-1, 1), b2m.at[any_hi], s.first[-1])
    yield from wait(r2p_hi, r2m_lo, r2p_lo, r2m_hi)

    def close(dw):
        add_two(s.at(0, dw), b2p.at[s.ws[dw]], b2m.at[s.ws[dw]])

    close(2)
    r1p = wire.put(s.at(0, 2, 0), c1p, s.second[1])
    r1m = wire.put(s.at(0, 2, 1), c1m, s.second[-1])
    close(1)
    r2p_hi = wire.put(s.at(0, 1, 1), c2p.at[any_hi], s.second[1])
    close(-1)
    r2m_lo = wire.put(s.at(0, -1, 0), c2m.at[any_lo], s.second[-1])
    close(0)
    yield from wait(r1p)
    add_one(s.at(0, 1, 0), c1p)
    r2p_lo = wire.put(s.at(0, 1, 0), c2p.at[any_lo], s.second[1])
    yield from wait(r1m)
    add_one(s.at(0, -1, 1), c1m)
    r2m_hi = wire.put(s.at(0, -1, 1), c2m.at[any_hi], s.second[-1])
    yield from wait(r2p_hi, r2m_lo, r2p_lo, r2m_hi)
    owners_rows(st, s.at(0, 0), (c2p, c2m), g)
    yield from over_planes(wire, me, g, k, bufs, st, rzp, rzm, rr, finals, done)


def over_planes(wire, me, g, k, bufs, st, rzp, rzm, rr, finals, done):
    a = wire.put(st.at[1 - me.zl], rzp, me.above)
    b = wire.put(st.at[1 - me.zl], rzm, me.below)
    c = wire.put(st.at[me.zl], rr, me.other)
    yield from wait(a, b, c)
    add_planes(me, g, k, st, rzp, rzm, rr, *finals, None if g in DOWN else bufs[-1])
    done.append(k)
    if g not in DOWN and len(done) == 2:
        at = pl.ds(pl.multiple_of(me.starts[g, None, 0], 128), WIDTH[g])
        yield from wait(wire.put(bufs[-1], finals[0].at[:, at], me.sibling))


def reduce_cross(wire, wide, down, bufs, got, z_in, g):
    me = wire.place
    theirs = Piece(me, wide, down, g, QO)
    lo, hi = halves(g, QO)
    yield from wait(got)
    for du in (2, 1, -1, 0):
        bu = theirs.us[du]
        add_blocks(lambda i: theirs.ref(bu, i), lambda i: bufs[26].at[i, bu])
        a = wire.put(theirs.along(du, 0), bufs[27].at[:, bu, ..., lo], me.below)
        b = wire.put(theirs.along(du, 1), bufs[27].at[:, bu, ..., hi], me.above)
        z_in[du] = a, b
        if du:
            yield None


def reduce_streams(wire, wide, down, bufs, finals, g):
    me = wire.place
    pieces = {k: Piece(me, wide, down, g, k) for k in (P_, QM, QO)}
    z_in, done, streams = {}, [], []
    if ZED[g]:
        got = wire.put(pieces[QO].of_sibling(), bufs[26], me.sibling)
        streams.append(reduce_cross(wire, wide, down, bufs, got, z_in, g))
    for k in (P_, QM):
        s, sb = pieces[k], bufs[13 * k]
        if SPLIT[g]:
            got = {}
            for du in (2, 1, -1, 0):
                bu = s.us[du]
                dst = sb.at[bu] if k == P_ else sb.at[:, bu]
                got[du] = wire.put(s.ref(s.us[du], slice(None), core=1), dst, me.sibling)
        else:
            got = {0: wire.put(s.of_sibling(), sb, me.sibling)}
        streams.append(reduce_plane(wire, wide, down, bufs, got, z_in, done, finals, g, k))
    return streams


class Conductor:
    def __init__(self, openers):
        self.openers = openers
        self.streams = {}
        self.place = 0

    def serve(self):
        for key, i in SCHEDULE[self.place]:
            if i < 0:
                self.streams.update({(key, k): s for k, s in enumerate(self.openers[key]())})
                for k in self.streams:
                    if k[0] == key:
                        next(self.streams[k])
            else:
                next(self.streams[key, i], None)
        self.place += 1


SCHEDULE = (
    ((5, -1),),
    (),
    ((6, -1), (7, -1),),
    ((5, 0), (6, 0), (5, 0), (0, -1), (7, 0), (6, 0), (7, 0), (0, 0), (0, 0), (0, 1), (0, 1), (0, 2), (0, 2), (0, 0),
     (1, -1), (0, 3), (0, 3), (0, 4), (0, 4), (0, 2), (0, 1), (1, 0), (0, 5), (1, 0), (0, 0), (0, 0), (0, 5), (0, 3),
     (0, 4), (1, 2), (1, 2), (0, 1), (0, 1), (0, 2), (1, 1), (1, 1), (1, 0), (0, 2), (0, 5), (0, 3), (0, 3), (1, 3),
     (1, 3), (1, 2), (0, 1), (0, 4), (0, 0), (1, 1), (1, 0), (1, 0), (0, 4), (0, 3), (0, 5), (0, 2), (2, -1), (1, 4),),
    ((1, 2), (1, 2), (1, 3), (1, 4),),
    ((0, 5), (1, 1), (1, 1), (1, 5),),
    ((0, 4), (1, 0),),
    (),
    ((1, 4), (1, 5), (2, 0), (2, 0),),
    ((1, 3),),
    ((1, 3), (2, 1), (0, 5),),
    (),
    ((1, 2), (1, 5), (2, 1), (2, 2), (2, 2),),
    ((1, 4),),
    ((2, 3),),
    ((1, 1), (2, 0), (2, 3), (1, 5), (2, 1), (1, 4), (1, 3), (2, 2), (2, 3), (2, 0), (2, 0), (1, 5), (2, 1), (2, 1),
     (1, 4), (2, 2), (2, 2), (2, 3), (2, 3), (1, 5),),
    ((2, 0), (2, 1),),
    (),
    (),
    (),
    (),
    (),
    (),
    (),
    ((2, 2),),
    ((14, -1), (2, 3),),
    (),
    (),
    (),
    ((14, 0), (14, 0), (14, 0), (14, 0),),
    (),
    ((16, -1), (14, 1),),
    ((14, 2),),
    ((14, 2),),
    ((16, 0),),
    ((16, 1), (14, 1), (14, 1), (14, 2),),
    (),
    ((14, 2),),
    (),
    ((17, -1),),
    (),
    ((14, 2), (14, 2), (14, 2),),
    (),
    ((17, 0), (16, 0), (16, 1), (17, 1),),
    (),
    ((14, 1),),
    ((17, 0), (17, 0), (14, 2),),
    ((13, -1), (16, 0),),
    (),
    ((17, 1), (17, 1),),
    ((13, 0), (13, 0), (13, 0), (13, 0), (13, 1), (13, 2), (16, 0), (16, 1), (17, 0), (14, 1), (14, 1), (14, 2),
     (14, 2),),
    ((13, 2),),
    ((15, -1), (13, 1), (13, 1), (13, 2), (17, 0), (17, 0), (17, 1), (13, 2), (14, 2), (14, 1), (13, 2), (13, 2),
     (13, 2), (15, 0), (13, 1), (15, 1), (17, 1), (17, 1), (16, 1), (17, 0), (14, 2), (13, 2), (13, 1), (13, 1),
     (14, 1), (16, 1), (17, 0), (15, 0), (17, 1), (13, 2), (13, 2), (15, 1), (13, 1), (13, 2), (15, 0), (15, 1),
     (17, 1), (13, 1), (13, 2), (17, 1), (15, 0), (15, 1), (13, 2), (15, 1),),
)


def dot(a, b):
    return lax.dot_general(a, b, (((1,), (0,)), ((), ())), preferred_element_type=F32)


def dot_nt(a, b):
    return lax.dot_general(a, b, (((1,), (1,)), ((), ())), preferred_element_type=F32)


def loop(n, body):
    if n <= UNROLLED:
        for i in range(n):
            body(i)
        return

    def step(i, carry):
        body(i)
        return carry

    lax.fori_loop(0, n, step, 0)


def mult(v, n):
    return v if isinstance(v, int) else pl.multiple_of(v, n)


def ds(i, n):
    return pl.ds(mult(i * n, n), n)


UNROLLED = 3
T = 256
SCALE = HEAD_DIM ** (-0.5)
O_AT, N1_AT, N2_AT = 4096, 1152, 2432


def set_at(half, s):
    return 1280 * half + 384 * s


def up_at(i):
    return 2560 + 768 * i + (768 if i > 1 else 0)


ROW = 64


def standardise(v):
    centre = jnp.mean(v, axis=-1, keepdims=True)
    centred = v - centre
    spread = jnp.mean(centred * centred, axis=-1, keepdims=True)
    rstd = lax.rsqrt(spread + 1e-05)
    return centred * rstd, rstd


def weight(wide, at, width):
    return wide[:, :, :, pl.ds(at, width)].reshape(D, width)


def layer_kernel(
    x_hbm, seg_ref, n1g_ref, n1b_ref, wq_ref, wk_ref, wv_ref, wo_ref, n2g_ref, n2b_ref, wu_ref, wd_ref, cot_hbm,
    out_hbm, ig_hbm, dn1g_ref, dn1b_ref, dq_ref, dk_ref, dv_ref, do_ref, dn2g_ref, dn2b_ref, du_ref, dd_ref,
    *scratch,
):
    bufs = {}
    for g in REDUCED:
        n = len(reduce_shapes(g))
        bufs[g], scratch = scratch[:n], scratch[n:]
    (
        wide, down, gwide, gdown, final,
        mask, xhat, rstd1, xhat2, rstd2, n1, n1t, n2, qkv, mixed, probs, hidden,
        act, slope, acc_in, dqkv, rows1, rows2, x_ref, cot_ref, out_ref, ig_ref, io, send, recv,
    ) = scratch
    stage = gwide.at[0, :, pl.ds(0, 16)]
    acc_out = ig_ref
    place = me = Place()
    x_in = pltpu.make_async_copy(x_hbm, x_ref, io.at[0])
    cot_in = pltpu.make_async_copy(cot_hbm, cot_ref, io.at[1])
    x_in.start()
    cot_in.start()
    barrier = call_out(place)
    wire = Wire(place, send, recv)
    openers = {g: lambda g=g: gather_streams(wire, wide, down, g) for g in range(3)}
    openers.update({5 + g: lambda g=g: [gather_front(wire, wd_ref, stage, wide, down, g)] for g in range(3)})
    finals = final, dd_ref
    openers.update({10 + g: lambda g=g: reduce_streams(wire, gwide, gdown, bufs[g], finals, g) for g in REDUCED})
    conductor = Conductor(openers)
    serve = conductor.serve
    mine = 2 * me.zl + me.c

    zero4 = lambda n: jnp.zeros((4, n), F32)

    def put_own(ref, width, place_of):
        for i in range(ref.shape[1] // width):
            rows = jnp.concatenate([ref[:, pl.ds(width * i, width)].astype(F32), zero4(width)], axis=0)
            stage[mine, :, pl.ds(place_of(i), width)] = rows.astype(BF)

    def put_norm(gain, shift, at):
        eye = lax.broadcasted_iota(jnp.int32, (16, 12), 0) == lax.broadcasted_iota(jnp.int32, (16, 12), 1)
        lane = lax.broadcasted_iota(jnp.int32, (16, 128), 1)
        a = jnp.sum(jnp.where(eye, gain[...].astype(F32), 0.0), axis=1, keepdims=True)
        b = jnp.sum(jnp.where(eye, shift[...].astype(F32), 0.0), axis=1, keepdims=True)
        both = jnp.where(lane == 0, a, jnp.where(lane == 1, b, 0.0))
        stage[mine, :, pl.ds(at, 128)] = both.astype(BF)

    for k, ref in enumerate((wq_ref, wk_ref, wv_ref)):
        put_own(ref, 128, lambda i: set_at(i // 3, i % 3) + 128 * k)
    put_norm(n1g_ref, n1b_ref, N1_AT)
    put_norm(n2g_ref, n2b_ref, N2_AT)
    pl.semaphore_wait(barrier, len(place.peers))
    serve()
    put_own(wo_ref, D, lambda i: O_AT)
    put_own(wu_ref, D, up_at)
    serve()

    segs = jnp.broadcast_to(seg_ref[...], (T, T))
    rows_iota = lax.broadcasted_iota(jnp.int32, (T, T), 0)
    cols_iota = lax.broadcasted_iota(jnp.int32, (T, T), 1)
    allowed = (rows_iota >= cols_iota) & (segs.astype(F32).T == segs.astype(F32))
    mask[...] = jnp.where(allowed, 0.0, -1e30)

    serve()

    def norm1_rows(i):
        at = ds(i, ROW)
        hat, rstd = standardise(x_ref[at, :].astype(F32))
        xhat[at, :] = hat
        rstd1[at, :] = rstd

    x_in.wait()
    loop(T // ROW, norm1_rows)
    serve()

    eye = (
        lax.broadcasted_iota(jnp.int32, (128, 128), 0) == lax.broadcasted_iota(jnp.int32, (128, 128), 1)
    ).astype(BF)
    rows1[...] = dot_nt(eye, weight(wide, N1_AT, 128))[:8]
    rows2[...] = dot_nt(eye, weight(wide, N2_AT, 128))[:8]

    def norm1_apply(i):
        at = ds(i, ROW)
        n1[at, :] = (xhat[at, :] * rows1[0:1, :] + rows1[1:2, :]).astype(BF)

    loop(T // ROW, norm1_apply)

    def project(half, s):
        w = wide[:, :, :, pl.ds(mult(set_at(half, s), 128), 384)].reshape(D, 384)
        qkv[:, pl.ds(mult(384 * (3 * half + s), 128), 384)] = dot(n1[...], w).astype(BF)

    lane = lax.broadcasted_iota(jnp.int32, (1, 128), 1)
    heads = [((lane >= 32 * h) & (lane < 32 * h + 32)).astype(F32).astype(BF) for h in range(4)]

    def group(ref, which, t, width=384):
        return ref[:, pl.ds(mult(width * t + 128 * which, 128), 128)]

    def attend(t):
        q4, k4, v4 = [group(qkv, i, t) for i in range(3)]
        vh = [v4 * heads[h] for h in range(4)]
        for rb in range(2):
            rows, nk = slice(128 * rb, 128 * rb + 128), 128 * rb + 128
            total = jnp.zeros((128, 128), F32)
            for h in range(4):
                s = dot_nt(q4[rows] * heads[h], k4[:nk]) * SCALE + mask[rows, :nk]
                e = jnp.exp(s - jnp.max(s, axis=1, keepdims=True))
                p = (e * (1.0 / jnp.sum(e, axis=1, keepdims=True))).astype(BF)
                probs[4 * t + h, rows, :nk] = p
                total = total + dot(p, vh[h][:nk])
            mixed[rows, pl.ds(mult(128 * t, 128), 128)] = total.astype(BF)

    for turn, s in enumerate((2, me.zl, 1 - me.zl)):
        if turn:
            serve()
        for half in range(2):
            project(half, s)
        serve()
        for half in range(2):
            attend(3 * half + s)
            serve()

    n2t, mixt = [gwide.at[:, :, :, pl.ds(256 * k, 256)] for k in range(2)]

    def transpose(src, dst):
        def body(i):
            dst[ds(i, 2)] = src[:, ds(i, 384)].T.reshape(2, 4, 48, T)

        loop(2, body)

    def turn_n1(i):
        n1t[ds(i, 384), :] = n1[:, ds(i, 384)].T

    transpose(mixed, mixt)
    loop(2, turn_n1)
    serve()

    def out_project(i):
        at = ds(i, 256)
        w = wide[:, :, :, pl.ds(mult(O_AT + 256 * i, 128), 256)].reshape(D, 256)
        hidden[:, at] = x_ref[:, at].astype(F32) + dot(mixed[...], w)

    loop(3, out_project)

    def norm2_rows(i):
        at = ds(i, ROW)
        hat, rstd = standardise(hidden[at, :])
        xhat2[at, :] = hat
        rstd2[at, :] = rstd
        n2[at, :] = (hat * rows2[0:1, :] + rows2[1:2, :]).astype(BF)

    loop(T // ROW, norm2_rows)
    transpose(n2, n2t)
    serve()

    cot_in.wait()
    c0 = (2.0 / 3.141592653589793) ** 0.5

    def feed(i):
        def part(j):
            at = pl.ds(up_at(i) + 256 * j, 256)
            v = dot(n2[...], wide[:, :, :, at].reshape(D, 256))
            sq = v * v
            th = jnp.tanh(c0 * v * (1.0 + 0.044715 * sq))
            half = 0.5 + 0.5 * th
            a = (v * half).astype(BF)
            keep = pl.ds(mult(768 * i + 256 * j, 128), 256)
            act[:, keep] = a
            slope[:, keep] = half + 0.5 * v * (1.0 - th * th) * (c0 * (1.0 + 0.134145 * sq))

        loop(3, part)
        serve()
        a = act[:, ds(i, 768)].T

        def grad(j):
            at = ds(j, 256)
            gdown[i, :, :, :, :, at] = dot(a, cot_ref[:, at]).astype(BF).reshape(4, 2, 2, 48, 256)

        loop(3, grad)

    for i in range(4):
        feed(i)
        serve()
    serve()

    acc_out[...] = hidden[...]
    acc_in[...] = jnp.zeros((T, D), F32)

    def feed_back(i):
        at = ds(i, 768)
        wd = down[i].reshape(768, 768)
        acc_out[...] += dot(act[:, at], wd)
        pg = (dot_nt(cot_ref[...], wd) * slope[:, at]).astype(BF)
        act[:, at] = pg
        serve()
        acc_in[...] += dot_nt(pg, weight(wide, up_at(i), D))
        serve()

        def grad(j):
            cols_j = pl.ds(up_at(i) + 256 * j, 256)
            pg_j = act[:, pl.ds(mult(768 * i + 256 * j, 128), 256)]
            gwide[:, :, :, cols_j] = dot(n2t[...].reshape(D, T), pg_j).astype(BF).reshape(4, 4, 48, 256)

        loop(3, grad)

    for i in range(4):
        feed_back(i)
        serve()
    out_ref[...] = acc_out[...].astype(BF)
    out_copy = pltpu.make_async_copy(out_ref, out_hbm, io.at[2])
    out_copy.start()

    def norm_back(grad, hat, rstd, gain, at):
        gn = gain * grad
        m1 = jnp.mean(gn, axis=-1, keepdims=True)
        m2 = jnp.mean(gn * hat, axis=-1, keepdims=True)
        return (gn - m1 - hat * m2) * rstd

    def norm2_back(i, sums):
        at = ds(i, ROW)
        grad, hat = acc_in[at, :], xhat2[at, :]
        extra = norm_back(grad, hat, rstd2[at, :], rows2[0:1, :], at)
        hidden[at, :] = cot_ref[at, :].astype(F32) + extra
        a, b = sums
        return a + jnp.sum(grad * hat, axis=0, keepdims=True), b + jnp.sum(grad, axis=0, keepdims=True)

    def as_columns(sums, at):
        rows = jnp.concatenate([*sums, jnp.zeros((126, D), F32)], axis=0)
        gwide[:, :, :, pl.ds(at, 128)] = rows.T.astype(BF).reshape(4, 4, 48, 128)

    nothing = jnp.zeros((1, D), F32)
    as_columns(lax.fori_loop(0, T // ROW, norm2_back, (nothing, nothing)), N2_AT)
    n2[...] = hidden[...].astype(BF)

    serve()

    def o_back(i):
        at = ds(i, 256)
        b = n2[:, at]
        gwide[:, :, :, pl.ds(mult(O_AT + 256 * i, 128), 256)] = (
            dot(mixt[...].reshape(D, T), b).astype(BF).reshape(4, 4, 48, 256)
        )

    loop(3, o_back)
    serve()
    mgrad = n1
    mgrad[...] = dot_nt(n2[...], weight(wide, O_AT, D)).astype(BF)
    serve()

    def attend_back(t):
        q4, k4, v4 = [group(qkv, i, t) for i in range(3)]
        do4, o4 = group(mgrad, 0, t, 128), group(mixed, 0, t, 128)
        q4t, do4t = q4.T, do4.T
        kh = [k4 * heads[h] for h in range(4)]
        dk, dv = [], []
        total = [jnp.zeros((128, 128), F32)] * 2
        for h in range(4):
            hrows = slice(32 * h, 32 * h + 32)
            dkh, dvh = [], []
            for rb in range(2):
                rows, nk = slice(128 * rb, 128 * rb + 128), 128 * rb + 128
                dob = do4[rows] * heads[h]
                dot_row = jnp.sum(dob.astype(F32) * o4[rows].astype(F32), axis=1, keepdims=True)
                p = probs[4 * t + h, rows, :nk]
                sg = (p.astype(F32) * (dot_nt(dob, v4[:nk]) - dot_row)).astype(BF)
                total[rb] = total[rb] + dot(sg, kh[h][:nk])
                dkh.append(dot(q4t[hrows, rows], sg))
                dvh.append(dot(do4t[hrows, rows], p))
            for both, parts in ((dk, dkh), (dv, dvh)):
                both.append(jnp.concatenate([parts[1][:, :128] + parts[0], parts[1][:, 128:]], axis=1))
        at = 384 * t
        for rb in range(2):
            dqkv[pl.ds(128 * rb, 128), pl.ds(at, 128)] = (total[rb] * SCALE).astype(BF)
        dqkv[:, pl.ds(at + 128, 128)] = (jnp.concatenate(dk, axis=0).T * SCALE).astype(BF)
        dqkv[:, pl.ds(at + 256, 128)] = jnp.concatenate(dv, axis=0).T.astype(BF)

    for s in range(3):
        for half in range(2):
            attend_back(3 * half + s)
            serve()
        for half in range(2):
            part = dqkv[:, pl.ds(384 * (3 * half + s), 384)]
            gwide[:, :, :, pl.ds(set_at(half, s), 384)] = dot(n1t[...], part).astype(BF).reshape(4, 4, 48, 384)
        serve()
        for half in range(2):
            part = dqkv[:, pl.ds(384 * (3 * half + s), 384)]
            grad = dot_nt(part, weight(wide, set_at(half, s), 384))
            acc_in[...] = grad if s + half == 0 else acc_in[...] + grad
        if s < 2:
            serve()

    def norm1_back(i, sums):
        at = ds(i, ROW)
        grad, hat = acc_in[at, :], xhat[at, :]
        extra = norm_back(grad, hat, rstd1[at, :], rows1[0:1, :], at)
        ig_ref[at, :] = hidden[at, :] + extra
        a, b = sums
        return a + jnp.sum(grad * hat, axis=0, keepdims=True), b + jnp.sum(grad, axis=0, keepdims=True)

    as_columns(lax.fori_loop(0, T // ROW, norm1_back, (nothing, nothing)), N1_AT)
    ig_copy = pltpu.make_async_copy(ig_ref, ig_hbm, io.at[3])
    ig_copy.start()
    serve()

    assert conductor.place == len(SCHEDULE)
    out_copy.wait()
    ig_copy.wait()
    wire.drain()

    for k, ref in enumerate((dq_ref, dk_ref, dv_ref)):
        for i in range(6):
            ref[:, pl.ds(128 * i, 128)] = final[:12, pl.ds(set_at(i // 3, i % 3) + 128 * k, 128)]
    do_ref[...] = final[:12, pl.ds(O_AT, D)]
    for i in range(4):
        du_ref[:, pl.ds(768 * i, 768)] = final[:12, pl.ds(up_at(i), 768)]
    diag = lax.broadcasted_iota(jnp.int32, (16, 128), 0) == lax.broadcasted_iota(jnp.int32, (16, 128), 1)
    for at, refs in ((N1_AT, (dn1g_ref, dn1b_ref)), (N2_AT, (dn2g_ref, dn2b_ref))):
        for k, ref in enumerate(refs):
            col = final[:, at + k : at + k + 1]
            ref[...] = jnp.sum(jnp.where(diag, col, 0.0), axis=0, keepdims=True)[:, :12]


def publish_kernel(*refs):
    n = len(refs) // 3
    sems = refs[-1]
    ins = [pltpu.make_async_copy(refs[i], refs[2 * n + i], sems.at[i]) for i in range(n)]
    outs = [pltpu.make_async_copy(refs[2 * n + i], refs[n + i], sems.at[n + i]) for i in range(n)]
    for copy in ins:
        copy.start()
    for come, go in zip(ins, outs):
        come.wait()
        go.start()
    for copy in outs:
        copy.wait()


VM = pl.BlockSpec(memory_space=pltpu.VMEM)
ANY = pl.BlockSpec(memory_space=pl.ANY)


def per_device(*args):
    args = [a.reshape(1, 12) if a.ndim == 1 else a for a in args]
    like = jax.ShapeDtypeStruct
    vec, square = like((1, 12), F32), like((12, D), F32)
    scratch = [pltpu.VMEM(s, t) for g in REDUCED for s, t in reduce_shapes(g)]
    wide, down = pltpu.VMEM((4, 4, 48, WIDE), BF), pltpu.VMEM((4, 4, 2, 2, 48, D), BF)
    scratch += [wide, down, wide, down, pltpu.VMEM((16, WIDE), F32)]
    f32s, bfs = pltpu.VMEM((T, D), F32), pltpu.VMEM((T, D), BF)
    one, turned = pltpu.VMEM((T, 1), F32), pltpu.VMEM((D, T), BF)
    scratch += [pltpu.VMEM((T, T), F32), f32s, one, f32s, one]
    scratch += [bfs, turned, bfs, pltpu.VMEM((T, 3 * D), BF), bfs]
    scratch += [pltpu.VMEM((HEADS, T, T), BF), f32s]
    scratch += [pltpu.VMEM((T, FF), BF), pltpu.VMEM((T, FF), F32), f32s]
    scratch += [pltpu.VMEM((T, 3 * D), BF), pltpu.VMEM((8, D), F32), pltpu.VMEM((8, D), F32)]
    scratch += [bfs, bfs, bfs, f32s, pltpu.SemaphoreType.DMA((4,))]
    scratch += [pltpu.SemaphoreType.DMA((N_SEND,)), pltpu.SemaphoreType.DMA((N_RECV,))]
    outs = pl.pallas_call(
        layer_kernel,
        out_shape=(
            like((T, D), BF), like((T, D), F32), vec, vec, square, square, square, square, vec, vec,
            like((12, FF), F32), like((48, D), F32),
        ),
        in_specs=[ANY] + [VM] * 11 + [ANY],
        out_specs=(ANY, ANY) + (VM,) * 10,
        scratch_shapes=scratch,
        compiler_params=pltpu.CompilerParams(
            collective_id=0, has_side_effects=True, vmem_limit_bytes=VMEM_BYTES
        ),
        cost_estimate=pl.CostEstimate(flops=13 * 10**9, bytes_accessed=6 * 10**6, transcendentals=3 * 10**6),
        name="layer",
    )(*args)
    outs = pl.pallas_call(
        publish_kernel,
        out_shape=tuple(like(o.shape, o.dtype) for o in outs),
        in_specs=[ANY] * 12,
        out_specs=(ANY,) * 12,
        scratch_shapes=[*[pltpu.VMEM(o.shape, o.dtype) for o in outs], pltpu.SemaphoreType.DMA((24,))],
        name="publish",
    )(*outs)
    return tuple(o.reshape(12) if o.shape == (1, 12) else o for o in outs)


def solution(mesh):
    placed = (
        P(("fsdp", "rep"), None),
        P(("fsdp", "rep"), None),
        P("fsdp"),
        P("fsdp"),
        P("fsdp", None),
        P("fsdp", None),
        P("fsdp", None),
        P("fsdp", None),
        P("fsdp"),
        P("fsdp"),
        P("fsdp", None),
        P("fsdp", None),
        P(("fsdp", "rep"), None),
    )
    return jax.shard_map(
        per_device,
        mesh=mesh,
        in_specs=placed,
        out_specs=(
            P(("fsdp", "rep"), None),
            P(("fsdp", "rep"), None),
            P("fsdp"),
            P("fsdp"),
            P("fsdp", None),
            P("fsdp", None),
            P("fsdp", None),
            P("fsdp", None),
            P("fsdp"),
            P("fsdp"),
            P("fsdp", None),
            P("fsdp", None),
        ),
        check_vma=False,
    )
```

```python
import functools

import jax
import jax.numpy as jnp
from jax import lax
from jax.experimental import pallas as pl
from jax.experimental.pallas import tpu as pltpu
from jax.sharding import PartitionSpec as P

HEADS = 24
HEAD_DIM = 32
D = 768
FF = 3072
BF = jnp.bfloat16
F32 = jnp.float32
MESH = pl.DeviceIdType.MESH

WIDE = 6400
DOWN = 2, 4
START = (0, 2560, 0, 0, 0, 768, 2560, 4096)
HALF = (1280, 1920, 0, 1280, 0, 1280, 768, 1152)
WIDTH = (1280, 1920, 768, 768, 768, 512, 768, 1152)
P_AT = (768, 0, 0, 0, 0, 0, 0, 0)
Q_AT = (0, 384, 384, 256, 256, 256, 384, 640)
SIZE = ((512, 384), (384, 768), (384, 384), (256, 256), (256, 256), (256, 256), (384, 384), (640, 512))
LOW = ((256, 256), (128, 384), (128, 256), (128, 128), (128, 128), (128, 128), (128, 256), (256, 256))
ZED = (True, True, False, True, True, False, False, False)
STRAIGHT = (False, False, False)
SPLIT = (False, False, False, False, False, False, False, False)
FINE = (0, 0, 0)
DIRECT = (False, False, False, False, False, True, True, False)
P_, QM, QO = 0, 1, 2
N_RECV = 256
N_SEND = 40
VMEM_BYTES = 66700000


class Place:
    def __init__(self):
        f = lax.axis_index("fsdp")
        r = lax.axis_index("rep")
        c = lax.rem(f, 2)
        zl = lax.rem(lax.div(f, 2), 2)
        y = lax.rem(lax.div(f, 4), 4)
        x = lax.div(f, 16)
        self.r, self.c, self.zl, self.y, self.x = r, c, zl, y, x
        self.xs = {d: lax.rem(x + (d + 4), 4) if d else x for d in (-1, 0, 1, 2)}
        self.ys = {d: lax.rem(y + (d + 4), 4) if d else y for d in (-1, 0, 1, 2)}
        low = zl * 2 + c
        self.dx = {d: {"fsdp": self.xs[d] * 16 + y * 4 + low, "rep": r} for d in (-1, 1, 2)}
        self.dy = {d: {"fsdp": x * 16 + self.ys[d] * 4 + low, "rep": r} for d in (-1, 1, 2)}
        turned = f + 2 - 4 * zl
        self.sibling = {"fsdp": f + 1 - 2 * c, "rep": r}
        self.other = {"fsdp": f, "rep": 1 - r}
        self.above = {"fsdp": turned, "rep": lax.rem(r + zl, 2)}
        self.below = {"fsdp": turned, "rep": lax.rem(r + 1 - zl, 2)}
        self.share_to = {"fsdp": turned, "rep": lax.rem(r + zl * (1 - c) + (1 - zl) * c, 2)}
        self.peers = [self.sibling, self.above, self.below, self.other, *self.dx.values(), *self.dy.values()]
        self.starts = {}
        for g in range(len(START)):
            for core, cc in ((0, c), (1, 1 - c)):
                base = START[g] + cc * HALF[g]
                self.starts[g, None, core] = base
                q = base + Q_AT[g]
                self.starts[g, P_, core] = base + P_AT[g]
                self.starts[g, QM, core] = q + zl * SIZE[g][1] if ZED[g] else q
                self.starts[g, QO, core] = q + (1 - zl) * SIZE[g][1]


class Wire:
    def __init__(self, place, send, recv):
        self.place, self.send_sem, self.recv_sem = place, send, recv
        self.n = self.m = 0
        self.open = {}
        self.key, self.spare = None, []

    def slot(self):
        k = self.m % N_SEND
        self.m += 1
        if k in self.open:
            self.open.pop(k).wait_send()
        return k

    def put(self, src, dst, to):
        k = self.slot()
        if self.key in (13, 15, 17) and self.spare:
            at = self.spare.pop(0)
        else:
            at = self.n
            self.n += 1
            if self.key in (0, 5, 6, 7):
                self.spare.append(at)
        assert at < N_RECV
        copy = pltpu.make_async_remote_copy(
            src_ref=src,
            dst_ref=dst,
            send_sem=self.send_sem.at[k],
            recv_sem=self.recv_sem.at[at],
            device_id=to,
            device_id_type=MESH,
        )
        copy.start()
        self.open[k] = copy
        return copy

    def drain(self):
        for copy in self.open.values():
            copy.wait_send()
        self.open = {}


def call_out(place):
    barrier = pltpu.get_barrier_semaphore()
    for peer in place.peers:
        pl.semaphore_signal(barrier, inc=1, device_id=peer, device_id_type=MESH)
    return barrier


def kind(k):
    return 0 if k == P_ else 1


def halves(g, k):
    n, low = SIZE[g][kind(k)], LOW[g][kind(k)]
    return pl.ds(0, low), pl.ds(low, n - low)


def columns_of(g, k, me, h=None, core=0):
    n, low = SIZE[g][kind(k)], LOW[g][kind(k)]
    off, width = (0, n) if h is None else ((0, low) if h == 0 else (low, n - low))
    base = me.starts[g, k, core]
    return pl.ds(pl.multiple_of(base + off if off else base, 128), width)


class Piece:
    def __init__(self, me, wide, down, g, k):
        self.me, self.wide, self.down, self.g, self.k = me, wide, down, g, k
        self.us, self.ws = (me.xs, me.ys) if k == P_ else (me.ys, me.xs)
        self.first, self.second = (me.dx, me.dy) if k == P_ else (me.dy, me.dx)

    def ref(self, bu, bw, h=None, core=0):
        bx, by = (bu, bw) if self.k == P_ else (bw, bu)
        at = columns_of(self.g, self.k, self.me, h, core)
        if self.g not in DOWN:
            return self.wide.at[bx, by, :, at]
        return self.down.at[bx, by, :, 1 - self.me.c if core else self.me.c, :, at]

    def at(self, du, dw, h=None):
        return self.ref(self.us[du], self.ws[dw], h)

    def across(self, dw, h=None):
        return self.ref(slice(None), self.ws[dw], h)

    def along(self, du, h=None):
        return self.ref(self.us[du], slice(None), h)

    def of_sibling(self):
        return self.ref(slice(None), slice(None), core=1)


def wait(*copies):
    yield copies
    for copy in copies:
        copy.wait_recv()


def gather_plane(wire, wide, down, g, k, sib, zs):
    me = wire.place
    s = Piece(me, wide, down, g, k)

    def go(ref, to):
        return wire.put(ref, ref, to)

    def share(name, *where):
        if k == QM and ZED[g]:
            lo, hi = [getattr(s, name)(*where, h) for h in range(2)]
            zs.append(((go(lo, me.above), go(hi, me.below)), name, where))
        sib.append(go(getattr(s, name)(*where), me.sibling))

    out = {}

    def spread(du):
        for d in reach:
            out[d, du] = go(s.at(du, 0), s.second[d])

    if not STRAIGHT[g]:
        reach = (1, -1)
        a, b = go(s.at(0, 0), s.first[1]), go(s.at(0, 0), s.first[-1])
        spread(0)
        yield from wait(a)
        a = go(s.at(-1, 0, 0), s.first[1])
        spread(-1)
        share("at", -1, 0)
        yield from wait(b)
        b = go(s.at(1, 0, 1), s.first[-1])
        spread(1)
        share("at", 1, 0)
        yield from wait(a, b)
        spread(2)
        share("at", 2, 0)
        if FINE[g] == 2 or (FINE[g] == 1 and k == QM):
            far = []
            for du in (0, -1, 1, 2):
                yield from wait(out[1, du])
                a = go(s.at(du, -1, 0), s.second[1])
                share("at", du, -1)
                yield from wait(out[-1, du])
                b = go(s.at(du, 1, 1), s.second[-1])
                share("at", du, 1)
                far.append((a, b))
            for du, copies in zip((0, -1, 1, 2), far):
                yield from wait(*copies)
                share("at", du, 2)
            return
        yield from wait(*[out[1, du] for du in (0, -1, 1, 2)])
        a = go(s.across(-1, 0), s.second[1])
        share("across", -1)
        yield from wait(*[out[-1, du] for du in (0, -1, 1, 2)])
        b = go(s.across(1, 1), s.second[-1])
        share("across", 1)
        yield from wait(a, b)
        share("across", 2)
        return
    reach = (1, -1, 2)
    near = {d: go(s.at(0, 0), s.first[d]) for d in reach}
    spread(0)
    for d in (1, -1, 2):
        du = -d if d < 2 else 2
        yield from wait(near[d])
        spread(du)
        share("at", du, 0)
    for d in (1, -1, 2):
        dw = -d if d < 2 else 2
        yield from wait(*[out[d, du] for du in (0, -1, 1, 2)])
        share("across", dw)


def gather_cross(wire, wide, down, g, sib, zs):
    me = wire.place
    theirs = Piece(me, wide, down, g, QO)
    for n in range(15 if FINE[g] else 6):
        yield lambda: zs[n][0] if len(zs) > n else None
        copies, name, where = zs[n]
        for copy in copies:
            copy.wait_recv()
        ref = getattr(theirs, name)(*where)
        sib.append(wire.put(ref, ref, me.sibling))


def gather_end(n, sib):
    for i in range(n):
        yield lambda: (sib[i],) if len(sib) > i else None
        sib[i].wait_recv()


def gather_streams(wire, wide, down, g):
    sib, zs = {P_: [], QM: [], QO: []}, []
    streams = [gather_plane(wire, wide, down, g, k, sib[k], zs) for k in (P_, QM)]
    fine = {P_: FINE[g] == 2, QM: FINE[g] > 0}
    streams += [gather_end(15 if fine[k] else 6, sib[k]) for k in (P_, QM)]
    if ZED[g]:
        streams += [gather_cross(wire, wide, down, g, sib[QO], zs), gather_end(15 if FINE[g] else 6, sib[QO])]
    return streams


def join(stage, wide, me, g):
    step = 640

    def body(i, carry):
        at = pl.ds(pl.multiple_of(START[g] + i * step, 128), step)
        rows = [stage[o, :, at].astype(F32)[:12] for o in range(4)]
        wide[me.x, me.y, :, at] = jnp.concatenate(rows, axis=0).astype(BF)
        return carry

    lax.fori_loop(0, 2 * HALF[g] // step, body, 0)


def gather_front(wire, own_down, stage, wide, down, g):
    me = wire.place
    mine = 2 * me.zl + me.c
    if g not in DOWN:
        at = pl.ds(START[g], 2 * HALF[g])
        src = dst = stage.at[mine, :, at]
        hers = stage.at[2 * (1 - me.zl) + me.c, :, at]
    else:
        src, dst = own_down, down.at[me.x, me.y, me.zl, me.c]
        hers = down.at[me.x, me.y, 1 - me.zl, me.c]
        down[me.x, me.y, me.zl, me.c] = own_down[...]
    a = wire.put(src, dst, me.share_to)
    b = wire.put(src, dst, me.sibling)
    yield from wait(a)
    c = wire.put(hers, hers, me.sibling)
    yield from wait(b, c)
    if g not in DOWN:
        join(stage, wide, me, g)


def rows_of(g):
    return (2, 48) if g in DOWN else (48,)


REDUCED = (3, 4, 5, 6, 7)


def reduce_shapes(g):
    rows, shapes = rows_of(g), []
    for k in (P_, QM):
        n, low = SIZE[g][kind(k)], LOW[g][kind(k)]
        high = n - low
        if DIRECT[g]:
            low, high = n, 128
        own = (48,) if g in DOWN else (2, 16)
        shapes += [(4, 4, *rows, n), (4, *rows, low), (4, *rows, high), (4, *rows, n), (4, *rows, n)]
        shapes += [(*rows, low), (*rows, high), (*rows, n), (*rows, n), (2, *own, n), (*own, n), (*own, n), (*own, n)]
    if ZED[g]:
        shapes += [(4, 4, *rows, SIZE[g][1])] * 2
    shapes = [(s, BF) for s in shapes]
    return shapes if g in DOWN else shapes + [((16, WIDTH[g]), F32)]


def add_blocks(dst, src):
    def body(i, carry):
        ref = dst(i)
        ref[...] = ref[...] + src(i)[...]
        return carry

    lax.fori_loop(0, 4, body, 0)


def add_one(ref, a):
    ref[...] = ref[...] + a[...]


def add_two(ref, a, b):
    ref[...] = (ref[...].astype(F32) + a[...].astype(F32) + b[...].astype(F32)).astype(BF)


def add_three(ref, a, b, c):
    total = ref[...].astype(F32) + a[...].astype(F32) + (b[...].astype(F32) + c[...].astype(F32))
    ref[...] = total.astype(BF)


def owners_rows(st, ref, others, g):
    total = ref[...].astype(F32)
    for other in others:
        total = total + other[...].astype(F32)
    if g not in DOWN:
        zero = jnp.zeros((4, total.shape[1]), F32)
        for o in range(4):
            st[o // 2, o % 2] = jnp.concatenate([total[12 * o : 12 * o + 12], zero], axis=0).astype(BF)
    else:
        st[...] = total.astype(BF)


def add_planes(me, g, k, st, rzp, rzm, rr, final, final_down, so):
    def total_of(core):
        def pick(ref):
            return (ref[...] if g in DOWN else ref[core]).astype(F32)

        first = pick(st.at[me.zl]) + pick(rr)
        second = pick(rzp) + pick(rzm)
        if k == QM and ZED[g]:
            return (QM, first), (QO, second)
        return ((k, first + second),)

    out = final_down if g in DOWN else final
    for kk, v in total_of(me.c):
        out[:, columns_of(g, kk, me)] = v
    if g not in DOWN:
        for kk, v in total_of(1 - me.c):
            base = me.starts[g, kk, 0] - me.starts[g, None, 0]
            so[:, pl.ds(pl.multiple_of(base, 128), v.shape[1])] = v


def reduce_plane(wire, wide, down, bufs, got, z_in, done, finals, g, k):
    me = wire.place
    s = Piece(me, wide, down, g, k)
    sb, b1p, b1m, b2p, b2m, c1p, c1m, c2p, c2m, st, rzp, rzm, rr = bufs[13 * k : 13 * k + 13]
    lo, hi = halves(g, k)
    any_lo, any_hi = (..., lo), (..., hi)
    crosses = k == QM and ZED[g]

    def add_along(du, buf):
        bu = s.us[du]
        add_blocks(lambda i: s.ref(bu, i), lambda i: buf.at[bu, i] if k == P_ else buf.at[i, bu])

    def add_half(du, h, buf):
        bu = s.us[du]
        add_blocks(lambda i: s.ref(bu, i, h), lambda i: buf.at[i])

    def ready(du):
        if crosses:
            yield lambda: z_in.get(du)
            for copy in z_in[du]:
                copy.wait_recv()
            add_along(du, bufs[27])
        else:
            if len(got) > 1:
                yield from wait(got[du])
            add_along(du, sb)

    if crosses or len(got) == 1:
        yield from wait(*got.values())
    if crosses:
        for du in (2, 1, -1, 0):
            add_along(du, sb)
    if DIRECT[g]:
        near = []
        for du, buf in ((2, b1p), (1, b2p), (-1, b2m)):
            yield from ready(du)
            near.append(wire.put(s.along(du), buf, s.first[du]))
        yield from ready(0)
        yield from wait(*near)
        near = []
        for dw, buf in ((2, c1p), (1, c2p), (-1, c2m), (0, None)):
            bw = s.ws[dw]
            add_three(s.at(0, dw), b1p.at[bw], b2p.at[bw], b2m.at[bw])
            if dw:
                near.append(wire.put(s.at(0, dw), buf, s.second[dw]))
        yield from wait(*near)
        owners_rows(st, s.at(0, 0), (c1p, c2p, c2m), g)
        yield from over_planes(wire, me, g, k, bufs, st, rzp, rzm, rr, finals, done)
        return
    yield from ready(2)
    r1p = wire.put(s.along(2, 0), b1p, s.first[1])
    r1m = wire.put(s.along(2, 1), b1m, s.first[-1])
    yield from ready(1)
    r2p_hi = wire.put(s.along(1, 1), b2p.at[any_hi], s.first[1])
    yield from ready(-1)
    r2m_lo = wire.put(s.along(-1, 0), b2m.at[any_lo], s.first[-1])
    yield from ready(0)
    yield from wait(r1p)
    add_half(1, 0, b1p)
    r2p_lo = wire.put(s.along(1, 0), b2p.at[any_lo], s.first[1])
    yield from wait(r1m)
    add_half(-1, 1, b1m)
    r2m_hi = wire.put(s.along(-1, 1), b2m.at[any_hi], s.first[-1])
    yield from wait(r2p_hi, r2m_lo, r2p_lo, r2m_hi)

    def close(dw):
        add_two(s.at(0, dw), b2p.at[s.ws[dw]], b2m.at[s.ws[dw]])

    close(2)
    r1p = wire.put(s.at(0, 2, 0), c1p, s.second[1])
    r1m = wire.put(s.at(0, 2, 1), c1m, s.second[-1])
    close(1)
    r2p_hi = wire.put(s.at(0, 1, 1), c2p.at[any_hi], s.second[1])
    close(-1)
    r2m_lo = wire.put(s.at(0, -1, 0), c2m.at[any_lo], s.second[-1])
    close(0)
    yield from wait(r1p)
    add_one(s.at(0, 1, 0), c1p)
    r2p_lo = wire.put(s.at(0, 1, 0), c2p.at[any_lo], s.second[1])
    yield from wait(r1m)
    add_one(s.at(0, -1, 1), c1m)
    r2m_hi = wire.put(s.at(0, -1, 1), c2m.at[any_hi], s.second[-1])
    yield from wait(r2p_hi, r2m_lo, r2p_lo, r2m_hi)
    owners_rows(st, s.at(0, 0), (c2p, c2m), g)
    yield from over_planes(wire, me, g, k, bufs, st, rzp, rzm, rr, finals, done)


def over_planes(wire, me, g, k, bufs, st, rzp, rzm, rr, finals, done):
    a = wire.put(st.at[1 - me.zl], rzp, me.above)
    b = wire.put(st.at[1 - me.zl], rzm, me.below)
    c = wire.put(st.at[me.zl], rr, me.other)
    yield from wait(a, b, c)
    add_planes(me, g, k, st, rzp, rzm, rr, *finals, None if g in DOWN else bufs[-1])
    done.append(k)
    if g not in DOWN and len(done) == 2:
        at = pl.ds(pl.multiple_of(me.starts[g, None, 0], 128), WIDTH[g])
        yield from wait(wire.put(bufs[-1], finals[0].at[:, at], me.sibling))


def reduce_cross(wire, wide, down, bufs, got, z_in, g):
    me = wire.place
    theirs = Piece(me, wide, down, g, QO)
    lo, hi = halves(g, QO)
    yield from wait(got)
    for du in (2, 1, -1, 0):
        bu = theirs.us[du]
        add_blocks(lambda i: theirs.ref(bu, i), lambda i: bufs[26].at[i, bu])
        a = wire.put(theirs.along(du, 0), bufs[27].at[:, bu, ..., lo], me.below)
        b = wire.put(theirs.along(du, 1), bufs[27].at[:, bu, ..., hi], me.above)
        z_in[du] = a, b
        if du:
            yield None


def reduce_streams(wire, wide, down, bufs, finals, g):
    me = wire.place
    pieces = {k: Piece(me, wide, down, g, k) for k in (P_, QM, QO)}
    z_in, done, streams = {}, [], []
    if ZED[g]:
        got = wire.put(pieces[QO].of_sibling(), bufs[26], me.sibling)
        streams.append(reduce_cross(wire, wide, down, bufs, got, z_in, g))
    for k in (P_, QM):
        s, sb = pieces[k], bufs[13 * k]
        if SPLIT[g]:
            got = {}
            for du in (2, 1, -1, 0):
                bu = s.us[du]
                dst = sb.at[bu] if k == P_ else sb.at[:, bu]
                got[du] = wire.put(s.ref(s.us[du], slice(None), core=1), dst, me.sibling)
        else:
            got = {0: wire.put(s.of_sibling(), sb, me.sibling)}
        streams.append(reduce_plane(wire, wide, down, bufs, got, z_in, done, finals, g, k))
    return streams


class Conductor:
    def __init__(self, wire, openers):
        self.wire, self.openers = wire, openers
        self.streams = {}
        self.place = 0

    def serve(self):
        for key, i in SCHEDULE[self.place]:
            self.wire.key = key
            if i < 0:
                self.streams.update({(key, k): s for k, s in enumerate(self.openers[key]())})
                for k in self.streams:
                    if k[0] == key:
                        next(self.streams[k])
            else:
                next(self.streams[key, i], None)
        self.place += 1


SCHEDULE = (
    ((5, -1),),
    (),
    ((6, -1), (7, -1),),
    ((5, 0), (6, 0), (5, 0), (0, -1), (7, 0), (6, 0), (7, 0), (0, 0), (0, 0), (0, 1), (0, 1), (0, 2), (0, 2), (0, 0),
     (1, -1), (0, 3), (0, 3), (0, 4), (0, 4), (0, 2), (0, 1), (1, 0), (0, 5), (1, 0), (0, 0), (0, 0), (0, 5), (0, 3),
     (0, 4), (1, 2), (1, 2), (0, 1), (0, 1), (0, 2), (1, 1), (1, 1), (1, 0), (0, 2), (0, 5), (0, 3), (0, 3), (1, 3),
     (1, 3), (1, 2), (0, 1), (0, 4), (0, 0), (1, 1), (1, 0), (1, 0), (0, 4), (0, 3), (0, 5), (0, 2), (2, -1), (1, 4),),
    ((1, 2), (1, 2), (1, 3), (1, 4),),
    ((0, 5), (1, 1), (1, 1), (1, 5),),
    ((0, 4), (1, 0),),
    (),
    ((1, 4), (1, 5), (2, 0), (2, 0),),
    ((1, 3),),
    ((1, 3), (2, 1), (0, 5),),
    (),
    ((1, 2), (1, 5), (2, 1), (2, 2), (2, 2),),
    ((1, 4),),
    ((2, 3),),
    ((1, 1), (2, 0), (2, 3), (1, 5), (2, 1), (1, 4), (1, 3), (2, 2), (2, 3), (2, 0), (2, 0), (1, 5), (2, 1), (2, 1),
     (1, 4), (2, 2), (2, 2), (2, 3), (2, 3), (1, 5),),
    ((2, 0), (2, 1),),
    (),
    (),
    (),
    (),
    (),
    (),
    (),
    ((2, 2),),
    ((14, -1), (2, 3),),
    (),
    (),
    (),
    ((14, 0), (14, 0), (14, 0), (14, 0),),
    (),
    ((16, -1), (14, 1),),
    ((14, 2),),
    ((14, 2),),
    ((16, 0),),
    ((16, 1), (14, 1), (14, 1), (14, 2),),
    (),
    ((14, 2),),
    (),
    ((17, -1),),
    (),
    ((14, 2), (14, 2), (14, 2),),
    (),
    ((17, 0), (16, 0), (16, 1), (17, 1),),
    (),
    ((14, 1),),
    ((17, 0), (17, 0), (14, 2),),
    ((13, -1), (16, 0),),
    (),
    ((17, 1), (17, 1),),
    ((13, 0), (13, 0), (13, 0), (13, 0), (13, 1), (13, 2), (16, 0), (16, 1), (17, 0), (14, 1), (14, 1), (14, 2),
     (14, 2),),
    ((13, 2),),
    ((15, -1), (13, 1), (13, 1), (13, 2), (17, 0), (17, 0), (17, 1), (13, 2), (14, 2), (14, 1), (13, 2), (13, 2),
     (13, 2), (15, 0), (13, 1), (15, 1), (17, 1), (17, 1), (16, 1), (17, 0), (14, 2), (13, 2), (13, 1), (13, 1),
     (14, 1), (16, 1), (17, 0), (15, 0), (17, 1), (13, 2), (13, 2), (15, 1), (13, 1), (13, 2), (15, 0), (15, 1),
     (17, 1), (13, 1), (13, 2), (17, 1), (15, 0), (15, 1), (13, 2), (15, 1),),
)


def dot(a, b):
    return lax.dot_general(a, b, (((1,), (0,)), ((), ())), preferred_element_type=F32)


def dot_nt(a, b):
    return lax.dot_general(a, b, (((1,), (1,)), ((), ())), preferred_element_type=F32)


def loop(n, body):
    if n <= UNROLLED:
        for i in range(n):
            body(i)
        return

    def step(i, carry):
        body(i)
        return carry

    lax.fori_loop(0, n, step, 0)


def mult(v, n):
    return v if isinstance(v, int) else pl.multiple_of(v, n)


def ds(i, n):
    return pl.ds(mult(i * n, n), n)


UNROLLED = 3
T = 256
SCALE = HEAD_DIM ** (-0.5)
O_AT, N1_AT, N2_AT = 4096, 1152, 2432


def set_at(half, s):
    return 1280 * half + 384 * s


def up_at(i):
    return 2560 + 768 * i + (768 if i > 1 else 0)


ROW = 64


def standardise(v):
    centre = jnp.mean(v, axis=-1, keepdims=True)
    centred = v - centre
    spread = jnp.mean(centred * centred, axis=-1, keepdims=True)
    rstd = lax.rsqrt(spread + 1e-05)
    return centred * rstd, rstd


def weight(wide, at, width):
    return wide[:, :, :, pl.ds(at, width)].reshape(D, width)


def layer_kernel(
    x_hbm, seg_ref, n1g_ref, n1b_ref, wq_ref, wk_ref, wv_ref, wo_ref, n2g_ref, n2b_ref, wu_ref, wd_ref, cot_hbm,
    out_hbm, ig_hbm, dn1g_ref, dn1b_ref, dq_ref, dk_ref, dv_ref, do_ref, dn2g_ref, dn2b_ref, du_ref, dd_ref,
    *scratch,
):
    bufs = {}
    for g in REDUCED:
        n = len(reduce_shapes(g))
        bufs[g], scratch = scratch[:n], scratch[n:]
    (
        wide, down, gwide, gdown, final,
        mask, xhat, rstd1, xhat2, rstd2, n1, n1t, n2, qkv, mixed, probs, hidden,
        act, slope, acc_in, dqkv, rows1, rows2, x_ref, cot_ref, out_ref, ig_ref, io, send, recv,
    ) = scratch
    stage = gwide.at[0, :, pl.ds(0, 16)]
    acc_out = ig_ref
    place = me = Place()
    x_in = pltpu.make_async_copy(x_hbm, x_ref, io.at[0])
    cot_in = pltpu.make_async_copy(cot_hbm, cot_ref, io.at[1])
    x_in.start()
    cot_in.start()
    barrier = call_out(place)
    wire = Wire(place, send, recv)
    openers = {g: lambda g=g: gather_streams(wire, wide, down, g) for g in range(3)}
    openers.update({5 + g: lambda g=g: [gather_front(wire, wd_ref, stage, wide, down, g)] for g in range(3)})
    finals = final, dd_ref
    openers.update({10 + g: lambda g=g: reduce_streams(wire, gwide, gdown, bufs[g], finals, g) for g in REDUCED})
    conductor = Conductor(wire, openers)
    serve = conductor.serve
    mine = 2 * me.zl + me.c

    zero4 = lambda n: jnp.zeros((4, n), F32)

    def put_own(ref, width, place_of):
        for i in range(ref.shape[1] // width):
            rows = jnp.concatenate([ref[:, pl.ds(width * i, width)].astype(F32), zero4(width)], axis=0)
            stage[mine, :, pl.ds(place_of(i), width)] = rows.astype(BF)

    def put_norm(gain, shift, at):
        eye = lax.broadcasted_iota(jnp.int32, (16, 12), 0) == lax.broadcasted_iota(jnp.int32, (16, 12), 1)
        lane = lax.broadcasted_iota(jnp.int32, (16, 128), 1)
        a = jnp.sum(jnp.where(eye, gain[...].astype(F32), 0.0), axis=1, keepdims=True)
        b = jnp.sum(jnp.where(eye, shift[...].astype(F32), 0.0), axis=1, keepdims=True)
        both = jnp.where(lane == 0, a, jnp.where(lane == 1, b, 0.0))
        stage[mine, :, pl.ds(at, 128)] = both.astype(BF)

    for k, ref in enumerate((wq_ref, wk_ref, wv_ref)):
        put_own(ref, 128, lambda i: set_at(i // 3, i % 3) + 128 * k)
    put_norm(n1g_ref, n1b_ref, N1_AT)
    put_norm(n2g_ref, n2b_ref, N2_AT)
    pl.semaphore_wait(barrier, len(place.peers))
    serve()
    put_own(wo_ref, D, lambda i: O_AT)
    put_own(wu_ref, D, up_at)
    serve()

    segs = jnp.broadcast_to(seg_ref[...], (T, T))
    rows_iota = lax.broadcasted_iota(jnp.int32, (T, T), 0)
    cols_iota = lax.broadcasted_iota(jnp.int32, (T, T), 1)
    allowed = (rows_iota >= cols_iota) & (segs.astype(F32).T == segs.astype(F32))
    mask[...] = jnp.where(allowed, 0.0, -1e30)

    serve()

    def norm1_rows(i):
        at = ds(i, ROW)
        hat, rstd = standardise(x_ref[at, :].astype(F32))
        xhat[at, :] = hat
        rstd1[at, :] = rstd

    x_in.wait()
    loop(T // ROW, norm1_rows)
    serve()

    eye = (
        lax.broadcasted_iota(jnp.int32, (128, 128), 0) == lax.broadcasted_iota(jnp.int32, (128, 128), 1)
    ).astype(BF)
    rows1[...] = dot_nt(eye, weight(wide, N1_AT, 128))[:8]
    rows2[...] = dot_nt(eye, weight(wide, N2_AT, 128))[:8]

    def norm1_apply(i):
        at = ds(i, ROW)
        n1[at, :] = (xhat[at, :] * rows1[0:1, :] + rows1[1:2, :]).astype(BF)

    loop(T // ROW, norm1_apply)

    def project(half, s):
        w = wide[:, :, :, pl.ds(mult(set_at(half, s), 128), 384)].reshape(D, 384)
        qkv[:, pl.ds(mult(384 * (3 * half + s), 128), 384)] = dot(n1[...], w).astype(BF)

    lane = lax.broadcasted_iota(jnp.int32, (1, 128), 1)
    heads = [((lane >= 32 * h) & (lane < 32 * h + 32)).astype(F32).astype(BF) for h in range(4)]

    def group(ref, which, t, width=384):
        return ref[:, pl.ds(mult(width * t + 128 * which, 128), 128)]

    def attend(t):
        q4, k4, v4 = [group(qkv, i, t) for i in range(3)]
        vh = [v4 * heads[h] for h in range(4)]
        for rb in range(2):
            rows, nk = slice(128 * rb, 128 * rb + 128), 128 * rb + 128
            total = jnp.zeros((128, 128), F32)
            for h in range(4):
                s = dot_nt(q4[rows] * heads[h], k4[:nk]) * SCALE + mask[rows, :nk]
                e = jnp.exp(s - jnp.max(s, axis=1, keepdims=True))
                p = (e * (1.0 / jnp.sum(e, axis=1, keepdims=True))).astype(BF)
                probs[4 * t + h, rows, :nk] = p
                total = total + dot(p, vh[h][:nk])
            mixed[rows, pl.ds(mult(128 * t, 128), 128)] = total.astype(BF)

    for turn, s in enumerate((2, me.zl, 1 - me.zl)):
        if turn:
            serve()
        for half in range(2):
            project(half, s)
        serve()
        for half in range(2):
            attend(3 * half + s)
            serve()

    n2t, mixt = [gwide.at[:, :, :, pl.ds(256 * k, 256)] for k in range(2)]

    def transpose(src, dst):
        def body(i):
            dst[ds(i, 2)] = src[:, ds(i, 384)].T.reshape(2, 4, 48, T)

        loop(2, body)

    def turn_n1(i):
        n1t[ds(i, 384), :] = n1[:, ds(i, 384)].T

    transpose(mixed, mixt)
    loop(2, turn_n1)
    serve()

    def out_project(i):
        at = ds(i, 256)
        w = wide[:, :, :, pl.ds(mult(O_AT + 256 * i, 128), 256)].reshape(D, 256)
        hidden[:, at] = x_ref[:, at].astype(F32) + dot(mixed[...], w)

    loop(3, out_project)

    def norm2_rows(i):
        at = ds(i, ROW)
        hat, rstd = standardise(hidden[at, :])
        xhat2[at, :] = hat
        rstd2[at, :] = rstd
        n2[at, :] = (hat * rows2[0:1, :] + rows2[1:2, :]).astype(BF)

    loop(T // ROW, norm2_rows)
    transpose(n2, n2t)
    serve()

    cot_in.wait()
    c0 = (2.0 / 3.141592653589793) ** 0.5

    def feed(i):
        def part(j):
            at = pl.ds(up_at(i) + 256 * j, 256)
            v = dot(n2[...], wide[:, :, :, at].reshape(D, 256))
            sq = v * v
            th = jnp.tanh(c0 * v * (1.0 + 0.044715 * sq))
            half = 0.5 + 0.5 * th
            a = (v * half).astype(BF)
            keep = pl.ds(mult(768 * i + 256 * j, 128), 256)
            act[:, keep] = a
            slope[:, keep] = half + 0.5 * v * (1.0 - th * th) * (c0 * (1.0 + 0.134145 * sq))

        loop(3, part)
        serve()
        a = act[:, ds(i, 768)].T

        def grad(j):
            at = ds(j, 256)
            gdown[i, :, :, :, :, at] = dot(a, cot_ref[:, at]).astype(BF).reshape(4, 2, 2, 48, 256)

        loop(3, grad)

    for i in range(4):
        feed(i)
        serve()
    serve()

    acc_out[...] = hidden[...]
    acc_in[...] = jnp.zeros((T, D), F32)

    def feed_back(i):
        at = ds(i, 768)
        wd = down[i].reshape(768, 768)
        acc_out[...] += dot(act[:, at], wd)
        pg = (dot_nt(cot_ref[...], wd) * slope[:, at]).astype(BF)
        act[:, at] = pg
        serve()
        acc_in[...] += dot_nt(pg, weight(wide, up_at(i), D))
        serve()

        def grad(j):
            cols_j = pl.ds(up_at(i) + 256 * j, 256)
            pg_j = act[:, pl.ds(mult(768 * i + 256 * j, 128), 256)]
            gwide[:, :, :, cols_j] = dot(n2t[...].reshape(D, T), pg_j).astype(BF).reshape(4, 4, 48, 256)

        loop(3, grad)

    for i in range(4):
        feed_back(i)
        serve()
    out_ref[...] = acc_out[...].astype(BF)
    out_copy = pltpu.make_async_copy(out_ref, out_hbm, io.at[2])
    out_copy.start()

    def norm_back(grad, hat, rstd, gain, at):
        gn = gain * grad
        m1 = jnp.mean(gn, axis=-1, keepdims=True)
        m2 = jnp.mean(gn * hat, axis=-1, keepdims=True)
        return (gn - m1 - hat * m2) * rstd

    def norm2_back(i, sums):
        at = ds(i, ROW)
        grad, hat = acc_in[at, :], xhat2[at, :]
        extra = norm_back(grad, hat, rstd2[at, :], rows2[0:1, :], at)
        hidden[at, :] = cot_ref[at, :].astype(F32) + extra
        a, b = sums
        return a + jnp.sum(grad * hat, axis=0, keepdims=True), b + jnp.sum(grad, axis=0, keepdims=True)

    def as_columns(sums, at):
        rows = jnp.concatenate([*sums, jnp.zeros((126, D), F32)], axis=0)
        gwide[:, :, :, pl.ds(at, 128)] = rows.T.astype(BF).reshape(4, 4, 48, 128)

    nothing = jnp.zeros((1, D), F32)
    as_columns(lax.fori_loop(0, T // ROW, norm2_back, (nothing, nothing)), N2_AT)
    n2[...] = hidden[...].astype(BF)

    serve()

    def o_back(i):
        at = ds(i, 256)
        b = n2[:, at]
        gwide[:, :, :, pl.ds(mult(O_AT + 256 * i, 128), 256)] = (
            dot(mixt[...].reshape(D, T), b).astype(BF).reshape(4, 4, 48, 256)
        )

    loop(3, o_back)
    serve()
    mgrad = n1
    mgrad[...] = dot_nt(n2[...], weight(wide, O_AT, D)).astype(BF)
    serve()

    def attend_back(t):
        q4, k4, v4 = [group(qkv, i, t) for i in range(3)]
        do4, o4 = group(mgrad, 0, t, 128), group(mixed, 0, t, 128)
        q4t, do4t = q4.T, do4.T
        kh = [k4 * heads[h] for h in range(4)]
        dk, dv = [], []
        total = [jnp.zeros((128, 128), F32)] * 2
        for h in range(4):
            hrows = slice(32 * h, 32 * h + 32)
            dkh, dvh = [], []
            for rb in range(2):
                rows, nk = slice(128 * rb, 128 * rb + 128), 128 * rb + 128
                dob = do4[rows] * heads[h]
                dot_row = jnp.sum(dob.astype(F32) * o4[rows].astype(F32), axis=1, keepdims=True)
                p = probs[4 * t + h, rows, :nk]
                sg = (p.astype(F32) * (dot_nt(dob, v4[:nk]) - dot_row)).astype(BF)
                total[rb] = total[rb] + dot(sg, kh[h][:nk])
                dkh.append(dot(q4t[hrows, rows], sg))
                dvh.append(dot(do4t[hrows, rows], p))
            for both, parts in ((dk, dkh), (dv, dvh)):
                both.append(jnp.concatenate([parts[1][:, :128] + parts[0], parts[1][:, 128:]], axis=1))
        at = 384 * t
        for rb in range(2):
            dqkv[pl.ds(128 * rb, 128), pl.ds(at, 128)] = (total[rb] * SCALE).astype(BF)
        dqkv[:, pl.ds(at + 128, 128)] = (jnp.concatenate(dk, axis=0).T * SCALE).astype(BF)
        dqkv[:, pl.ds(at + 256, 128)] = jnp.concatenate(dv, axis=0).T.astype(BF)

    for s in range(3):
        for half in range(2):
            attend_back(3 * half + s)
            serve()
        for half in range(2):
            part = dqkv[:, pl.ds(384 * (3 * half + s), 384)]
            gwide[:, :, :, pl.ds(set_at(half, s), 384)] = dot(n1t[...], part).astype(BF).reshape(4, 4, 48, 384)
        serve()
        for half in range(2):
            part = dqkv[:, pl.ds(384 * (3 * half + s), 384)]
            grad = dot_nt(part, weight(wide, set_at(half, s), 384))
            acc_in[...] = grad if s + half == 0 else acc_in[...] + grad
        if s < 2:
            serve()

    def norm1_back(i, sums):
        at = ds(i, ROW)
        grad, hat = acc_in[at, :], xhat[at, :]
        extra = norm_back(grad, hat, rstd1[at, :], rows1[0:1, :], at)
        ig_ref[at, :] = hidden[at, :] + extra
        a, b = sums
        return a + jnp.sum(grad * hat, axis=0, keepdims=True), b + jnp.sum(grad, axis=0, keepdims=True)

    as_columns(lax.fori_loop(0, T // ROW, norm1_back, (nothing, nothing)), N1_AT)
    ig_copy = pltpu.make_async_copy(ig_ref, ig_hbm, io.at[3])
    ig_copy.start()
    serve()

    assert conductor.place == len(SCHEDULE)
    out_copy.wait()
    ig_copy.wait()
    wire.drain()

    for k, ref in enumerate((dq_ref, dk_ref, dv_ref)):
        for i in range(6):
            ref[:, pl.ds(128 * i, 128)] = final[:12, pl.ds(set_at(i // 3, i % 3) + 128 * k, 128)]
    do_ref[...] = final[:12, pl.ds(O_AT, D)]
    for i in range(4):
        du_ref[:, pl.ds(768 * i, 768)] = final[:12, pl.ds(up_at(i), 768)]
    diag = lax.broadcasted_iota(jnp.int32, (16, 128), 0) == lax.broadcasted_iota(jnp.int32, (16, 128), 1)
    for at, refs in ((N1_AT, (dn1g_ref, dn1b_ref)), (N2_AT, (dn2g_ref, dn2b_ref))):
        for k, ref in enumerate(refs):
            col = final[:, at + k : at + k + 1]
            ref[...] = jnp.sum(jnp.where(diag, col, 0.0), axis=0, keepdims=True)[:, :12]


def publish_kernel(*refs):
    n = len(refs) // 3
    sems = refs[-1]
    ins = [pltpu.make_async_copy(refs[i], refs[2 * n + i], sems.at[i]) for i in range(n)]
    outs = [pltpu.make_async_copy(refs[2 * n + i], refs[n + i], sems.at[n + i]) for i in range(n)]
    for copy in ins:
        copy.start()
    for come, go in zip(ins, outs):
        come.wait()
        go.start()
    for copy in outs:
        copy.wait()


VM = pl.BlockSpec(memory_space=pltpu.VMEM)
ANY = pl.BlockSpec(memory_space=pl.ANY)


def per_device(*args):
    args = [a.reshape(1, 12) if a.ndim == 1 else a for a in args]
    like = jax.ShapeDtypeStruct
    vec, square = like((1, 12), F32), like((12, D), F32)
    scratch = [pltpu.VMEM(s, t) for g in REDUCED for s, t in reduce_shapes(g)]
    wide, down = pltpu.VMEM((4, 4, 48, WIDE), BF), pltpu.VMEM((4, 4, 2, 2, 48, D), BF)
    scratch += [wide, down, wide, down, pltpu.VMEM((16, WIDE), F32)]
    f32s, bfs = pltpu.VMEM((T, D), F32), pltpu.VMEM((T, D), BF)
    one, turned = pltpu.VMEM((T, 1), F32), pltpu.VMEM((D, T), BF)
    scratch += [pltpu.VMEM((T, T), F32), f32s, one, f32s, one]
    scratch += [bfs, turned, bfs, pltpu.VMEM((T, 3 * D), BF), bfs]
    scratch += [pltpu.VMEM((HEADS, T, T), BF), f32s]
    scratch += [pltpu.VMEM((T, FF), BF), pltpu.VMEM((T, FF), F32), f32s]
    scratch += [pltpu.VMEM((T, 3 * D), BF), pltpu.VMEM((8, D), F32), pltpu.VMEM((8, D), F32)]
    scratch += [bfs, bfs, bfs, f32s, pltpu.SemaphoreType.DMA((4,))]
    scratch += [pltpu.SemaphoreType.DMA((N_SEND,)), pltpu.SemaphoreType.DMA((N_RECV,))]
    outs = pl.pallas_call(
        layer_kernel,
        out_shape=(
            like((T, D), BF), like((T, D), F32), vec, vec, square, square, square, square, vec, vec,
            like((12, FF), F32), like((48, D), F32),
        ),
        in_specs=[ANY] + [VM] * 11 + [ANY],
        out_specs=(ANY, ANY) + (VM,) * 10,
        scratch_shapes=scratch,
        compiler_params=pltpu.CompilerParams(
            collective_id=0, has_side_effects=True, vmem_limit_bytes=VMEM_BYTES
        ),
        cost_estimate=pl.CostEstimate(flops=13 * 10**9, bytes_accessed=6 * 10**6, transcendentals=3 * 10**6),
        name="layer",
    )(*args)
    outs = pl.pallas_call(
        publish_kernel,
        out_shape=tuple(like(o.shape, o.dtype) for o in outs),
        in_specs=[ANY] * 12,
        out_specs=(ANY,) * 12,
        scratch_shapes=[*[pltpu.VMEM(o.shape, o.dtype) for o in outs], pltpu.SemaphoreType.DMA((24,))],
        name="publish",
    )(*outs)
    return tuple(o.reshape(12) if o.shape == (1, 12) else o for o in outs)


def solution(mesh):
    placed = (
        P(("fsdp", "rep"), None),
        P(("fsdp", "rep"), None),
        P("fsdp"),
        P("fsdp"),
        P("fsdp", None),
        P("fsdp", None),
        P("fsdp", None),
        P("fsdp", None),
        P("fsdp"),
        P("fsdp"),
        P("fsdp", None),
        P("fsdp", None),
        P(("fsdp", "rep"), None),
    )
    return jax.shard_map(
        per_device,
        mesh=mesh,
        in_specs=placed,
        out_specs=(
            P(("fsdp", "rep"), None),
            P(("fsdp", "rep"), None),
            P("fsdp"),
            P("fsdp"),
            P("fsdp", None),
            P("fsdp", None),
            P("fsdp", None),
            P("fsdp", None),
            P("fsdp"),
            P("fsdp"),
            P("fsdp", None),
            P("fsdp", None),
        ),
        check_vma=False,
    )
```
